128 devices in a mesh: gy: 8 (over x, core), gz: 16 (over y, z).
Axes of the slice: x: 4, y: 4, z: 4, core: 2. Of those that a mesh axis runs over, the one named last changes fastest.
Arguments:
- velocity: float32 [3, 768, 12288], P(None, 'gy', 'gz'), may hold values from -250 to 250
- strain: bfloat16 [6, 768, 12288], P(None, 'gy', 'gz'), may hold values from -250 to 250
- cell_height: float32 [768], P('gy'), may hold values from 0.5 to 2
- stencil_reach: int32 [2, 768], P(None, 'gy'), may hold values from 1 to 8, as said below
Outputs:
- coefficient: float32 [768], P('gy')
The draws below stay inside these ranges and needn't reach their ends.
Inputs may be any that keep to these rules, and one draw needn't show every extreme that they name: `stencil_reach`: in every draw some plane reaches 8 planes on both sides; stencils are cut at the walls by the steps.
All inputs are finite; a program needn't handle non-finite values.
Results may differ from the reference program's by a relative error of at most 0.0003.
Values sent between devices are 32-bit elements; how exact they have to be, the bound alone decides.
No kernel may reach another device: no remote copies, remote signals or barrier semaphores. Data moves between devices by JAX's collectives and lax.ppermute only.
A program may use at most 128 MiB of HBM per device.

```python
import math
import jax
import jax.numpy as jnp
from jax import lax

CZ = 96
NX = 8
HMAX = 8
NY = 768
NZ = 1536


def column_scales(key):
    spread = math.log(10.0)
    stream_scale = jnp.exp(jax.random.uniform(jax.random.fold_in(key, 3), (NX,), jnp.float32, -0.5, 0.5) * spread)
    span_index = jnp.arange(NZ, dtype=jnp.int32)
    span_trend = jnp.exp(math.log(3.0) * (span_index.astype(jnp.float32) / NZ - 0.5))
    edge_cell = (span_index % CZ == 0) | (span_index % CZ == CZ - 1)
    edge_boost = jnp.where(edge_cell, 4.0, 1.0)
    span_scale = jnp.exp(jax.random.uniform(jax.random.fold_in(key, 5), (NZ,), jnp.float32, -0.5, 0.5) * spread) * span_trend * edge_boost
    return span_scale[:, None] * stream_scale[None, :]


def noise_field(key, array_shape):
    return jnp.clip(jax.random.normal(key, array_shape, jnp.float32), -5.0, 5.0)


def draw_velocity(key, part):
    scales = column_scales(jax.random.fold_in(key, 7))
    noise_data = noise_field(jax.random.fold_in(key, 11), (3, NY, NZ, NX))
    mean_flow = jax.random.uniform(jax.random.fold_in(key, 13), (NY,), jnp.float32, 0.5, 3.0)
    along_flow = mean_flow[:, None, None] + noise_data[0] * scales
    normal_part = (noise_data[1] - 0.5 * noise_data[0]) * scales
    across = noise_data[2] * scales
    stacked = jnp.stack([along_flow, normal_part, across])
    return jnp.clip(stacked, -249.0, 249.0).reshape(3, NY, NZ * NX).astype(jnp.float32)


def draw_strain(key, part):
    scales = column_scales(jax.random.fold_in(key, 7))
    noise_data = noise_field(jax.random.fold_in(key, 17), (6, NY, NZ, NX))
    shear_mean = jax.random.uniform(jax.random.fold_in(key, 19), (NY,), jnp.float32, 1.0, 3.0)
    lifted = noise_data.at[3].add(shear_mean[:, None, None])
    return jnp.clip(lifted * scales[None, None], -249.0, 249.0).reshape(6, NY, NZ * NX).astype(jnp.bfloat16)


def draw_stencil_reach(key, part):
    reach_draw = jax.random.randint(jax.random.fold_in(key, 23), (2, NY), 1, HMAX + 1, jnp.int32)
    return reach_draw.at[:, NY // 2].set(HMAX)


def levels(rng, extent, shards, least, top_value):
    gain = 1.0
    for dim, blocks in shards:
        steps = jax.random.uniform(jax.random.fold_in(jax.random.fold_in(rng, 6), dim), (blocks,), jnp.float32, least / len(shards), top_value / len(shards))
        gain = gain * jnp.repeat(jnp.exp(steps), extent[dim] // blocks).reshape((-1,) + (1,) * (len(extent) - 1 - dim))
    return gain


def setup_inputs(seed: int = 0) -> dict:
    keys = jax.random.split(jax.random.key(seed), 5)
    velocity = draw_velocity(jax.random.fold_in(keys[4], 71), 0)
    strain = draw_strain(jax.random.fold_in(keys[4], 71), 0)
    cell_height = jnp.clip(jnp.exp(math.log(2.0) - 1.3862944 * jax.random.uniform(keys[2], (NY,), jnp.float32) ** levels(keys[2], (NY,), ((0, 8),), -0.2, 0.2)), 0.5, 2.0)
    stencil_reach = draw_stencil_reach(jax.random.fold_in(keys[4], 71), 0)
    return dict(velocity=velocity, strain=strain, cell_height=cell_height, stencil_reach=stencil_reach)


LEAD_INDEX = (0, 1, 2, 0, 0, 1)
TAIL_INDEX = (0, 1, 2, 1, 2, 2)
TENSOR_WEIGHTS = (1.0, 1.0, 1.0, 2.0, 2.0, 2.0)

def strain_rate(tensor):
    squares = 2.0 * (tensor[0] * tensor[0] + tensor[1] * tensor[1] + tensor[2] * tensor[2])
    squares = squares + 4.0 * (tensor[3] * tensor[3] + tensor[4] * tensor[4] + tensor[5] * tensor[5])
    return jnp.sqrt(squares)

def axis_filter(field_data, axis_number):
    return 0.25 * jnp.roll(field_data, 1, axis_number) + 0.5 * field_data + 0.25 * jnp.roll(field_data, -1, axis_number)

def wall_coefficients(cell_height, stencil_reach):
    planes = jnp.arange(NY, dtype=jnp.int32)
    lowest = jnp.maximum(planes - stencil_reach[0], 0)
    highest = jnp.minimum(planes + stencil_reach[1], NY - 1)
    heights = jnp.pad(cell_height, (HMAX, HMAX))
    weight_terms = []
    for offset_plane in range(-HMAX, HMAX + 1):
        column = planes + offset_plane
        inside = (column >= lowest) & (column <= highest)
        weight_terms.append(jnp.where(inside, heights[HMAX + offset_plane:HMAX + offset_plane + NY], 0.0))
    weight_terms = jnp.stack(weight_terms)
    return weight_terms / lax.optimization_barrier(jnp.sum(weight_terms, axis=0, keepdims=True))

def test_filter(field_data, coefficients):
    field_data = axis_filter(field_data, 2)
    field_data = axis_filter(field_data, 1)
    padded = jnp.pad(field_data, ((HMAX, HMAX), (0, 0), (0, 0)))
    running_sum = jnp.zeros_like(field_data)
    for offset_plane in range(-HMAX, HMAX + 1):
        running_sum = running_sum + coefficients[offset_plane + HMAX][:, None, None] * padded[offset_plane + HMAX:offset_plane + HMAX + NY]
    return running_sum

def reference(velocity, strain, cell_height, stencil_reach):
    velocity = velocity.reshape(3, NY, NZ, NX)
    tensor = strain.astype(jnp.float32).reshape(6, NY, NZ, NX)
    coefficients = wall_coefficients(cell_height, stencil_reach)
    magnitude = strain_rate(tensor)
    velocity_bar = [test_filter(velocity[component], coefficients) for component in range(3)]
    tensor_bar = [test_filter(tensor[component], coefficients) for component in range(6)]
    rate_bar = strain_rate(tensor_bar)
    numerator = jnp.zeros((NY,), velocity.dtype)
    denominator = jnp.zeros((NY,), velocity.dtype)
    for component in range(6):
        first_index = LEAD_INDEX[component]
        second_index = TAIL_INDEX[component]
        product_bar = test_filter(velocity[first_index] * velocity[second_index], coefficients)
        model_bar = test_filter(magnitude * tensor[component], coefficients)
        leonard = product_bar - velocity_bar[first_index] * velocity_bar[second_index]
        model_term = model_bar - 4.0 * rate_bar * tensor_bar[component]
        numerator = numerator + lax.optimization_barrier(jnp.sum(TENSOR_WEIGHTS[component] * leonard * model_term, axis=(1, 2)))
        denominator = denominator + lax.optimization_barrier(jnp.sum(TENSOR_WEIGHTS[component] * model_term * model_term, axis=(1, 2)))
    cell_count = NZ * NX
    return numerator / cell_count / (denominator / cell_count + 1e-06)
```

```python
import jax
import jax.numpy as jnp
from jax import lax
from jax.experimental import pallas as pl
from jax.experimental.pallas import tpu as pltpu
from jax.sharding import PartitionSpec as P

NX = 8
HMAX = 8
LANES = 128
LEAD_INDEX = (0, 1, 2, 0, 0, 1)
TAIL_INDEX = (0, 1, 2, 1, 2, 2)
TENSOR_WEIGHTS = (1.0, 1.0, 1.0, 2.0, 2.0, 2.0)
F32 = jnp.float32
BF16 = jnp.bfloat16


def strain_rate(s):
    squares = 2.0 * (s[0] * s[0] + s[1] * s[1] + s[2] * s[2])
    squares = squares + 4.0 * (s[3] * s[3] + s[4] * s[4] + s[5] * s[5])
    return jnp.sqrt(squares)


def lane_iota(shape):
    return lax.broadcasted_iota(jnp.int32, shape, len(shape) - 1)


def rot(x, amount):
    amount = amount % LANES
    return pltpu.roll(x, amount, x.ndim - 1) if amount else x


def pack_span_kernel(vl, vr, sl, sr, near_ref, far_ref):
    rows = vl.shape[1]
    lane = lane_iota((rows, LANES))
    left = jnp.zeros((rows, LANES), F32)
    right = jnp.zeros((rows, LANES), F32)
    for f in range(9):
        a = vl[f] if f < 3 else sl[f - 3].astype(F32)
        b = vr[f] if f < 3 else sr[f - 3].astype(F32)
        here = (lane >= NX * f) & (lane < NX * (f + 1))
        left = jnp.where(here, rot(a, NX * f), left)
        right = jnp.where(here, rot(b, NX * f + NX), right)
    odd = lax.axis_index("gz") % 2 == 1
    near_ref[...] = jnp.where(odd, left, right)
    far_ref[...] = jnp.where(odd, right, left)


def pack_span(velocity, strain):
    rows, cells = velocity.shape[1:]
    last = cells // LANES - 1
    return pl.pallas_call(
        pack_span_kernel,
        grid=(1,),
        in_specs=[
            pl.BlockSpec((3, rows, LANES), lambda i: (0, 0, 0)),
            pl.BlockSpec((3, rows, LANES), lambda i: (0, 0, last)),
            pl.BlockSpec((6, rows, LANES), lambda i: (0, 0, 0)),
            pl.BlockSpec((6, rows, LANES), lambda i: (0, 0, last)),
        ],
        out_specs=[pl.BlockSpec((rows, LANES), lambda i: (0, 0))] * 2,
        out_shape=[jax.ShapeDtypeStruct((rows, LANES), F32)] * 2,
    )(velocity, velocity, strain, strain)


def pack_wall_kernel(vlo, vhi, slo, shi, h_ref, znear, zfar, near_ref, far_ref):
    cells = vlo.shape[2]
    rows = znear.shape[0]
    gz_odd = lax.axis_index("gz") % 2 == 1
    gy_odd = lax.axis_index("gy") % 2 == 1
    tail = 9 * cells
    lane = lane_iota((HMAX, LANES))
    row = lax.broadcasted_iota(jnp.int32, (HMAX, LANES), 0)
    stamp = (row == 0) & (lane >= 9 * NX) & (lane < 10 * NX)
    heights = jnp.broadcast_to(jnp.pad(h_ref[...], ((0, 0), (0, LANES - rows))), (HMAX, LANES))

    def emit(ref, high):
        v = vhi if high else vlo
        s = shi if high else slo
        r0 = rows - HMAX if high else 0
        for f in range(3):
            ref[:, f * cells : (f + 1) * cells] = v[f]
        for f in range(6):
            part = s[f].astype(F32)
            ref[:, (3 + f) * cells : (4 + f) * cells] = part[HMAX:] if high else part[:HMAX]
        zn = znear[r0 : r0 + HMAX, :]
        zf = zfar[r0 : r0 + HMAX, :]
        zl = jnp.where(gz_odd, zn, zf)
        zr = jnp.where(gz_odd, zf, zn)
        ref[:, tail : tail + LANES] = jnp.where(stamp, rot(heights, 9 * NX - r0), zl)
        ref[:, tail + LANES : tail + 2 * LANES] = zr

    @pl.when(gy_odd)
    def _():
        emit(near_ref, False)
        emit(far_ref, True)

    @pl.when(jnp.logical_not(gy_odd))
    def _():
        emit(near_ref, True)
        emit(far_ref, False)


def pack_wall(velocity, strain, heights, znear, zfar):
    rows, cells = velocity.shape[1:]
    width = 9 * cells + 2 * LANES
    return pl.pallas_call(
        pack_wall_kernel,
        grid=(1,),
        in_specs=[
            pl.BlockSpec((3, HMAX, cells), lambda i: (0, 0, 0)),
            pl.BlockSpec((3, HMAX, cells), lambda i: (0, rows // HMAX - 1, 0)),
            pl.BlockSpec((6, 2 * HMAX, cells), lambda i: (0, 0, 0)),
            pl.BlockSpec((6, 2 * HMAX, cells), lambda i: (0, rows // (2 * HMAX) - 1, 0)),
            pl.BlockSpec((1, rows), lambda i: (0, 0)),
            pl.BlockSpec((rows, LANES), lambda i: (0, 0)),
            pl.BlockSpec((rows, LANES), lambda i: (0, 0)),
        ],
        out_specs=[pl.BlockSpec((HMAX, width), lambda i: (0, 0))] * 2,
        out_shape=[jax.ShapeDtypeStruct((HMAX, width), F32)] * 2,
    )(velocity, velocity, strain, strain, heights, znear, zfar)


def split2(x):
    hi = x.astype(BF16)
    return hi, (x - hi.astype(F32)).astype(BF16)


def main_kernel(v_ref, s_ref, h_ref, reach_ref, znear, zfar, ynear, yfar, out_ref, raw, stack, filt, acc):
    rows, cells = v_ref.shape[1:]
    tiles = cells // LANES
    ext = rows + 2 * HMAX
    total_planes = lax.axis_size("gy") * rows
    gy = lax.axis_index("gy")
    gz_odd = lax.axis_index("gz") % 2 == 1
    gy_odd = gy % 2 == 1
    offset = gy * rows
    tail = 9 * cells

    ylo = jnp.where(gy_odd, ynear[:, tail:], yfar[:, tail:])
    yhi = jnp.where(gy_odd, yfar[:, tail:], ynear[:, tail:])

    column = lane_iota((rows, LANES))
    place = jnp.where(column < rows, column, jnp.where(column < rows + HMAX, column - rows - HMAX, column - HMAX))
    row = lax.broadcasted_iota(jnp.int32, (rows, LANES), 0)
    hpad = jnp.pad(h_ref[...], ((0, 0), (0, LANES - rows)))
    hrow = lane_iota((1, LANES))
    hext = jnp.where(
        hrow < rows,
        hpad,
        jnp.where(hrow < rows + HMAX, rot(ylo[:, :LANES], rows - 9 * NX)[0:1], rot(yhi[:, :LANES], rows + HMAX - 9 * NX)[0:1]),
    )
    eye = row == column
    reach = jnp.pad(reach_ref[...].astype(F32), ((0, 0), (0, LANES - rows)))
    down = jnp.sum(jnp.where(eye, reach[0:1], 0.0), axis=1, keepdims=True).astype(jnp.int32)
    up = jnp.sum(jnp.where(eye, reach[1:2], 0.0), axis=1, keepdims=True).astype(jnp.int32)
    inside = (place >= row - down) & (place <= row + up) & (place + offset >= 0) & (place + offset < total_planes)
    inside = inside & (column < ext)
    weights = jnp.where(inside, jnp.broadcast_to(hext, (rows, LANES)), 0.0)
    inv = 1.0 / jnp.sum(weights, axis=1, keepdims=True)
    whi, wlo = split2(weights * inv)
    lhs = jnp.concatenate(
        [jnp.concatenate([whi, whi], axis=1), jnp.concatenate([wlo, jnp.zeros_like(wlo)], axis=1)], axis=0
    )

    zl_own = jnp.where(gz_odd, znear[...], zfar[...])
    zr_own = jnp.where(gz_odd, zfar[...], znear[...])
    zl = jnp.concatenate([zl_own, ylo[:, :LANES], yhi[:, :LANES]], axis=0)
    zr = jnp.concatenate([zr_own, ylo[:, LANES:], yhi[:, LANES:]], axis=0)
    elane = lane_iota((ext, LANES))
    for f in range(9):
        raw[f, 0:rows, 0:cells] = v_ref[f] if f < 3 else s_ref[f - 3].astype(F32)
        near = ynear[:, f * cells : (f + 1) * cells]
        far = yfar[:, f * cells : (f + 1) * cells]
        raw[f, rows : rows + HMAX, 0:cells] = jnp.where(gy_odd, near, far)
        raw[f, rows + HMAX : ext, 0:cells] = jnp.where(gy_odd, far, near)
        edge = jnp.where(elane < NX, rot(zl, -NX * f), jnp.where(elane < 2 * NX, rot(zr, NX - NX * f), 0.0))
        raw[f, 0:ext, cells : cells + LANES] = edge
    stack[...] = jnp.zeros_like(stack)

    def tile_step(t, carry):
        at = pl.ds(pl.multiple_of(t * LANES, LANES), LANES)
        for r in range(0, ext, 16):
            u = [raw[f, r : r + 16, at] for f in range(3)]
            s = [raw[f, r : r + 16, at] for f in range(3, 9)]
            rate = strain_rate(s)
            fields = u + [u[a] * u[b] for a, b in zip(LEAD_INDEX, TAIL_INDEX)] + s + [rate * x for x in s]
            for f in range(21):
                hi, lo = split2(fields[f])
                stack[r : r + 16, f * LANES : (f + 1) * LANES] = hi
                stack[LANES + r : LANES + r + 16, f * LANES : (f + 1) * LANES] = lo
        both = jnp.dot(lhs, stack[...], preferred_element_type=F32)
        merged = both[:rows] + both[rows:]
        for f in range(21):
            filt[f, :, at] = merged[:, f * LANES : (f + 1) * LANES]
        return carry

    lax.fori_loop(0, tiles + 1, tile_step, 0)

    lane8 = lane_iota((HMAX, LANES))
    phase = lane8 % NX
    first, last = phase == 0, phase == NX - 1

    def row_step(r, carry):
        rr = pl.ds(pl.multiple_of(r * HMAX, HMAX), HMAX)
        num = jnp.zeros((HMAX, LANES), F32)
        den = jnp.zeros((HMAX, LANES), F32)
        for t in range(tiles):
            g = []
            for f in range(21):
                c = filt[f, rr, t * LANES : (t + 1) * LANES]
                e = filt[f, rr, cells : cells + LANES]
                below = rot(filt[f, rr, (t - 1) * LANES : t * LANES], NX) if t else e
                above = rot(filt[f, rr, (t + 1) * LANES : (t + 2) * LANES], -NX) if t < tiles - 1 else rot(e, -2 * NX)
                below = jnp.where(lane8 < NX, below, rot(c, NX))
                above = jnp.where(lane8 >= LANES - NX, above, rot(c, -NX))
                z = 0.5 * c + 0.25 * (below + above)
                behind = jnp.where(first, rot(z, 1 - NX), rot(z, 1))
                ahead = jnp.where(last, rot(z, NX - 1), rot(z, -1))
                g.append(0.5 * z + 0.25 * (behind + ahead))
            u, p, s, m = g[0:3], g[3:9], g[9:15], g[15:21]
            rate = 4.0 * strain_rate(s)
            for k in range(6):
                leonard = p[k] - u[LEAD_INDEX[k]] * u[TAIL_INDEX[k]]
                model = m[k] - rate * s[k]
                weighted = TENSOR_WEIGHTS[k] * model
                num = num + weighted * leonard
                den = den + weighted * model
        acc[0, rr, :] = num
        acc[1, rr, :] = den
        return carry

    lax.fori_loop(0, rows // HMAX, row_step, 0)
    ones = jnp.ones((HMAX, LANES), F32)
    for k in range(2):
        sums = lax.dot_general(
            ones, acc[k], (((1,), (1,)), ((), ())), precision=lax.Precision.HIGHEST, preferred_element_type=F32
        )
        out_ref[k : k + 1, :] = sums[0:1]


def main_call(velocity, strain, heights, reach, znear, zfar, ynear, yfar):
    rows, cells = velocity.shape[1:]
    ext = rows + 2 * HMAX
    vmem = pl.BlockSpec(memory_space=pltpu.VMEM)
    return pl.pallas_call(
        main_kernel,
        in_specs=[vmem] * 8,
        out_specs=vmem,
        out_shape=jax.ShapeDtypeStruct((2, rows), F32),
        scratch_shapes=[
            pltpu.VMEM((9, ext, cells + LANES), F32),
            pltpu.VMEM((2 * LANES, 21 * LANES), BF16),
            pltpu.VMEM((21, rows, cells + LANES), F32),
            pltpu.VMEM((2, rows, LANES), F32),
        ],
        compiler_params=pltpu.CompilerParams(vmem_limit_bytes=40 * 1024 * 1024),
    )(velocity, strain, heights, reach, znear, zfar, ynear, yfar)


def near_pairs(axis):
    return [(i, i ^ 1) for i in range(lax.axis_size(axis))]


def far_pairs(axis, closed):
    n = lax.axis_size(axis)
    pairs = []
    for i in range(1, n if closed else n - 1, 2):
        pairs += [(i, (i + 1) % n), ((i + 1) % n, i)]
    return pairs


def local(velocity, strain, cell_height, stencil_reach):
    rows, cells = velocity.shape[1:]
    heights = cell_height.reshape(1, rows)
    near, far = pack_span(velocity, strain)
    zfar = lax.ppermute(far, "gz", far_pairs("gz", True))
    znear = lax.ppermute(near, "gz", near_pairs("gz"))
    near, far = pack_wall(velocity, strain, heights, znear, zfar)
    yfar = lax.ppermute(far, "gy", far_pairs("gy", False))
    ynear = lax.ppermute(near, "gy", near_pairs("gy"))
    sums = main_call(velocity, strain, heights, stencil_reach, znear, zfar, ynear, yfar)
    for mask in (1, 3, 4, 12):
        sums = sums + lax.ppermute(sums, "gz", [(i, i ^ mask) for i in range(16)])
    total = lax.axis_size("gz") * cells
    return sums[0] / total / (sums[1] / total + 1e-06)


def solution(mesh):
    in_specs = (P(None, "gy", "gz"), P(None, "gy", "gz"), P("gy"), P(None, "gy"))
    return jax.shard_map(local, mesh=mesh, in_specs=in_specs, out_specs=P("gy"), check_vma=False)
```

```python
import jax
import jax.numpy as jnp
import numpy as np
from jax import lax
from jax.experimental import pallas as pl
from jax.experimental.pallas import tpu as pltpu
from jax.sharding import PartitionSpec as P

NX = 8
HMAX = 8
LANES = 128
LEAD_INDEX = (0, 1, 2, 0, 0, 1)
TAIL_INDEX = (0, 1, 2, 1, 2, 2)
TENSOR_WEIGHTS = (1.0, 1.0, 1.0, 2.0, 2.0, 2.0)
F32 = jnp.float32
BF16 = jnp.bfloat16


def strain_rate(s):
    squares = 2.0 * (s[0] * s[0] + s[1] * s[1] + s[2] * s[2])
    squares = squares + 4.0 * (s[3] * s[3] + s[4] * s[4] + s[5] * s[5])
    return jnp.sqrt(squares)


def lane_iota(shape):
    return lax.broadcasted_iota(jnp.int32, shape, len(shape) - 1)


def rot(x, amount):
    amount = amount % LANES
    return pltpu.roll(x, amount, x.ndim - 1) if amount else x


def pack_span_kernel(vl, vr, sl, sr, near_ref, far_ref):
    rows = vl.shape[1]
    lane = lane_iota((rows, LANES))
    left = jnp.zeros((rows, LANES), F32)
    right = jnp.zeros((rows, LANES), F32)
    for f in range(9):
        a = vl[f] if f < 3 else sl[f - 3].astype(F32)
        b = vr[f] if f < 3 else sr[f - 3].astype(F32)
        here = (lane >= NX * f) & (lane < NX * (f + 1))
        left = jnp.where(here, rot(a, NX * f), left)
        right = jnp.where(here, rot(b, NX * f + NX), right)
    odd = lax.axis_index("gz") % 2 == 1
    near_ref[...] = jnp.where(odd, left, right)
    far_ref[...] = jnp.where(odd, right, left)


def pack_span(velocity, strain):
    rows, cells = velocity.shape[1:]
    last = cells // LANES - 1
    return pl.pallas_call(
        pack_span_kernel,
        grid=(1,),
        in_specs=[
            pl.BlockSpec((3, rows, LANES), lambda i: (0, 0, 0)),
            pl.BlockSpec((3, rows, LANES), lambda i: (0, 0, last)),
            pl.BlockSpec((6, rows, LANES), lambda i: (0, 0, 0)),
            pl.BlockSpec((6, rows, LANES), lambda i: (0, 0, last)),
        ],
        out_specs=[pl.BlockSpec((rows, LANES), lambda i: (0, 0))] * 2,
        out_shape=[jax.ShapeDtypeStruct((rows, LANES), F32)] * 2,
    )(velocity, velocity, strain, strain)


def pack_wall_kernel(vlo, vhi, slo, shi, h_ref, znear, zfar, near_ref, far_ref):
    cells = vlo.shape[2]
    rows = znear.shape[0]
    gz_odd = lax.axis_index("gz") % 2 == 1
    gy_odd = lax.axis_index("gy") % 2 == 1
    tail = 9 * cells
    lane = lane_iota((HMAX, LANES))
    row = lax.broadcasted_iota(jnp.int32, (HMAX, LANES), 0)
    stamp = (row == 0) & (lane >= 9 * NX) & (lane < 10 * NX)
    heights = jnp.broadcast_to(jnp.pad(h_ref[...], ((0, 0), (0, LANES - rows))), (HMAX, LANES))

    def emit(ref, high):
        v = vhi if high else vlo
        s = shi if high else slo
        r0 = rows - HMAX if high else 0
        for f in range(3):
            ref[:, f * cells : (f + 1) * cells] = v[f]
        for f in range(6):
            part = s[f].astype(F32)
            ref[:, (3 + f) * cells : (4 + f) * cells] = part[HMAX:] if high else part[:HMAX]
        zn = znear[r0 : r0 + HMAX, :]
        zf = zfar[r0 : r0 + HMAX, :]
        zl = jnp.where(gz_odd, zn, zf)
        zr = jnp.where(gz_odd, zf, zn)
        ref[:, tail : tail + LANES] = jnp.where(stamp, rot(heights, 9 * NX - r0), zl)
        ref[:, tail + LANES : tail + 2 * LANES] = zr

    @pl.when(gy_odd)
    def _():
        emit(near_ref, False)
        emit(far_ref, True)

    @pl.when(jnp.logical_not(gy_odd))
    def _():
        emit(near_ref, True)
        emit(far_ref, False)


def pack_wall(velocity, strain, heights, znear, zfar):
    rows, cells = velocity.shape[1:]
    width = 9 * cells + 2 * LANES
    return pl.pallas_call(
        pack_wall_kernel,
        grid=(1,),
        in_specs=[
            pl.BlockSpec((3, HMAX, cells), lambda i: (0, 0, 0)),
            pl.BlockSpec((3, HMAX, cells), lambda i: (0, rows // HMAX - 1, 0)),
            pl.BlockSpec((6, 2 * HMAX, cells), lambda i: (0, 0, 0)),
            pl.BlockSpec((6, 2 * HMAX, cells), lambda i: (0, rows // (2 * HMAX) - 1, 0)),
            pl.BlockSpec((1, rows), lambda i: (0, 0)),
            pl.BlockSpec((rows, LANES), lambda i: (0, 0)),
            pl.BlockSpec((rows, LANES), lambda i: (0, 0)),
        ],
        out_specs=[pl.BlockSpec((HMAX, width), lambda i: (0, 0))] * 2,
        out_shape=[jax.ShapeDtypeStruct((HMAX, width), F32)] * 2,
    )(velocity, velocity, strain, strain, heights, znear, zfar)


def plane_filter():
    k = np.arange(4 * LANES)[:, None]
    m = np.arange(2 * LANES)[None, :] + LANES
    turn = (k - m) % NX
    along = np.where(turn == 0, 0.5, np.where((turn == 1) | (turn == NX - 1), 0.25, 0.0))
    step = np.abs(k // NX - m // NX)
    across = np.where(step == 0, 0.5, np.where(step == 1, 0.25, 0.0))
    return jnp.asarray(along * across, BF16)


def split2(x):
    hi = x.astype(BF16)
    return hi, (x - hi.astype(F32)).astype(BF16)


def main_kernel(v_ref, s_ref, h_ref, reach_ref, znear, zfar, ynear, yfar, plane_ref, out_ref, raw, stack, fh, fl, smooth, acc):
    rows, cells = v_ref.shape[1:]
    tiles = cells // LANES
    ext = rows + 2 * HMAX
    total_planes = lax.axis_size("gy") * rows
    gy = lax.axis_index("gy")
    gz_odd = lax.axis_index("gz") % 2 == 1
    gy_odd = gy % 2 == 1
    offset = gy * rows
    tail = 9 * cells

    ylo = jnp.where(gy_odd, ynear[:, tail:], yfar[:, tail:])
    yhi = jnp.where(gy_odd, yfar[:, tail:], ynear[:, tail:])

    column = lane_iota((rows, LANES))
    place = jnp.where(column < rows, column, jnp.where(column < rows + HMAX, column - rows - HMAX, column - HMAX))
    row = lax.broadcasted_iota(jnp.int32, (rows, LANES), 0)
    hpad = jnp.pad(h_ref[...], ((0, 0), (0, LANES - rows)))
    hrow = lane_iota((1, LANES))
    hext = jnp.where(
        hrow < rows,
        hpad,
        jnp.where(hrow < rows + HMAX, rot(ylo[:, :LANES], rows - 9 * NX)[0:1], rot(yhi[:, :LANES], rows + HMAX - 9 * NX)[0:1]),
    )
    eye = row == column
    reach = jnp.pad(reach_ref[...].astype(F32), ((0, 0), (0, LANES - rows)))
    down = jnp.sum(jnp.where(eye, reach[0:1], 0.0), axis=1, keepdims=True).astype(jnp.int32)
    up = jnp.sum(jnp.where(eye, reach[1:2], 0.0), axis=1, keepdims=True).astype(jnp.int32)
    inside = (place >= row - down) & (place <= row + up) & (place + offset >= 0) & (place + offset < total_planes)
    inside = inside & (column < ext)
    weights = jnp.where(inside, jnp.broadcast_to(hext, (rows, LANES)), 0.0)
    inv = 1.0 / jnp.sum(weights, axis=1, keepdims=True)
    whi, wlo = split2(weights * inv)
    lhs = jnp.concatenate(
        [jnp.concatenate([whi, whi], axis=1), jnp.concatenate([wlo, jnp.zeros_like(wlo)], axis=1)], axis=0
    )

    zl_own = jnp.where(gz_odd, znear[...], zfar[...])
    zr_own = jnp.where(gz_odd, zfar[...], znear[...])
    zl = jnp.concatenate([zl_own, ylo[:, :LANES], yhi[:, :LANES]], axis=0)
    zr = jnp.concatenate([zr_own, ylo[:, LANES:], yhi[:, LANES:]], axis=0)
    elane = lane_iota((ext, LANES))
    for f in range(9):
        raw[f, 0:rows, 0:cells] = v_ref[f] if f < 3 else s_ref[f - 3].astype(F32)
        near = ynear[:, f * cells : (f + 1) * cells]
        far = yfar[:, f * cells : (f + 1) * cells]
        raw[f, rows : rows + HMAX, 0:cells] = jnp.where(gy_odd, near, far)
        raw[f, rows + HMAX : ext, 0:cells] = jnp.where(gy_odd, far, near)
        edge = jnp.where(elane < NX, rot(zr, -NX * f), jnp.where(elane >= LANES - NX, rot(zl, -NX * f - NX), 0.0))
        raw[f, 0:ext, cells : cells + LANES] = edge
    stack[...] = jnp.zeros_like(stack)

    def tile_step(t, carry):
        at = pl.ds(pl.multiple_of(t * LANES, LANES), LANES)
        to = pl.ds(pl.multiple_of(t * LANES + LANES, LANES), LANES)
        for r in range(0, ext, 16):
            u = [raw[f, r : r + 16, at] for f in range(3)]
            s = [raw[f, r : r + 16, at] for f in range(3, 9)]
            rate = strain_rate(s)
            fields = u + [u[a] * u[b] for a, b in zip(LEAD_INDEX, TAIL_INDEX)] + s + [rate * x for x in s]
            for f in range(21):
                hi, lo = split2(fields[f])
                stack[r : r + 16, f * LANES : (f + 1) * LANES] = hi
                stack[LANES + r : LANES + r + 16, f * LANES : (f + 1) * LANES] = lo
        both = jnp.dot(lhs, stack[...], preferred_element_type=F32)
        merged = both[:rows] + both[rows:]
        for f in range(21):
            hi, lo = split2(merged[:, f * LANES : (f + 1) * LANES])
            fh[f, :, to] = hi
            fl[f, :, to] = lo
        return carry

    lax.fori_loop(0, tiles + 1, tile_step, 0)

    fh[:, :, 0:LANES] = fh[:, :, cells + LANES :]
    fl[:, :, 0:LANES] = fl[:, :, cells + LANES :]
    acc[...] = jnp.zeros_like(acc)

    def block_step(n, carry):
        at = pl.ds(pl.multiple_of(n * 2 * LANES, LANES), 4 * LANES)
        for f in range(21):
            hi = jnp.dot(fh[f, :, at], plane_ref[...], preferred_element_type=F32)
            lo = jnp.dot(fl[f, :, at], plane_ref[...], preferred_element_type=F32)
            smooth[f] = hi + lo
        for r in range(0, rows, HMAX):
            rr = slice(r, r + HMAX)
            for c in range(2):
                g = [smooth[f, rr, c * LANES : (c + 1) * LANES] for f in range(21)]
                u, p, s, m = g[0:3], g[3:9], g[9:15], g[15:21]
                rate = 4.0 * strain_rate(s)
                num = acc[0, rr, :]
                den = acc[1, rr, :]
                for k in range(6):
                    leonard = p[k] - u[LEAD_INDEX[k]] * u[TAIL_INDEX[k]]
                    model = m[k] - rate * s[k]
                    weighted = TENSOR_WEIGHTS[k] * model
                    num = num + weighted * leonard
                    den = den + weighted * model
                acc[0, rr, :] = num
                acc[1, rr, :] = den
        return carry

    lax.fori_loop(0, tiles // 2, block_step, 0)
    ones = jnp.ones((HMAX, LANES), F32)
    for k in range(2):
        sums = lax.dot_general(
            ones, acc[k], (((1,), (1,)), ((), ())), precision=lax.Precision.HIGHEST, preferred_element_type=F32
        )
        out_ref[k : k + 1, :] = sums[0:1]


def main_call(velocity, strain, heights, reach, znear, zfar, ynear, yfar):
    rows, cells = velocity.shape[1:]
    ext = rows + 2 * HMAX
    vmem = pl.BlockSpec(memory_space=pltpu.VMEM)
    return pl.pallas_call(
        main_kernel,
        in_specs=[vmem] * 9,
        out_specs=vmem,
        out_shape=jax.ShapeDtypeStruct((2, rows), F32),
        scratch_shapes=[
            pltpu.VMEM((9, ext, cells + LANES), F32),
            pltpu.VMEM((2 * LANES, 21 * LANES), BF16),
            pltpu.VMEM((21, rows, cells + 2 * LANES), BF16),
            pltpu.VMEM((21, rows, cells + 2 * LANES), BF16),
            pltpu.VMEM((21, rows, 2 * LANES), F32),
            pltpu.VMEM((2, rows, LANES), F32),
        ],
        compiler_params=pltpu.CompilerParams(vmem_limit_bytes=40 * 1024 * 1024),
    )(velocity, strain, heights, reach, znear, zfar, ynear, yfar, plane_filter())


def near_pairs(axis):
    return [(i, i ^ 1) for i in range(lax.axis_size(axis))]


def far_pairs(axis, closed):
    n = lax.axis_size(axis)
    pairs = []
    for i in range(1, n if closed else n - 1, 2):
        pairs += [(i, (i + 1) % n), ((i + 1) % n, i)]
    return pairs


def local(velocity, strain, cell_height, stencil_reach):
    rows, cells = velocity.shape[1:]
    heights = cell_height.reshape(1, rows)
    near, far = pack_span(velocity, strain)
    zfar = lax.ppermute(far, "gz", far_pairs("gz", True))
    znear = lax.ppermute(near, "gz", near_pairs("gz"))
    near, far = pack_wall(velocity, strain, heights, znear, zfar)
    yfar = lax.ppermute(far, "gy", far_pairs("gy", False))
    ynear = lax.ppermute(near, "gy", near_pairs("gy"))
    sums = main_call(velocity, strain, heights, stencil_reach, znear, zfar, ynear, yfar)
    for mask in (1, 3, 4, 12):
        sums = sums + lax.ppermute(sums, "gz", [(i, i ^ mask) for i in range(16)])
    total = lax.axis_size("gz") * cells
    return sums[0] / total / (sums[1] / total + 1e-06)


def solution(mesh):
    in_specs = (P(None, "gy", "gz"), P(None, "gy", "gz"), P("gy"), P(None, "gy"))
    return jax.shard_map(local, mesh=mesh, in_specs=in_specs, out_specs=P("gy"), check_vma=False)
```

```python
import jax
import jax.numpy as jnp
import numpy as np
from jax import lax
from jax.experimental import pallas as pl
from jax.experimental.pallas import tpu as pltpu
from jax.sharding import PartitionSpec as P

NX = 8
HMAX = 8
LANES = 128
LEAD_INDEX = (0, 1, 2, 0, 0, 1)
TAIL_INDEX = (0, 1, 2, 1, 2, 2)
TENSOR_WEIGHTS = (1.0, 1.0, 1.0, 2.0, 2.0, 2.0)
F32 = jnp.float32
BF16 = jnp.bfloat16


def strain_rate(s):
    squares = 2.0 * (s[0] * s[0] + s[1] * s[1] + s[2] * s[2])
    squares = squares + 4.0 * (s[3] * s[3] + s[4] * s[4] + s[5] * s[5])
    return jnp.sqrt(squares)


def lane_iota(shape):
    return lax.broadcasted_iota(jnp.int32, shape, len(shape) - 1)


def rot(x, amount):
    amount = amount % LANES
    return pltpu.roll(x, amount, x.ndim - 1) if amount else x


def pack_span_kernel(v_ref, s_ref, near_ref, far_ref):
    rows, cells = v_ref.shape[1:]
    lane = lane_iota((rows, LANES))
    left = jnp.zeros((rows, LANES), F32)
    right = jnp.zeros((rows, LANES), F32)
    for f in range(9):
        ref, at = (v_ref, f) if f < 3 else (s_ref, f - 3)
        here = (lane >= NX * f) & (lane < NX * (f + 1))
        left = jnp.where(here, rot(ref[at, :, :LANES].astype(F32), NX * f), left)
        right = jnp.where(here, rot(ref[at, :, cells - LANES :].astype(F32), NX * f + NX), right)
    odd = lax.axis_index("gz") % 2 == 1
    near_ref[...] = jnp.where(odd, left, right)
    far_ref[...] = jnp.where(odd, right, left)


def pack_span(velocity, strain):
    rows = velocity.shape[1]
    vmem = pl.BlockSpec(memory_space=pltpu.VMEM)
    return pl.pallas_call(
        pack_span_kernel,
        in_specs=[vmem] * 2,
        out_specs=[vmem] * 2,
        out_shape=[jax.ShapeDtypeStruct((rows, LANES), F32)] * 2,
        compiler_params=pltpu.CompilerParams(vmem_limit_bytes=4 * 1024 * 1024),
    )(velocity, strain)


def pack_wall_kernel(v_ref, s_ref, h_ref, znear, zfar, near_ref, far_ref):
    rows, cells = v_ref.shape[1:]
    gz_odd = lax.axis_index("gz") % 2 == 1
    gy_odd = lax.axis_index("gy") % 2 == 1
    tail = 9 * cells
    lane = lane_iota((HMAX, LANES))
    row = lax.broadcasted_iota(jnp.int32, (HMAX, LANES), 0)
    stamp = (row == 0) & (lane >= 9 * NX) & (lane < 10 * NX)
    heights = jnp.broadcast_to(jnp.pad(h_ref[...], ((0, 0), (0, LANES - rows))), (HMAX, LANES))

    def emit(ref, high):
        r0 = rows - HMAX if high else 0
        for f in range(3):
            ref[:, f * cells : (f + 1) * cells] = v_ref[f, r0 : r0 + HMAX, :]
        for f in range(6):
            part = (s_ref[f, rows - 2 * HMAX :, :] if high else s_ref[f, : 2 * HMAX, :]).astype(F32)
            ref[:, (3 + f) * cells : (4 + f) * cells] = part[HMAX:] if high else part[:HMAX]
        zn = znear[r0 : r0 + HMAX, :]
        zf = zfar[r0 : r0 + HMAX, :]
        zl = jnp.where(gz_odd, zn, zf)
        zr = jnp.where(gz_odd, zf, zn)
        ref[:, tail : tail + LANES] = jnp.where(stamp, rot(heights, 9 * NX - r0), zl)
        ref[:, tail + LANES : tail + 2 * LANES] = zr

    @pl.when(gy_odd)
    def _():
        emit(near_ref, False)
        emit(far_ref, True)

    @pl.when(jnp.logical_not(gy_odd))
    def _():
        emit(near_ref, True)
        emit(far_ref, False)


def pack_wall(velocity, strain, heights, znear, zfar):
    rows, cells = velocity.shape[1:]
    width = 9 * cells + 2 * LANES
    vmem = pl.BlockSpec(memory_space=pltpu.VMEM)
    return pl.pallas_call(
        pack_wall_kernel,
        in_specs=[vmem] * 5,
        out_specs=[vmem] * 2,
        out_shape=[jax.ShapeDtypeStruct((HMAX, width), F32)] * 2,
        compiler_params=pltpu.CompilerParams(vmem_limit_bytes=4 * 1024 * 1024),
    )(velocity, strain, heights, znear, zfar)


def plane_filter():
    k = np.arange(4 * LANES)[:, None]
    m = np.arange(2 * LANES)[None, :] + LANES
    turn = (k - m) % NX
    along = np.where(turn == 0, 0.5, np.where((turn == 1) | (turn == NX - 1), 0.25, 0.0))
    step = np.abs(k // NX - m // NX)
    across = np.where(step == 0, 0.5, np.where(step == 1, 0.25, 0.0))
    full = along * across
    edge = np.concatenate([full[3 * LANES : 3 * LANES + LANES // 2], full[LANES // 2 : LANES]])
    middle = full[LANES : 3 * LANES]
    return jnp.asarray(np.concatenate([middle, edge, edge, middle]), BF16)


def split2(x):
    hi = x.astype(BF16)
    return hi, (x - hi.astype(F32)).astype(BF16)


def main_kernel(v_ref, s_ref, h_ref, reach_ref, znear, zfar, ynear, yfar, plane_ref, out_ref, raw, stack, fh, fl, smooth, acc):
    rows, cells = v_ref.shape[1:]
    tiles = cells // LANES
    ext = rows + 2 * HMAX
    total_planes = lax.axis_size("gy") * rows
    gy = lax.axis_index("gy")
    gz_odd = lax.axis_index("gz") % 2 == 1
    gy_odd = gy % 2 == 1
    offset = gy * rows
    tail = 9 * cells

    ylo = jnp.where(gy_odd, ynear[:, tail:], yfar[:, tail:])
    yhi = jnp.where(gy_odd, yfar[:, tail:], ynear[:, tail:])

    column = lane_iota((rows, LANES))
    place = jnp.where(column < rows, column, jnp.where(column < rows + HMAX, column - rows - HMAX, column - HMAX))
    row = lax.broadcasted_iota(jnp.int32, (rows, LANES), 0)
    hpad = jnp.pad(h_ref[...], ((0, 0), (0, LANES - rows)))
    hrow = lane_iota((1, LANES))
    hext = jnp.where(
        hrow < rows,
        hpad,
        jnp.where(hrow < rows + HMAX, rot(ylo[:, :LANES], rows - 9 * NX)[0:1], rot(yhi[:, :LANES], rows + HMAX - 9 * NX)[0:1]),
    )
    eye = row == column
    reach = jnp.pad(reach_ref[...].astype(F32), ((0, 0), (0, LANES - rows)))
    down = jnp.sum(jnp.where(eye, reach[0:1], 0.0), axis=1, keepdims=True).astype(jnp.int32)
    up = jnp.sum(jnp.where(eye, reach[1:2], 0.0), axis=1, keepdims=True).astype(jnp.int32)
    inside = (place >= row - down) & (place <= row + up) & (place + offset >= 0) & (place + offset < total_planes)
    inside = inside & (column < ext)
    weights = jnp.where(inside, jnp.broadcast_to(hext, (rows, LANES)), 0.0)
    inv = 1.0 / jnp.sum(weights, axis=1, keepdims=True)
    whi, wlo = split2(weights * inv)
    lhs = jnp.concatenate(
        [jnp.concatenate([whi, whi], axis=1), jnp.concatenate([wlo, jnp.zeros_like(wlo)], axis=1)], axis=0
    )

    zl_own = jnp.where(gz_odd, znear[...], zfar[...])
    zr_own = jnp.where(gz_odd, zfar[...], znear[...])
    zl = jnp.concatenate([zl_own, ylo[:, :LANES], yhi[:, :LANES]], axis=0)
    zr = jnp.concatenate([zr_own, ylo[:, LANES:], yhi[:, LANES:]], axis=0)
    elane = lane_iota((ext, LANES))
    for f in range(9):
        raw[f, 0:rows, 0:cells] = v_ref[f] if f < 3 else s_ref[f - 3].astype(F32)
        near = ynear[:, f * cells : (f + 1) * cells]
        far = yfar[:, f * cells : (f + 1) * cells]
        raw[f, rows : rows + HMAX, 0:cells] = jnp.where(gy_odd, near, far)
        raw[f, rows + HMAX : ext, 0:cells] = jnp.where(gy_odd, far, near)
        edge = jnp.where(elane < NX, rot(zr, -NX * f), jnp.where(elane >= LANES - NX, rot(zl, -NX * f - NX), 0.0))
        raw[f, 0:ext, cells : cells + LANES] = edge
    stack[...] = jnp.zeros_like(stack)

    def tile_step(t, carry):
        at = pl.ds(pl.multiple_of(t * LANES, LANES), LANES)
        for r in range(0, ext, 16):
            u = [raw[f, r : r + 16, at] for f in range(3)]
            s = [raw[f, r : r + 16, at] for f in range(3, 9)]
            rate = strain_rate(s)
            fields = u + [u[a] * u[b] for a, b in zip(LEAD_INDEX, TAIL_INDEX)] + s + [rate * x for x in s]
            for f in range(21):
                hi, lo = split2(fields[f])
                stack[r : r + 16, f * LANES : (f + 1) * LANES] = hi
                stack[LANES + r : LANES + r + 16, f * LANES : (f + 1) * LANES] = lo
        both = jnp.dot(lhs, stack[...], preferred_element_type=F32)
        merged = both[:rows] + both[rows:]
        for f in range(21):
            hi, lo = split2(merged[:, f * LANES : (f + 1) * LANES])
            fh[f, :, at] = hi
            fl[f, :, at] = lo
        return carry

    lax.fori_loop(0, tiles + 1, tile_step, 0, unroll=True)

    acc[...] = jnp.zeros_like(acc)
    pick = lane_iota((21, rows, LANES)) < LANES // 2

    for n in range(tiles // 2):
        at = slice(2 * n * LANES, (2 * n + 2) * LANES)
        before = (2 * n - 1 if n else tiles) * LANES
        after = (2 * n + 2) * LANES
        edge_hi = jnp.where(pick, fh[:, :, after : after + LANES], fh[:, :, before : before + LANES])
        edge_lo = jnp.where(pick, fl[:, :, after : after + LANES], fl[:, :, before : before + LANES])
        lhs_plane = jnp.concatenate([fh[:, :, at], edge_hi, edge_lo, fl[:, :, at]], axis=-1)
        lhs_plane = lhs_plane.reshape(21 * rows, 6 * LANES)
        smooth[...] = jnp.dot(lhs_plane, plane_ref[...], preferred_element_type=F32).reshape(21, rows, 2 * LANES)
        for r in range(0, rows, HMAX):
            rr = slice(r, r + HMAX)
            for c in range(2):
                g = [smooth[f, rr, c * LANES : (c + 1) * LANES] for f in range(21)]
                u, p, s, m = g[0:3], g[3:9], g[9:15], g[15:21]
                rate = 4.0 * strain_rate(s)
                num = acc[0, rr, :]
                den = acc[1, rr, :]
                for k in range(6):
                    leonard = p[k] - u[LEAD_INDEX[k]] * u[TAIL_INDEX[k]]
                    model = m[k] - rate * s[k]
                    weighted = TENSOR_WEIGHTS[k] * model
                    num = num + weighted * leonard
                    den = den + weighted * model
                acc[0, rr, :] = num
                acc[1, rr, :] = den

    ones = jnp.ones((HMAX, LANES), F32)
    for k in range(2):
        sums = lax.dot_general(
            ones, acc[k], (((1,), (1,)), ((), ())), precision=lax.Precision.HIGHEST, preferred_element_type=F32
        )
        out_ref[:, k : k + 1, :] = jnp.broadcast_to(sums[0:1][None], (out_ref.shape[0], 1, rows))


def main_call(velocity, strain, heights, reach, znear, zfar, ynear, yfar):
    rows, cells = velocity.shape[1:]
    ext = rows + 2 * HMAX
    vmem = pl.BlockSpec(memory_space=pltpu.VMEM)
    return pl.pallas_call(
        main_kernel,
        in_specs=[vmem] * 9,
        out_specs=vmem,
        out_shape=jax.ShapeDtypeStruct((lax.axis_size("gz"), 2, rows), F32),
        scratch_shapes=[
            pltpu.VMEM((9, ext, cells + LANES), F32),
            pltpu.VMEM((2 * LANES, 21 * LANES), BF16),
            pltpu.VMEM((21, rows, cells + LANES), BF16),
            pltpu.VMEM((21, rows, cells + LANES), BF16),
            pltpu.VMEM((21, rows, 2 * LANES), F32),
            pltpu.VMEM((2, rows, LANES), F32),
        ],
        compiler_params=pltpu.CompilerParams(vmem_limit_bytes=32 * 1024 * 1024),
    )(velocity, strain, heights, reach, znear, zfar, ynear, yfar, plane_filter())


def near_pairs(axis):
    return [(i, i ^ 1) for i in range(lax.axis_size(axis))]


def far_pairs(axis, closed):
    n = lax.axis_size(axis)
    pairs = []
    for i in range(1, n if closed else n - 1, 2):
        pairs += [(i, (i + 1) % n), ((i + 1) % n, i)]
    return pairs


def local(velocity, strain, cell_height, stencil_reach):
    rows, cells = velocity.shape[1:]
    heights = cell_height.reshape(1, rows)
    near, far = pack_span(velocity, strain)
    zfar = lax.ppermute(far, "gz", far_pairs("gz", True))
    znear = lax.ppermute(near, "gz", near_pairs("gz"))
    near, far = pack_wall(velocity, strain, heights, znear, zfar)
    yfar = lax.ppermute(far, "gy", far_pairs("gy", False))
    ynear = lax.ppermute(near, "gy", near_pairs("gy"))
    sums = main_call(velocity, strain, heights, stencil_reach, znear, zfar, ynear, yfar)
    sums = jnp.sum(lax.all_to_all(sums, "gz", 0, 0), axis=0)
    total = lax.axis_size("gz") * cells
    return sums[0] / total / (sums[1] / total + 1e-06)


def solution(mesh):
    in_specs = (P(None, "gy", "gz"), P(None, "gy", "gz"), P("gy"), P(None, "gy"))
    return jax.shard_map(local, mesh=mesh, in_specs=in_specs, out_specs=P("gy"), check_vma=False)
```

```python
import jax
import jax.numpy as jnp
from jax import lax
from jax.experimental import pallas as pl
from jax.experimental.pallas import tpu as pltpu
from jax.sharding import PartitionSpec as P

NX = 8
HMAX = 8
LANES = 128
FIELDS = 21
WIDE = 15
FIRST_VMEM = 51 * 1024 * 1024
SMALL_VMEM = 24 * 1024 * 1024
LARGE_VMEM = 24 * 1024 * 1024
LEAD_INDEX = (0, 1, 2, 0, 0, 1)
TAIL_INDEX = (0, 1, 2, 1, 2, 2)
TENSOR_WEIGHTS = (1.0, 1.0, 1.0, 2.0, 2.0, 2.0)
F32 = jnp.float32
BF16 = jnp.bfloat16


def strain_rate(s):
    squares = 2.0 * (s[0] * s[0] + s[1] * s[1] + s[2] * s[2])
    squares = squares + 4.0 * (s[3] * s[3] + s[4] * s[4] + s[5] * s[5])
    return jnp.sqrt(squares)


def lane_iota(shape):
    return lax.broadcasted_iota(jnp.int32, shape, len(shape) - 1)


def rot(x, amount):
    amount = amount % LANES
    return pltpu.roll(x, amount, x.ndim - 1) if amount else x


def plane_filter():
    shape = (3 * LANES, 2 * LANES)
    k = lax.broadcasted_iota(jnp.int32, shape, 0)
    m = lane_iota(shape)
    k = jnp.where(k < 5 * LANES // 2, k, k - 3 * LANES)
    turn = (k - m) & (NX - 1)
    along = jnp.where(turn == 0, 0.5, jnp.where((turn == 1) | (turn == NX - 1), 0.25, 0.0))
    step = ((k + LANES) >> 3) - ((m + LANES) >> 3)
    across = jnp.where(step == 0, 0.5, jnp.where((step == 1) | (step == -1), 0.25, 0.0))
    return (along * across).astype(BF16)


def pack_span_kernel(v_ref, s_ref, near_ref, far_ref, v_out, s_out, plane_ref, sems):
    rows, cells = v_ref.shape[1:]
    spans = ((0, LANES), (cells - LANES, LANES), (LANES, cells - 2 * LANES))
    copies = []
    for i, (start, size) in enumerate(spans):
        for j, (ref, out) in enumerate(((v_ref, v_out), (s_ref, s_out))):
            at = pl.ds(start, size)
            copies.append(pltpu.make_async_copy(ref.at[:, :, at], out.at[:, :, at], sems.at[i, j]))
    for copy in copies:
        copy.start()
    once = plane_filter()
    plane_ref[: 3 * LANES] = once
    plane_ref[3 * LANES :] = once
    for copy in copies[:4]:
        copy.wait()
    lane = lane_iota((rows, LANES))
    left = jnp.zeros((rows, LANES), F32)
    right = jnp.zeros((rows, LANES), F32)
    for f in range(9):
        ref, at = (v_out, f) if f < 3 else (s_out, f - 3)
        here = (lane >= NX * f) & (lane < NX * (f + 1))
        left = jnp.where(here, rot(ref[at, :, :LANES].astype(F32), NX * f), left)
        right = jnp.where(here, rot(ref[at, :, cells - LANES :].astype(F32), NX * f + NX), right)
    odd = lax.axis_index("gz") % 2 == 1
    near_ref[...] = jnp.where(odd, left, right)
    far_ref[...] = jnp.where(odd, right, left)
    for copy in copies[4:]:
        copy.wait()


def pack_span(velocity, strain):
    rows = velocity.shape[1]
    hbm = pl.BlockSpec(memory_space=pltpu.HBM)
    vmem = pl.BlockSpec(memory_space=pltpu.VMEM)
    return pl.pallas_call(
        pack_span_kernel,
        in_specs=[hbm] * 2,
        out_specs=[vmem] * 5,
        out_shape=[jax.ShapeDtypeStruct((rows, LANES), F32)] * 2
        + [jax.ShapeDtypeStruct(x.shape, x.dtype) for x in (velocity, strain)]
        + [jax.ShapeDtypeStruct((6 * LANES, 2 * LANES), BF16)],
        scratch_shapes=[pltpu.SemaphoreType.DMA((3, 2))],
        compiler_params=pltpu.CompilerParams(vmem_limit_bytes=FIRST_VMEM),
    )(velocity, strain)


def pack_wall_kernel(v_ref, s_ref, h_ref, znear, zfar, near_ref, far_ref):
    rows, cells = v_ref.shape[1:]
    gz_odd = lax.axis_index("gz") % 2 == 1
    gy_odd = lax.axis_index("gy") % 2 == 1
    tail = 9 * cells
    lane = lane_iota((HMAX, LANES))
    row = lax.broadcasted_iota(jnp.int32, (HMAX, LANES), 0)
    stamp = (row == 0) & (lane >= 9 * NX) & (lane < 10 * NX)
    heights = jnp.broadcast_to(jnp.pad(h_ref[...], ((0, 0), (0, LANES - rows))), (HMAX, LANES))

    def emit(ref, high):
        r0 = rows - HMAX if high else 0
        for f in range(3):
            ref[:, f * cells : (f + 1) * cells] = v_ref[f, r0 : r0 + HMAX, :]
        for f in range(6):
            part = (s_ref[f, rows - 2 * HMAX :, :] if high else s_ref[f, : 2 * HMAX, :]).astype(F32)
            ref[:, (3 + f) * cells : (4 + f) * cells] = part[HMAX:] if high else part[:HMAX]
        zn = znear[r0 : r0 + HMAX, :]
        zf = zfar[r0 : r0 + HMAX, :]
        zl = jnp.where(gz_odd, zn, zf)
        zr = jnp.where(gz_odd, zf, zn)
        ref[:, tail : tail + LANES] = jnp.where(stamp, rot(heights, 9 * NX - r0), zl)
        ref[:, tail + LANES : tail + 2 * LANES] = zr

    @pl.when(gy_odd)
    def _():
        emit(near_ref, False)
        emit(far_ref, True)

    @pl.when(jnp.logical_not(gy_odd))
    def _():
        emit(near_ref, True)
        emit(far_ref, False)


def pack_wall(velocity, strain, heights, znear, zfar):
    rows, cells = velocity.shape[1:]
    width = 9 * cells + 2 * LANES
    vmem = pl.BlockSpec(memory_space=pltpu.VMEM)
    return pl.pallas_call(
        pack_wall_kernel,
        in_specs=[vmem] * 5,
        out_specs=[vmem] * 2,
        out_shape=[jax.ShapeDtypeStruct((HMAX, width), F32)] * 2,
        compiler_params=pltpu.CompilerParams(vmem_limit_bytes=SMALL_VMEM),
    )(velocity, strain, heights, znear, zfar)


def split2(x):
    hi = x.astype(BF16)
    return hi, (x - hi.astype(F32)).astype(BF16)


def store_fields(u, s, put_high, put_low):
    tensor = [x.astype(F32) for x in s]
    rate = strain_rate(tensor)
    wide = u + [u[a] * u[b] for a, b in zip(LEAD_INDEX, TAIL_INDEX)] + [rate * x for x in tensor]
    for f, value in enumerate(wide):
        hi, lo = split2(value)
        put_high(f, hi)
        put_low(f, lo)
    for f, value in enumerate(s):
        put_high(WIDE + f, value.astype(BF16))


def smooth_block(n, tiles, fh, fl, eh, el, plane_ref):
    rows = fh.shape[1]
    at = slice(2 * n * LANES, (2 * n + 2) * LANES)

    def edge(ref, outer, fields):
        before = ref[fields, :, (2 * n - 1) * LANES : 2 * n * LANES] if n else outer[fields]
        after = ref[fields, :, (2 * n + 2) * LANES : (2 * n + 3) * LANES] if 2 * n + 2 < tiles else outer[fields]
        return jnp.where(lane_iota(before.shape) < LANES // 2, after, before)

    wide, narrow = slice(0, WIDE), slice(WIDE, FIELDS)
    lhs = jnp.concatenate([fh[wide, :, at], edge(fh, eh, wide), fl[wide, :, at], edge(fl, el, wide)], axis=-1)
    first = jnp.dot(lhs.reshape(WIDE * rows, 6 * LANES), plane_ref[...], preferred_element_type=F32)
    lhs = jnp.concatenate([fh[narrow, :, at], edge(fh, eh, narrow)], axis=-1)
    second = jnp.dot(
        lhs.reshape((FIELDS - WIDE) * rows, 3 * LANES), plane_ref[: 3 * LANES], preferred_element_type=F32
    )
    return [first[f * rows : (f + 1) * rows] for f in range(WIDE)] + [
        second[f * rows : (f + 1) * rows] for f in range(FIELDS - WIDE)
    ]


def contract(g, num, den):
    u, p, m, s = g[0:3], g[3:9], g[9:15], g[15:21]
    rate = 4.0 * strain_rate(s)
    for k in range(6):
        leonard = p[k] - u[LEAD_INDEX[k]] * u[TAIL_INDEX[k]]
        model = m[k] - rate * s[k]
        weighted = TENSOR_WEIGHTS[k] * model
        num = num + weighted * leonard
        den = den + weighted * model
    return num, den


def wall_inside(reach_ref, rows, offset, total_planes):
    column = lane_iota((rows, LANES))
    place = jnp.where(column < rows, column, jnp.where(column < rows + HMAX, column - rows - HMAX, column - HMAX))
    row = lax.broadcasted_iota(jnp.int32, (rows, LANES), 0)
    eye = row == column
    reach = jnp.pad(reach_ref[...].astype(F32), ((0, 0), (0, LANES - rows)))
    down = jnp.sum(jnp.where(eye, reach[0:1], 0.0), axis=1, keepdims=True).astype(jnp.int32)
    up = jnp.sum(jnp.where(eye, reach[1:2], 0.0), axis=1, keepdims=True).astype(jnp.int32)
    inside = (place >= row - down) & (place <= row + up) & (place + offset >= 0) & (place + offset < total_planes)
    return inside & (column < rows + 2 * HMAX)


def wall_block(g, lhs_ref, stack, acc_ref, part_ref):
    rows = g[0].shape[0]
    width = 2 * LANES
    for f in range(FIELDS):
        hi, lo = split2(g[f])
        stack[0:rows, f * width : (f + 1) * width] = hi
        stack[LANES : LANES + rows, f * width : (f + 1) * width] = lo
    both = jnp.dot(lhs_ref[...], stack[...], preferred_element_type=F32)
    merged = both[:rows] + both[rows:]
    for f in range(FIELDS):
        part_ref[f, 0:HMAX, :] = merged[0:HMAX, f * width : (f + 1) * width]
        part_ref[f, HMAX:, :] = merged[rows - HMAX :, f * width : (f + 1) * width]
    for r in range(HMAX, rows - HMAX, HMAX):
        num = acc_ref[0, r : r + HMAX, :]
        den = acc_ref[1, r : r + HMAX, :]
        for c in range(2):
            parts = [
                merged[r : r + HMAX, f * width + c * LANES : f * width + (c + 1) * LANES] for f in range(FIELDS)
            ]
            num, den = contract(parts, num, den)
        acc_ref[0, r : r + HMAX, :] = num
        acc_ref[1, r : r + HMAX, :] = den


def clear_gaps(stack, rows):
    gap = jnp.zeros((LANES - rows, stack.shape[1]), BF16)
    stack[rows:LANES, :] = gap
    stack[LANES + rows :, :] = gap


def inner_kernel(v_ref, s_ref, h_ref, reach_ref, plane_ref, fh, fl, lhs_ref, acc_ref, part_ref, stack):
    rows, cells = v_ref.shape[1:]
    tiles = cells // LANES
    total_planes = lax.axis_size("gy") * rows
    offset = lax.axis_index("gy") * rows
    column = lane_iota((rows, LANES))
    row = lax.broadcasted_iota(jnp.int32, (rows, LANES), 0)
    inside = wall_inside(reach_ref, rows, offset, total_planes) & (column < rows)
    hpad = jnp.pad(h_ref[...], ((0, 0), (0, LANES - rows)))
    weights = jnp.where(inside, jnp.broadcast_to(hpad, (rows, LANES)), 0.0)
    whole = (row >= HMAX) & (row < rows - HMAX)
    weights = jnp.where(whole, weights / jnp.sum(weights, axis=1, keepdims=True), weights)
    whi, wlo = split2(weights)
    lhs_ref[0:rows, 0:LANES] = whi
    lhs_ref[0:rows, LANES:] = whi
    lhs_ref[rows:, 0:LANES] = wlo
    lhs_ref[rows:, LANES:] = jnp.zeros_like(wlo)
    clear_gaps(stack, rows)
    acc_ref[...] = jnp.zeros_like(acc_ref)
    for t in range(tiles):
        at = slice(t * LANES, (t + 1) * LANES)
        for r in range(0, rows, 16):
            rr = slice(r, r + 16)

            def put_high(f, x):
                fh[f, rr, at] = x

            def put_low(f, x):
                fl[f, rr, at] = x

            store_fields(
                [v_ref[f, rr, at] for f in range(3)], [s_ref[f, rr, at] for f in range(6)], put_high, put_low
            )
    for n in range(1, tiles // 2 - 1):
        g = smooth_block(n, tiles, fh, fl, None, None, plane_ref)
        wall_block(g, lhs_ref, stack, acc_ref, part_ref.at[n - 1])


def outer_kernel(fh, fl, lhs_ref, acc_in, znear, zfar, plane_ref, acc_ref, part_ref, eh, el, stack):
    rows, cells = fh.shape[1:]
    tiles = cells // LANES
    gz_odd = lax.axis_index("gz") % 2 == 1
    clear_gaps(stack, rows)
    acc_ref[...] = acc_in[...]
    edge_fields(jnp.where(gz_odd, znear[...], zfar[...]), jnp.where(gz_odd, zfar[...], znear[...]), eh, el)
    for i, n in enumerate((0, tiles // 2 - 1)):
        g = smooth_block(n, tiles, fh, fl, eh, el, plane_ref)
        wall_block(g, lhs_ref, stack, acc_ref, part_ref.at[i])


def edge_fields(zl, zr, eh, el):
    rows = zl.shape[0]
    lane = lane_iota((16, LANES))
    for r in range(0, rows, 16):
        rr = slice(r, r + 16)
        raw = [
            jnp.where(
                lane < NX, rot(zr[rr], -NX * f), jnp.where(lane >= LANES - NX, rot(zl[rr], -NX * f - NX), 0.0)
            )
            for f in range(9)
        ]

        def put_high(f, x):
            eh[f, rr, :] = x

        def put_low(f, x):
            el[f, rr, :] = x

        store_fields(raw[:3], raw[3:], put_high, put_low)


def last_kernel(h_ref, reach_ref, ynear, yfar, acc_in, part_inner, part_outer, plane_ref, out_ref, fh, fl, eh, el, stack, acc):
    rows = h_ref.shape[1]
    cells = (ynear.shape[1] - 2 * LANES) // 9
    tiles = cells // LANES
    width = 2 * LANES
    total_planes = lax.axis_size("gy") * rows
    gy = lax.axis_index("gy")
    gy_odd = gy % 2 == 1
    tail = 9 * cells
    both_rows = 2 * HMAX

    def halo(at):
        near, far = ynear[:, at], yfar[:, at]
        return jnp.concatenate([jnp.where(gy_odd, near, far), jnp.where(gy_odd, far, near)], axis=0)

    zl = halo(slice(tail, tail + LANES))
    zr = halo(slice(tail + LANES, tail + 2 * LANES))
    hpad = jnp.pad(h_ref[...], ((0, 0), (0, LANES - rows)))
    hrow = lane_iota((1, LANES))
    below = rot(zl[:HMAX], rows - 9 * NX)[0:1]
    above = rot(zl[HMAX:], rows + HMAX - 9 * NX)[0:1]
    hext = jnp.where(hrow < rows, hpad, jnp.where(hrow < rows + HMAX, below, above))
    inside = wall_inside(reach_ref, rows, gy * rows, total_planes)
    weights = jnp.where(inside, jnp.broadcast_to(hext, (rows, LANES)), 0.0)
    weights = jnp.concatenate([weights[:HMAX], weights[rows - HMAX :]], axis=0)
    scale = 1.0 / jnp.sum(weights, axis=1, keepdims=True)
    lane = lane_iota((both_rows, LANES))
    outside = jnp.where(lane < both_rows, rot(weights, -rows), 0.0)
    whi, wlo = split2(outside)
    twice = whi.astype(F32) + rot(whi.astype(F32), both_rows)
    lhs = jnp.concatenate([twice, wlo.astype(F32)], axis=0).astype(BF16)[:, : 2 * both_rows]

    edge_fields(zl, zr, eh, el)
    for t in range(tiles):
        at = slice(t * LANES, (t + 1) * LANES)

        def put_high(f, x):
            fh[f, :, at] = x

        def put_low(f, x):
            fl[f, :, at] = x

        raw = [halo(slice(f * cells + t * LANES, f * cells + (t + 1) * LANES)) for f in range(9)]
        store_fields(raw[:3], raw[3:], put_high, put_low)

    zero = jnp.zeros((HMAX, LANES), F32)
    sums = [[zero, zero], [zero, zero]]
    for n in range(tiles // 2):
        g = smooth_block(n, tiles, fh, fl, eh, el, plane_ref)
        for f in range(FIELDS):
            hi, lo = split2(g[f])
            stack[0:both_rows, f * width : (f + 1) * width] = hi
            stack[both_rows:, f * width : (f + 1) * width] = lo
        both = jnp.dot(lhs, stack[...], preferred_element_type=F32)
        merged = both[:both_rows] + both[both_rows:]
        if n == 0:
            part = part_outer.at[0]
        elif n == tiles // 2 - 1:
            part = part_outer.at[1]
        else:
            part = part_inner.at[n - 1]
        for i in range(2):
            rr = slice(i * HMAX, (i + 1) * HMAX)
            for c in range(2):
                at = slice(c * LANES, (c + 1) * LANES)
                values = [
                    scale[rr] * (part[f, rr, at] + merged[rr, f * width + c * LANES : f * width + (c + 1) * LANES])
                    for f in range(FIELDS)
                ]
                sums[i] = list(contract(values, *sums[i]))
    ones = jnp.ones((HMAX, LANES), F32)
    for k in range(2):
        acc[0:HMAX, :] = sums[0][k]
        acc[HMAX : rows - HMAX, :] = acc_in[k, HMAX : rows - HMAX, :]
        acc[rows - HMAX :, :] = sums[1][k]
        total = lax.dot_general(
            ones, acc[...], (((1,), (1,)), ((), ())), precision=lax.Precision.HIGHEST, preferred_element_type=F32
        )
        out_ref[:, k : k + 1, :] = jnp.broadcast_to(total[0:1][None], (out_ref.shape[0], 1, rows))


def call(kernel, out_shape, scratch, limit, *operands):
    vmem = pl.BlockSpec(memory_space=pltpu.VMEM)
    return pl.pallas_call(
        kernel,
        in_specs=[vmem] * len(operands),
        out_specs=jax.tree.map(lambda _: vmem, out_shape),
        out_shape=out_shape,
        scratch_shapes=scratch,
        compiler_params=pltpu.CompilerParams(vmem_limit_bytes=limit),
        cost_estimate=pl.CostEstimate(flops=4 * 10**9, bytes_accessed=2**20, transcendentals=0),
    )(*operands)


def inner_call(velocity, strain, heights, reach, plane):
    rows, cells = velocity.shape[1:]
    width = 2 * LANES
    shape = jax.ShapeDtypeStruct
    return call(
        inner_kernel,
        [
            shape((FIELDS, rows, cells), BF16),
            shape((WIDE, rows, cells), BF16),
            shape((2 * rows, width), BF16),
            shape((2, rows, LANES), F32),
            shape((cells // width - 2, FIELDS, 2 * HMAX, width), F32),
        ],
        [pltpu.VMEM((width, FIELDS * width), BF16)],
        LARGE_VMEM,
        velocity,
        strain,
        heights,
        reach,
        plane,
    )


def outer_call(fh, fl, lhs, acc, znear, zfar, plane):
    rows = fh.shape[1]
    width = 2 * LANES
    shape = jax.ShapeDtypeStruct
    return call(
        outer_kernel,
        [shape((2, rows, LANES), F32), shape((2, FIELDS, 2 * HMAX, width), F32)],
        [
            pltpu.VMEM((FIELDS, rows, LANES), BF16),
            pltpu.VMEM((WIDE, rows, LANES), BF16),
            pltpu.VMEM((width, FIELDS * width), BF16),
        ],
        LARGE_VMEM,
        fh,
        fl,
        lhs,
        acc,
        znear,
        zfar,
        plane,
    )


def last_call(heights, reach, ynear, yfar, acc, part_inner, part_outer, plane, cells):
    rows = heights.shape[1]
    width = 2 * LANES
    return call(
        last_kernel,
        jax.ShapeDtypeStruct((lax.axis_size("gz"), 2, rows), F32),
        [
            pltpu.VMEM((FIELDS, 2 * HMAX, cells), BF16),
            pltpu.VMEM((WIDE, 2 * HMAX, cells), BF16),
            pltpu.VMEM((FIELDS, 2 * HMAX, LANES), BF16),
            pltpu.VMEM((WIDE, 2 * HMAX, LANES), BF16),
            pltpu.VMEM((4 * HMAX, FIELDS * width), BF16),
            pltpu.VMEM((rows, LANES), F32),
        ],
        LARGE_VMEM,
        heights,
        reach,
        ynear,
        yfar,
        acc,
        part_inner,
        part_outer,
        plane,
    )


def near_pairs(axis):
    return [(i, i ^ 1) for i in range(lax.axis_size(axis))]


def far_pairs(axis, closed):
    n = lax.axis_size(axis)
    pairs = []
    for i in range(1, n if closed else n - 1, 2):
        pairs += [(i, (i + 1) % n), ((i + 1) % n, i)]
    return pairs


def local(velocity, strain, cell_height, stencil_reach):
    rows, cells = velocity.shape[1:]
    heights = cell_height.reshape(1, rows)
    near, far, velocity, strain, plane = pack_span(velocity, strain)
    zfar = lax.ppermute(far, "gz", far_pairs("gz", True))
    znear = lax.ppermute(near, "gz", near_pairs("gz"))
    fh, fl, lhs, acc, part_inner = inner_call(velocity, strain, heights, stencil_reach, plane)
    near, far = pack_wall(velocity, strain, heights, znear, zfar)
    yfar = lax.ppermute(far, "gy", far_pairs("gy", False))
    ynear = lax.ppermute(near, "gy", near_pairs("gy"))
    acc, part_outer = outer_call(fh, fl, lhs, acc, znear, zfar, plane)
    sums = last_call(heights, stencil_reach, ynear, yfar, acc, part_inner, part_outer, plane, cells)
    sums = jnp.sum(lax.all_to_all(sums, "gz", 0, 0), axis=0)
    total = lax.axis_size("gz") * cells
    return sums[0] / total / (sums[1] / total + 1e-06)


def solution(mesh):
    in_specs = (P(None, "gy", "gz"), P(None, "gy", "gz"), P("gy"), P(None, "gy"))
    return jax.shard_map(local, mesh=mesh, in_specs=in_specs, out_specs=P("gy"), check_vma=False)
```

```python
import jax
import jax.numpy as jnp
from jax import lax
from jax.experimental import pallas as pl
from jax.experimental.pallas import tpu as pltpu
from jax.sharding import PartitionSpec as P

NX = 8
HMAX = 8
LANES = 128
FIELDS = 21
WIDE = 15
FIRST_VMEM = 51 * 1024 * 1024
SMALL_VMEM = 24 * 1024 * 1024
LARGE_VMEM = 24 * 1024 * 1024
LEAD_INDEX = (0, 1, 2, 0, 0, 1)
TAIL_INDEX = (0, 1, 2, 1, 2, 2)
TENSOR_WEIGHTS = (1.0, 1.0, 1.0, 2.0, 2.0, 2.0)
F32 = jnp.float32
BF16 = jnp.bfloat16


def strain_rate(s):
    squares = 2.0 * (s[0] * s[0] + s[1] * s[1] + s[2] * s[2])
    squares = squares + 4.0 * (s[3] * s[3] + s[4] * s[4] + s[5] * s[5])
    return jnp.sqrt(squares)


def lane_iota(shape):
    return lax.broadcasted_iota(jnp.int32, shape, len(shape) - 1)


def rot(x, amount):
    amount = amount % LANES
    return pltpu.roll(x, amount, x.ndim - 1) if amount else x


def plane_filter():
    shape = (3 * LANES, 2 * LANES)
    k = lax.broadcasted_iota(jnp.int32, shape, 0)
    m = lane_iota(shape)
    k = jnp.where(k < 5 * LANES // 2, k, k - 3 * LANES)
    turn = (k - m) & (NX - 1)
    along = jnp.where(turn == 0, 0.5, jnp.where((turn == 1) | (turn == NX - 1), 0.25, 0.0))
    step = ((k + LANES) >> 3) - ((m + LANES) >> 3)
    across = jnp.where(step == 0, 0.5, jnp.where((step == 1) | (step == -1), 0.25, 0.0))
    return (along * across).astype(BF16)


def pack_span_kernel(v_ref, s_ref, near_ref, far_ref, v_out, s_out, plane_ref, sems):
    rows, cells = v_ref.shape[1:]
    spans = ((0, LANES), (cells - LANES, LANES), (LANES, cells - 2 * LANES))
    copies = []
    for i, (start, size) in enumerate(spans):
        for j, (ref, out) in enumerate(((v_ref, v_out), (s_ref, s_out))):
            at = pl.ds(start, size)
            copies.append(pltpu.make_async_copy(ref.at[:, :, at], out.at[:, :, at], sems.at[i, j]))
    for copy in copies:
        copy.start()
    once = plane_filter()
    plane_ref[: 3 * LANES] = once
    plane_ref[3 * LANES :] = once
    for copy in copies[:4]:
        copy.wait()
    lane = lane_iota((rows, LANES))
    left = jnp.zeros((rows, LANES), F32)
    right = jnp.zeros((rows, LANES), F32)
    for f in range(9):
        ref, at = (v_out, f) if f < 3 else (s_out, f - 3)
        here = (lane >= NX * f) & (lane < NX * (f + 1))
        left = jnp.where(here, rot(ref[at, :, :LANES].astype(F32), NX * f), left)
        right = jnp.where(here, rot(ref[at, :, cells - LANES :].astype(F32), NX * f + NX), right)
    odd = lax.axis_index("gz") % 2 == 1
    near_ref[...] = jnp.where(odd, left, right)
    far_ref[...] = jnp.where(odd, right, left)
    for copy in copies[4:]:
        copy.wait()


def pack_span(velocity, strain):
    rows = velocity.shape[1]
    hbm = pl.BlockSpec(memory_space=pltpu.HBM)
    vmem = pl.BlockSpec(memory_space=pltpu.VMEM)
    return pl.pallas_call(
        pack_span_kernel,
        in_specs=[hbm] * 2,
        out_specs=[vmem] * 5,
        out_shape=[jax.ShapeDtypeStruct((rows, LANES), F32)] * 2
        + [jax.ShapeDtypeStruct(x.shape, x.dtype) for x in (velocity, strain)]
        + [jax.ShapeDtypeStruct((6 * LANES, 2 * LANES), BF16)],
        scratch_shapes=[pltpu.SemaphoreType.DMA((3, 2))],
        compiler_params=pltpu.CompilerParams(vmem_limit_bytes=FIRST_VMEM),
    )(velocity, strain)


def pack_wall_kernel(v_ref, s_ref, h_ref, znear, zfar, near_ref, far_ref):
    rows, cells = v_ref.shape[1:]
    gz_odd = lax.axis_index("gz") % 2 == 1
    gy_odd = lax.axis_index("gy") % 2 == 1
    tail = 9 * cells
    lane = lane_iota((HMAX, LANES))
    row = lax.broadcasted_iota(jnp.int32, (HMAX, LANES), 0)
    stamp = (row == 0) & (lane >= 9 * NX) & (lane < 10 * NX)
    heights = jnp.broadcast_to(jnp.pad(h_ref[...], ((0, 0), (0, LANES - rows))), (HMAX, LANES))

    def emit(ref, high):
        r0 = rows - HMAX if high else 0
        for f in range(3):
            ref[:, f * cells : (f + 1) * cells] = v_ref[f, r0 : r0 + HMAX, :]
        for f in range(6):
            part = (s_ref[f, rows - 2 * HMAX :, :] if high else s_ref[f, : 2 * HMAX, :]).astype(F32)
            ref[:, (3 + f) * cells : (4 + f) * cells] = part[HMAX:] if high else part[:HMAX]
        zn = znear[r0 : r0 + HMAX, :]
        zf = zfar[r0 : r0 + HMAX, :]
        zl = jnp.where(gz_odd, zn, zf)
        zr = jnp.where(gz_odd, zf, zn)
        ref[:, tail : tail + LANES] = jnp.where(stamp, rot(heights, 9 * NX - r0), zl)
        ref[:, tail + LANES : tail + 2 * LANES] = zr

    @pl.when(gy_odd)
    def _():
        emit(near_ref, False)
        emit(far_ref, True)

    @pl.when(jnp.logical_not(gy_odd))
    def _():
        emit(near_ref, True)
        emit(far_ref, False)


def pack_wall(velocity, strain, heights, znear, zfar):
    rows, cells = velocity.shape[1:]
    width = 9 * cells + 2 * LANES
    vmem = pl.BlockSpec(memory_space=pltpu.VMEM)
    return pl.pallas_call(
        pack_wall_kernel,
        in_specs=[vmem] * 5,
        out_specs=[vmem] * 2,
        out_shape=[jax.ShapeDtypeStruct((HMAX, width), F32)] * 2,
        compiler_params=pltpu.CompilerParams(vmem_limit_bytes=SMALL_VMEM),
    )(velocity, strain, heights, znear, zfar)


def split2(x):
    hi = x.astype(BF16)
    return hi, (x - hi.astype(F32)).astype(BF16)


def store_fields(u, s, put_high, put_low):
    tensor = [x.astype(F32) for x in s]
    rate = strain_rate(tensor)
    wide = u + [u[a] * u[b] for a, b in zip(LEAD_INDEX, TAIL_INDEX)] + [rate * x for x in tensor]
    for f, value in enumerate(wide):
        hi, lo = split2(value)
        put_high(f, hi)
        put_low(f, lo)
    for f, value in enumerate(s):
        put_high(WIDE + f, value.astype(BF16))


def smooth_block(n, tiles, fh, fl, eh, el, plane_ref):
    rows = fh.shape[1]
    at = slice(2 * n * LANES, (2 * n + 2) * LANES)

    def edge(ref, outer, fields):
        before = ref[fields, :, (2 * n - 1) * LANES : 2 * n * LANES] if n else outer[fields]
        after = ref[fields, :, (2 * n + 2) * LANES : (2 * n + 3) * LANES] if 2 * n + 2 < tiles else outer[fields]
        return jnp.where(lane_iota(before.shape) < LANES // 2, after, before)

    wide, narrow = slice(0, WIDE), slice(WIDE, FIELDS)
    lhs = jnp.concatenate([fh[wide, :, at], edge(fh, eh, wide), fl[wide, :, at], edge(fl, el, wide)], axis=-1)
    first = jnp.dot(lhs.reshape(WIDE * rows, 6 * LANES), plane_ref[...], preferred_element_type=F32)
    lhs = jnp.concatenate([fh[narrow, :, at], edge(fh, eh, narrow)], axis=-1)
    second = jnp.dot(
        lhs.reshape((FIELDS - WIDE) * rows, 3 * LANES), plane_ref[: 3 * LANES], preferred_element_type=F32
    )
    return [first[f * rows : (f + 1) * rows] for f in range(WIDE)] + [
        second[f * rows : (f + 1) * rows] for f in range(FIELDS - WIDE)
    ]


def contract(g, inv, num, den):
    u, p, m, s = g[0:3], g[3:9], g[9:15], g[15:21]
    rate = 4.0 * inv * strain_rate(s)
    scaled = [inv * x for x in u]
    for k in range(6):
        leonard = p[k] - scaled[LEAD_INDEX[k]] * u[TAIL_INDEX[k]]
        model = m[k] - rate * s[k]
        weighted = TENSOR_WEIGHTS[k] * model
        num = num + weighted * leonard
        den = den + weighted * model
    return num, den


def to_column(row_vector, size):
    shape = (size, LANES)
    eye = lax.broadcasted_iota(jnp.int32, shape, 0) == lane_iota(shape)
    return jnp.sum(jnp.where(eye, jnp.broadcast_to(row_vector, shape), 0.0), axis=1, keepdims=True)


def pad_lanes(x):
    return jnp.pad(x, ((0, 0), (0, LANES - x.shape[1])))


def wall_inside(reach_ref, place, rows):
    gy = lax.axis_index("gy")
    reach = pad_lanes(reach_ref[...].astype(F32))
    down = to_column(reach[0:1], rows).astype(jnp.int32)
    up = to_column(reach[1:2], rows).astype(jnp.int32)
    row = lax.broadcasted_iota(jnp.int32, place.shape, 0)
    lowest = jnp.maximum(row - down, -gy * rows)
    highest = jnp.minimum(row + up, (lax.axis_size("gy") - gy) * rows - 1)
    return (place >= lowest) & (place <= highest)


def wall_block(g, mask, height, inv, stack, acc_ref, part_ref):
    rows = g[0].shape[0]
    width = 2 * LANES
    for f in range(FIELDS):
        hi, lo = split2(g[f] * height)
        stack[0:rows, f * width : (f + 1) * width] = hi
        stack[rows:, f * width : (f + 1) * width] = lo
    merged = jnp.dot(mask, stack[...], preferred_element_type=F32)
    for f in range(FIELDS):
        part_ref[f, 0:HMAX, :] = merged[0:HMAX, f * width : (f + 1) * width]
        part_ref[f, HMAX:, :] = merged[rows - HMAX :, f * width : (f + 1) * width]
    for r in range(HMAX, rows - HMAX, HMAX):
        num = acc_ref[0, r : r + HMAX, :]
        den = acc_ref[1, r : r + HMAX, :]
        scale = jnp.broadcast_to(inv[r : r + HMAX], (HMAX, LANES))
        for c in range(2):
            parts = [
                merged[r : r + HMAX, f * width + c * LANES : f * width + (c + 1) * LANES] for f in range(FIELDS)
            ]
            num, den = contract(parts, scale, num, den)
        acc_ref[0, r : r + HMAX, :] = num
        acc_ref[1, r : r + HMAX, :] = den


def inner_kernel(v_ref, s_ref, plane_ref, fh, fl, smooth):
    rows, cells = v_ref.shape[1:]
    tiles = cells // LANES
    for t in range(tiles):
        at = slice(t * LANES, (t + 1) * LANES)
        for r in range(0, rows, 16):
            rr = slice(r, r + 16)

            def put_high(f, x):
                fh[f, rr, at] = x

            def put_low(f, x):
                fl[f, rr, at] = x

            store_fields(
                [v_ref[f, rr, at] for f in range(3)], [s_ref[f, rr, at] for f in range(6)], put_high, put_low
            )
    for n in range(1, tiles // 2 - 1):
        g = smooth_block(n, tiles, fh, fl, None, None, plane_ref)
        for f in range(FIELDS):
            smooth[n - 1, f] = g[f]


def outer_kernel(h_ref, reach_ref, fh, fl, smooth, znear, zfar, plane_ref, acc_ref, part_ref, eh, el, stack):
    rows, cells = fh.shape[1:]
    tiles = cells // LANES
    gz_odd = lax.axis_index("gz") % 2 == 1
    column = lane_iota((rows, 2 * LANES))
    place = jnp.where(column < rows, column, column - rows)
    inside = wall_inside(reach_ref, place, rows)
    mask = jnp.where(inside, 1.0, 0.0)[:, : 2 * rows].astype(BF16)
    heights = pad_lanes(h_ref[...])
    height = to_column(heights, rows)
    first = (column < rows) & inside
    total = jnp.sum(jnp.where(first, jnp.pad(heights, ((0, 0), (0, LANES))), 0.0), axis=1, keepdims=True)
    inv = 1.0 / total
    acc_ref[...] = jnp.zeros_like(acc_ref)
    edge_fields(jnp.where(gz_odd, znear[...], zfar[...]), jnp.where(gz_odd, zfar[...], znear[...]), eh, el)
    for n in range(tiles // 2):
        if 0 < n < tiles // 2 - 1:
            g = [smooth[n - 1, f] for f in range(FIELDS)]
        else:
            g = smooth_block(n, tiles, fh, fl, eh, el, plane_ref)
        wall_block(g, mask, height, inv, stack.at[n], acc_ref, part_ref.at[n])


def edge_fields(zl, zr, eh, el):
    rows = zl.shape[0]
    lane = lane_iota((16, LANES))
    for r in range(0, rows, 16):
        rr = slice(r, r + 16)
        raw = [
            jnp.where(
                lane < NX, rot(zr[rr], -NX * f), jnp.where(lane >= LANES - NX, rot(zl[rr], -NX * f - NX), 0.0)
            )
            for f in range(9)
        ]

        def put_high(f, x):
            eh[f, rr, :] = x

        def put_low(f, x):
            el[f, rr, :] = x

        store_fields(raw[:3], raw[3:], put_high, put_low)


def last_kernel(h_ref, reach_ref, ynear, yfar, acc_in, part, plane_ref, out_ref, fh, fl, eh, el, stack, acc):
    rows = h_ref.shape[1]
    cells = (ynear.shape[1] - 2 * LANES) // 9
    tiles = cells // LANES
    width = 2 * LANES
    gy_odd = lax.axis_index("gy") % 2 == 1
    tail = 9 * cells
    both_rows = 2 * HMAX

    def halo(at):
        near, far = ynear[:, at], yfar[:, at]
        return jnp.concatenate([jnp.where(gy_odd, near, far), jnp.where(gy_odd, far, near)], axis=0)

    zl = halo(slice(tail, tail + LANES))
    zr = halo(slice(tail + LANES, tail + 2 * LANES))
    below = rot(zl[:HMAX], -9 * NX)[0:1]
    above = rot(zl[HMAX:], -9 * NX)[0:1]
    height = jnp.concatenate([to_column(below, HMAX), to_column(above, HMAX)], axis=0)
    column = lane_iota((rows, LANES))
    place = jnp.where(column < rows, column, jnp.where(column < rows + HMAX, column - rows - HMAX, column - HMAX))
    hrow = lane_iota((1, LANES))
    heights = jnp.where(
        hrow < rows, pad_lanes(h_ref[...]), jnp.where(hrow < rows + HMAX, rot(below, rows), rot(above, rows + HMAX))
    )
    inside = wall_inside(reach_ref, place, rows) & (column < rows + both_rows)
    inv = 1.0 / jnp.sum(jnp.where(inside, jnp.broadcast_to(heights, (rows, LANES)), 0.0), axis=1, keepdims=True)
    scale = [jnp.broadcast_to(inv[r : r + HMAX], (HMAX, LANES)) for r in (0, rows - HMAX)]
    mask = jnp.where(inside, 1.0, 0.0)
    mask = rot(jnp.concatenate([mask[:HMAX], mask[rows - HMAX :]], axis=0), -rows)
    lane = lane_iota((both_rows, LANES))
    mask = jnp.where(lane < both_rows, mask, rot(mask, both_rows))[:, : 2 * both_rows].astype(BF16)

    edge_fields(zl, zr, eh, el)
    for t in range(tiles):
        at = slice(t * LANES, (t + 1) * LANES)

        def put_high(f, x):
            fh[f, :, at] = x

        def put_low(f, x):
            fl[f, :, at] = x

        raw = [halo(slice(f * cells + t * LANES, f * cells + (t + 1) * LANES)) for f in range(9)]
        store_fields(raw[:3], raw[3:], put_high, put_low)

    zero = jnp.zeros((HMAX, LANES), F32)
    sums = [[zero, zero], [zero, zero]]
    for n in range(tiles // 2):
        g = smooth_block(n, tiles, fh, fl, eh, el, plane_ref)
        for f in range(FIELDS):
            hi, lo = split2(g[f] * height)
            stack[0:both_rows, f * width : (f + 1) * width] = hi
            stack[both_rows:, f * width : (f + 1) * width] = lo
        merged = jnp.dot(mask, stack[...], preferred_element_type=F32)
        for i in range(2):
            rr = slice(i * HMAX, (i + 1) * HMAX)
            for c in range(2):
                at = slice(c * LANES, (c + 1) * LANES)
                values = [
                    part[n, f, rr, at] + merged[rr, f * width + c * LANES : f * width + (c + 1) * LANES]
                    for f in range(FIELDS)
                ]
                sums[i] = list(contract(values, scale[i], *sums[i]))
    ones = jnp.ones((HMAX, LANES), F32)
    for k in range(2):
        acc[0:HMAX, :] = sums[0][k]
        acc[HMAX : rows - HMAX, :] = acc_in[k, HMAX : rows - HMAX, :]
        acc[rows - HMAX :, :] = sums[1][k]
        total = lax.dot_general(
            ones, acc[...] * (inv * inv), (((1,), (1,)), ((), ())), precision=lax.Precision.HIGHEST, preferred_element_type=F32
        )
        out_ref[:, k : k + 1, :] = jnp.broadcast_to(total[0:1][None], (out_ref.shape[0], 1, rows))


def call(kernel, out_shape, scratch, limit, *operands):
    vmem = pl.BlockSpec(memory_space=pltpu.VMEM)
    return pl.pallas_call(
        kernel,
        in_specs=[vmem] * len(operands),
        out_specs=jax.tree.map(lambda _: vmem, out_shape),
        out_shape=out_shape,
        scratch_shapes=scratch,
        compiler_params=pltpu.CompilerParams(vmem_limit_bytes=limit),
        cost_estimate=pl.CostEstimate(flops=4 * 10**9, bytes_accessed=2**20, transcendentals=0),
    )(*operands)


def inner_call(velocity, strain, plane):
    rows, cells = velocity.shape[1:]
    width = 2 * LANES
    shape = jax.ShapeDtypeStruct
    return call(
        inner_kernel,
        [
            shape((FIELDS, rows, cells), BF16),
            shape((WIDE, rows, cells), BF16),
            shape((cells // width - 2, FIELDS, rows, width), F32),
        ],
        [],
        LARGE_VMEM,
        velocity,
        strain,
        plane,
    )


def outer_call(heights, reach, fh, fl, smooth, znear, zfar, plane):
    rows, cells = fh.shape[1:]
    width = 2 * LANES
    shape = jax.ShapeDtypeStruct
    return call(
        outer_kernel,
        [shape((2, rows, LANES), F32), shape((cells // width, FIELDS, 2 * HMAX, width), F32)],
        [
            pltpu.VMEM((FIELDS, rows, LANES), BF16),
            pltpu.VMEM((WIDE, rows, LANES), BF16),
            pltpu.VMEM((cells // width, 2 * rows, FIELDS * width), BF16),
        ],
        LARGE_VMEM,
        heights,
        reach,
        fh,
        fl,
        smooth,
        znear,
        zfar,
        plane,
    )


def last_call(heights, reach, ynear, yfar, acc, part, plane, cells):
    rows = heights.shape[1]
    width = 2 * LANES
    return call(
        last_kernel,
        jax.ShapeDtypeStruct((lax.axis_size("gz"), 2, rows), F32),
        [
            pltpu.VMEM((FIELDS, 2 * HMAX, cells), BF16),
            pltpu.VMEM((WIDE, 2 * HMAX, cells), BF16),
            pltpu.VMEM((FIELDS, 2 * HMAX, LANES), BF16),
            pltpu.VMEM((WIDE, 2 * HMAX, LANES), BF16),
            pltpu.VMEM((4 * HMAX, FIELDS * width), BF16),
            pltpu.VMEM((rows, LANES), F32),
        ],
        LARGE_VMEM,
        heights,
        reach,
        ynear,
        yfar,
        acc,
        part,
        plane,
    )


def near_pairs(axis):
    return [(i, i ^ 1) for i in range(lax.axis_size(axis))]


def far_pairs(axis, closed):
    n = lax.axis_size(axis)
    pairs = []
    for i in range(1, n if closed else n - 1, 2):
        pairs += [(i, (i + 1) % n), ((i + 1) % n, i)]
    return pairs


def local(velocity, strain, cell_height, stencil_reach):
    rows, cells = velocity.shape[1:]
    heights = cell_height.reshape(1, rows)
    near, far, velocity, strain, plane = pack_span(velocity, strain)
    zfar = lax.ppermute(far, "gz", far_pairs("gz", True))
    znear = lax.ppermute(near, "gz", near_pairs("gz"))
    fh, fl, smooth = inner_call(velocity, strain, plane)
    near, far = pack_wall(velocity, strain, heights, znear, zfar)
    yfar = lax.ppermute(far, "gy", far_pairs("gy", False))
    ynear = lax.ppermute(near, "gy", near_pairs("gy"))
    acc, part = outer_call(heights, stencil_reach, fh, fl, smooth, znear, zfar, plane)
    sums = last_call(heights, stencil_reach, ynear, yfar, acc, part, plane, cells)
    sums = jnp.sum(lax.all_to_all(sums, "gz", 0, 0), axis=0)
    total = lax.axis_size("gz") * cells
    return sums[0] / total / (sums[1] / total + 1e-06)


def solution(mesh):
    in_specs = (P(None, "gy", "gz"), P(None, "gy", "gz"), P("gy"), P(None, "gy"))
    return jax.shard_map(local, mesh=mesh, in_specs=in_specs, out_specs=P("gy"), check_vma=False)
```

```python
import jax
import jax.numpy as jnp
from jax import lax
from jax.experimental import pallas as pl
from jax.experimental.pallas import tpu as pltpu
from jax.sharding import PartitionSpec as P

NX = 8
HMAX = 8
LANES = 128
FIELDS = 21
WIDE = 15
FIRST_VMEM = 51 * 1024 * 1024
SMALL_VMEM = 24 * 1024 * 1024
LARGE_VMEM = 24 * 1024 * 1024
LEAD_INDEX = (0, 1, 2, 0, 0, 1)
TAIL_INDEX = (0, 1, 2, 1, 2, 2)
TENSOR_WEIGHTS = (1.0, 1.0, 1.0, 2.0, 2.0, 2.0)
F32 = jnp.float32
BF16 = jnp.bfloat16


def strain_rate(s):
    squares = 2.0 * (s[0] * s[0] + s[1] * s[1] + s[2] * s[2])
    squares = squares + 4.0 * (s[3] * s[3] + s[4] * s[4] + s[5] * s[5])
    return jnp.sqrt(squares)


def lane_iota(shape):
    return lax.broadcasted_iota(jnp.int32, shape, len(shape) - 1)


def rot(x, amount):
    amount = amount % LANES
    return pltpu.roll(x, amount, x.ndim - 1) if amount else x


def cell_weights(source, target):
    turn = (source - target) & (NX - 1)
    along = jnp.where(turn == 0, 0.5, jnp.where((turn == 1) | (turn == NX - 1), 0.25, 0.0))
    step = ((source + LANES) >> 3) - ((target + LANES) >> 3)
    across = jnp.where(step == 0, 0.5, jnp.where((step == 1) | (step == -1), 0.25, 0.0))
    return along * across


def pair_filter():
    shape = (3 * LANES, 2 * LANES)
    k = lax.broadcasted_iota(jnp.int32, shape, 0)
    return cell_weights(jnp.where(k < 5 * LANES // 2, k, k - 3 * LANES), lane_iota(shape)).astype(BF16)


def ends_filter():
    shape = (4 * LANES, 2 * LANES)
    k = lax.broadcasted_iota(jnp.int32, shape, 0)
    m = lane_iota(shape)
    place = k & (LANES - 1)
    outer = k >= 2 * LANES
    source = jnp.where(outer, jnp.where(place < LANES // 2, place + LANES, place - LANES), place)
    same = ((k >> 7) & 1) == (m >> 7)
    return jnp.where(same, cell_weights(source, m & (LANES - 1)), 0.0).astype(BF16)


def first_kernel(v_ref, s_ref, near_ref, far_ref, wall_near, wall_far, v_out, s_out, pair_ref, ends_ref, sems):
    rows, cells = v_ref.shape[1:]
    spans = ((0, LANES), (cells - LANES, LANES), (LANES, cells - 2 * LANES))
    copies = []
    for i, (start, size) in enumerate(spans):
        for j, (ref, out) in enumerate(((v_ref, v_out), (s_ref, s_out))):
            at = pl.ds(start, size)
            copies.append(pltpu.make_async_copy(ref.at[:, :, at], out.at[:, :, at], sems.at[i, j]))
    for copy in copies:
        copy.start()
    pair_ref[...] = pair_filter()
    ends_ref[...] = ends_filter()
    for copy in copies[:4]:
        copy.wait()
    lane = lane_iota((rows, LANES))
    left = jnp.zeros((rows, LANES), F32)
    right = jnp.zeros((rows, LANES), F32)
    for f in range(9):
        ref, at = (v_out, f) if f < 3 else (s_out, f - 3)
        here = (lane >= NX * f) & (lane < NX * (f + 1))
        left = jnp.where(here, rot(ref[at, :, :LANES].astype(F32), NX * f), left)
        right = jnp.where(here, rot(ref[at, :, cells - LANES :].astype(F32), NX * f + NX), right)
    odd = lax.axis_index("gz") % 2 == 1
    near_ref[...] = jnp.where(odd, left, right)
    far_ref[...] = jnp.where(odd, right, left)
    for copy in copies[4:]:
        copy.wait()
    gy_odd = lax.axis_index("gy") % 2 == 1
    for f in range(9):
        at = slice(f * cells, (f + 1) * cells)
        if f < 3:
            low, high = v_out[f, :HMAX, :], v_out[f, rows - HMAX :, :]
        else:
            low = s_out[f - 3, : 2 * HMAX, :].astype(F32)[:HMAX]
            high = s_out[f - 3, rows - 2 * HMAX :, :].astype(F32)[HMAX:]
        wall_near[:, at] = jnp.where(gy_odd, low, high)
        wall_far[:, at] = jnp.where(gy_odd, high, low)


def first_call(velocity, strain):
    rows, cells = velocity.shape[1:]
    hbm = pl.BlockSpec(memory_space=pltpu.HBM)
    vmem = pl.BlockSpec(memory_space=pltpu.VMEM)
    shape = jax.ShapeDtypeStruct
    return pl.pallas_call(
        first_kernel,
        in_specs=[hbm] * 2,
        out_specs=[vmem] * 8,
        out_shape=[shape((rows, LANES), F32)] * 2
        + [shape((HMAX, 9 * cells), F32)] * 2
        + [shape(x.shape, x.dtype) for x in (velocity, strain)]
        + [shape((3 * LANES, 2 * LANES), BF16), shape((4 * LANES, 2 * LANES), BF16)],
        scratch_shapes=[pltpu.SemaphoreType.DMA((3, 2))],
        compiler_params=pltpu.CompilerParams(vmem_limit_bytes=FIRST_VMEM),
    )(velocity, strain)


def corner_kernel(h_ref, znear, zfar, near_ref, far_ref):
    rows = znear.shape[0]
    gz_odd = lax.axis_index("gz") % 2 == 1
    gy_odd = lax.axis_index("gy") % 2 == 1
    lane = lane_iota((HMAX, LANES))
    row = lax.broadcasted_iota(jnp.int32, (HMAX, LANES), 0)
    stamp = (row == 0) & (lane >= 9 * NX) & (lane < 10 * NX)
    heights = jnp.broadcast_to(jnp.pad(h_ref[...], ((0, 0), (0, LANES - rows))), (HMAX, LANES))
    sides = []
    for r0 in (0, rows - HMAX):
        zn = znear[r0 : r0 + HMAX, :]
        zf = zfar[r0 : r0 + HMAX, :]
        zl = jnp.where(stamp, rot(heights, 9 * NX - r0), jnp.where(gz_odd, zn, zf))
        sides.append((zl, jnp.where(gz_odd, zf, zn)))
    (low_left, low_right), (high_left, high_right) = sides
    near_ref[:, :LANES] = jnp.where(gy_odd, low_left, high_left)
    near_ref[:, LANES:] = jnp.where(gy_odd, low_right, high_right)
    far_ref[:, :LANES] = jnp.where(gy_odd, high_left, low_left)
    far_ref[:, LANES:] = jnp.where(gy_odd, high_right, low_right)


def corner_call(heights, znear, zfar):
    vmem = pl.BlockSpec(memory_space=pltpu.VMEM)
    return pl.pallas_call(
        corner_kernel,
        in_specs=[vmem] * 3,
        out_specs=[vmem] * 2,
        out_shape=[jax.ShapeDtypeStruct((HMAX, 2 * LANES), F32)] * 2,
        compiler_params=pltpu.CompilerParams(vmem_limit_bytes=SMALL_VMEM),
    )(heights, znear, zfar)


def split2(x):
    hi = x.astype(BF16)
    return hi, (x - hi.astype(F32)).astype(BF16)


def store_fields(u, s, put_high, put_low):
    tensor = [x.astype(F32) for x in s]
    rate = strain_rate(tensor)
    wide = u + [u[a] * u[b] for a, b in zip(LEAD_INDEX, TAIL_INDEX)] + [rate * x for x in tensor]
    for f, value in enumerate(wide):
        hi, lo = split2(value)
        put_high(f, hi)
        put_low(f, lo)
    for f, value in enumerate(s):
        put_high(WIDE + f, value.astype(BF16))


def smooth(rows, operand, matrix_ref):
    wide, narrow = slice(0, WIDE), slice(WIDE, FIELDS)
    lhs = jnp.concatenate([operand(True, wide), operand(False, wide)], axis=-1).reshape(WIDE * rows, -1)
    matrix = matrix_ref[...]
    first = jnp.dot(lhs, jnp.concatenate([matrix, matrix], axis=0), preferred_element_type=F32)
    lhs = operand(True, narrow).reshape((FIELDS - WIDE) * rows, -1)
    second = jnp.dot(lhs, matrix, preferred_element_type=F32)
    return [first[f * rows : (f + 1) * rows] for f in range(WIDE)] + [
        second[f * rows : (f + 1) * rows] for f in range(FIELDS - WIDE)
    ]


def pick(after, before):
    return jnp.where(lane_iota(after.shape) < LANES // 2, after, before)


def smooth_pair(n, fh, fl, pair_ref):
    def operand(high, fields):
        ref = fh if high else fl
        tile = [ref[fields, :, (2 * n + i) * LANES : (2 * n + i + 1) * LANES] for i in range(4)]
        return jnp.concatenate([tile[1], tile[2], pick(tile[3], tile[0])], axis=-1)

    return smooth(fh.shape[1], operand, pair_ref)


def smooth_ends(fh, fl, eh, el, ends_ref):
    cells = fh.shape[2]

    def operand(high, fields):
        ref, outer = (fh, eh) if high else (fl, el)
        head, second = ref[fields, :, :LANES], ref[fields, :, LANES : 2 * LANES]
        ahead, last = ref[fields, :, cells - 2 * LANES : cells - LANES], ref[fields, :, cells - LANES :]
        edge = outer[fields]
        return jnp.concatenate([head, last, pick(second, edge), pick(edge, ahead)], axis=-1)

    return smooth(fh.shape[1], operand, ends_ref)


def contract(g, inv, num, den):
    u, p, m, s = g[0:3], g[3:9], g[9:15], g[15:21]
    rate = 4.0 * inv * strain_rate(s)
    scaled = [inv * x for x in u]
    for k in range(6):
        leonard = p[k] - scaled[LEAD_INDEX[k]] * u[TAIL_INDEX[k]]
        model = m[k] - rate * s[k]
        weighted = TENSOR_WEIGHTS[k] * model
        num = num + weighted * leonard
        den = den + weighted * model
    return num, den


def to_column(row_vector, size):
    shape = (size, LANES)
    eye = lax.broadcasted_iota(jnp.int32, shape, 0) == lane_iota(shape)
    return jnp.sum(jnp.where(eye, jnp.broadcast_to(row_vector, shape), 0.0), axis=1, keepdims=True)


def pad_lanes(x):
    return jnp.pad(x, ((0, 0), (0, LANES - x.shape[1])))


def wall_inside(reach_ref, place, rows):
    gy = lax.axis_index("gy")
    reach = pad_lanes(reach_ref[...].astype(F32))
    down = to_column(reach[0:1], rows).astype(jnp.int32)
    up = to_column(reach[1:2], rows).astype(jnp.int32)
    row = lax.broadcasted_iota(jnp.int32, place.shape, 0)
    lowest = jnp.maximum(row - down, -gy * rows)
    highest = jnp.minimum(row + up, (lax.axis_size("gy") - gy) * rows - 1)
    return (place >= lowest) & (place <= highest)


def wall_block(g, mask, height, inv, stack, acc_ref, part_ref):
    rows = g[0].shape[0]
    width = 2 * LANES
    for f in range(FIELDS):
        hi, lo = split2(g[f] * height)
        stack[0:rows, f * width : (f + 1) * width] = hi
        stack[rows:, f * width : (f + 1) * width] = lo
    merged = jnp.dot(mask, stack[...], preferred_element_type=F32)
    for f in range(FIELDS):
        part_ref[f, 0:HMAX, :] = merged[0:HMAX, f * width : (f + 1) * width]
        part_ref[f, HMAX:, :] = merged[rows - HMAX :, f * width : (f + 1) * width]
    for r in range(HMAX, rows - HMAX, HMAX):
        num = acc_ref[0, r : r + HMAX, :]
        den = acc_ref[1, r : r + HMAX, :]
        scale = jnp.broadcast_to(inv[r : r + HMAX], (HMAX, LANES))
        for c in range(2):
            parts = [
                merged[r : r + HMAX, f * width + c * LANES : f * width + (c + 1) * LANES] for f in range(FIELDS)
            ]
            num, den = contract(parts, scale, num, den)
        acc_ref[0, r : r + HMAX, :] = num
        acc_ref[1, r : r + HMAX, :] = den


def inner_kernel(v_ref, s_ref, pair_ref, fh, fl, inner):
    rows, cells = v_ref.shape[1:]
    for t in range(cells // LANES):
        at = slice(t * LANES, (t + 1) * LANES)
        for r in range(0, rows, 16):
            rr = slice(r, r + 16)

            def put_high(f, x):
                fh[f, rr, at] = x

            def put_low(f, x):
                fl[f, rr, at] = x

            store_fields(
                [v_ref[f, rr, at] for f in range(3)], [s_ref[f, rr, at] for f in range(6)], put_high, put_low
            )
    for n in range(inner.shape[0]):
        g = smooth_pair(n, fh, fl, pair_ref)
        for f in range(FIELDS):
            inner[n, f] = g[f]


def outer_kernel(
    h_ref, reach_ref, fh, fl, inner, znear, zfar, ynear, yfar, pair_ref, ends_ref,
    acc_ref, part_ref, hh, hl, halo_inner, eh, el, stack,
):
    rows, cells = fh.shape[1:]
    blocks = inner.shape[0]
    gz_odd = lax.axis_index("gz") % 2 == 1
    gy_odd = lax.axis_index("gy") % 2 == 1
    column = lane_iota((rows, 2 * LANES))
    place = jnp.where(column < rows, column, column - rows)
    inside = wall_inside(reach_ref, place, rows)
    mask = jnp.where(inside, 1.0, 0.0)[:, : 2 * rows].astype(BF16)
    heights = pad_lanes(h_ref[...])
    height = to_column(heights, rows)
    first = (column < rows) & inside
    total = jnp.sum(jnp.where(first, jnp.pad(heights, ((0, 0), (0, LANES))), 0.0), axis=1, keepdims=True)
    inv = 1.0 / total
    acc_ref[...] = jnp.zeros_like(acc_ref)
    edge_fields(jnp.where(gz_odd, znear[...], zfar[...]), jnp.where(gz_odd, zfar[...], znear[...]), eh, el)
    for n in range(blocks + 1):
        if n < blocks:
            g = [inner[n, f] for f in range(FIELDS)]
        else:
            g = smooth_ends(fh, fl, eh, el, ends_ref)
        wall_block(g, mask, height, inv, stack.at[n], acc_ref, part_ref.at[n])
    for t in range(cells // LANES):
        at = slice(t * LANES, (t + 1) * LANES)

        def put_high(f, x):
            hh[f, :, at] = x

        def put_low(f, x):
            hl[f, :, at] = x

        raw = []
        for f in range(9):
            span = slice(f * cells + t * LANES, f * cells + (t + 1) * LANES)
            near, far = ynear[:, span], yfar[:, span]
            raw.append(jnp.concatenate([jnp.where(gy_odd, near, far), jnp.where(gy_odd, far, near)], axis=0))
        store_fields(raw[:3], raw[3:], put_high, put_low)
    for n in range(blocks):
        g = smooth_pair(n, hh, hl, pair_ref)
        for f in range(FIELDS):
            halo_inner[n, f] = g[f]


def edge_fields(zl, zr, eh, el):
    rows = zl.shape[0]
    lane = lane_iota((16, LANES))
    for r in range(0, rows, 16):
        rr = slice(r, r + 16)
        raw = [
            jnp.where(
                lane < NX, rot(zr[rr], -NX * f), jnp.where(lane >= LANES - NX, rot(zl[rr], -NX * f - NX), 0.0)
            )
            for f in range(9)
        ]

        def put_high(f, x):
            eh[f, rr, :] = x

        def put_low(f, x):
            el[f, rr, :] = x

        store_fields(raw[:3], raw[3:], put_high, put_low)


def last_kernel(h_ref, reach_ref, near_ref, far_ref, acc_in, part, hh, hl, halo_inner, ends_ref, out_ref, eh, el, stack, acc):
    rows = h_ref.shape[1]
    width = 2 * LANES
    gy_odd = lax.axis_index("gy") % 2 == 1
    both_rows = 2 * HMAX

    def halo(at):
        near, far = near_ref[:, at], far_ref[:, at]
        return jnp.concatenate([jnp.where(gy_odd, near, far), jnp.where(gy_odd, far, near)], axis=0)

    zl = halo(slice(0, LANES))
    zr = halo(slice(LANES, 2 * LANES))
    below = rot(zl[:HMAX], -9 * NX)[0:1]
    above = rot(zl[HMAX:], -9 * NX)[0:1]
    height = jnp.concatenate([to_column(below, HMAX), to_column(above, HMAX)], axis=0)
    column = lane_iota((rows, LANES))
    place = jnp.where(column < rows, column, jnp.where(column < rows + HMAX, column - rows - HMAX, column - HMAX))
    hrow = lane_iota((1, LANES))
    heights = jnp.where(
        hrow < rows, pad_lanes(h_ref[...]), jnp.where(hrow < rows + HMAX, rot(below, rows), rot(above, rows + HMAX))
    )
    inside = wall_inside(reach_ref, place, rows) & (column < rows + both_rows)
    inv = 1.0 / jnp.sum(jnp.where(inside, jnp.broadcast_to(heights, (rows, LANES)), 0.0), axis=1, keepdims=True)
    scale = [jnp.broadcast_to(inv[r : r + HMAX], (HMAX, LANES)) for r in (0, rows - HMAX)]
    mask = jnp.where(inside, 1.0, 0.0)
    mask = rot(jnp.concatenate([mask[:HMAX], mask[rows - HMAX :]], axis=0), -rows)
    lane = lane_iota((both_rows, LANES))
    mask = jnp.where(lane < both_rows, mask, rot(mask, both_rows))[:, : 2 * both_rows].astype(BF16)

    edge_fields(zl, zr, eh, el)
    zero = jnp.zeros((HMAX, LANES), F32)
    sums = [[zero, zero], [zero, zero]]
    blocks = halo_inner.shape[0]
    for n in range(blocks + 1):
        if n < blocks:
            g = [halo_inner[n, f] for f in range(FIELDS)]
        else:
            g = smooth_ends(hh, hl, eh, el, ends_ref)
        for f in range(FIELDS):
            hi, lo = split2(g[f] * height)
            stack[n, 0:both_rows, f * width : (f + 1) * width] = hi
            stack[n, both_rows:, f * width : (f + 1) * width] = lo
        merged = jnp.dot(mask, stack[n], preferred_element_type=F32)
        for i in range(2):
            rr = slice(i * HMAX, (i + 1) * HMAX)
            for c in range(2):
                at = slice(c * LANES, (c + 1) * LANES)
                values = [
                    part[n, f, rr, at] + merged[rr, f * width + c * LANES : f * width + (c + 1) * LANES]
                    for f in range(FIELDS)
                ]
                sums[i] = list(contract(values, scale[i], *sums[i]))
    ones = jnp.ones((HMAX, LANES), F32)
    for k in range(2):
        acc[0:HMAX, :] = sums[0][k]
        acc[HMAX : rows - HMAX, :] = acc_in[k, HMAX : rows - HMAX, :]
        acc[rows - HMAX :, :] = sums[1][k]
        total = lax.dot_general(
            ones, acc[...] * (inv * inv), (((1,), (1,)), ((), ())), precision=lax.Precision.HIGHEST, preferred_element_type=F32
        )
        out_ref[:, k : k + 1, :] = jnp.broadcast_to(total[0:1][None], (out_ref.shape[0], 1, rows))


def call(kernel, out_shape, scratch, limit, *operands):
    vmem = pl.BlockSpec(memory_space=pltpu.VMEM)
    return pl.pallas_call(
        kernel,
        in_specs=[vmem] * len(operands),
        out_specs=jax.tree.map(lambda _: vmem, out_shape),
        out_shape=out_shape,
        scratch_shapes=scratch,
        compiler_params=pltpu.CompilerParams(vmem_limit_bytes=limit),
        cost_estimate=pl.CostEstimate(flops=4 * 10**9, bytes_accessed=2**20, transcendentals=0),
    )(*operands)


def local(velocity, strain, cell_height, stencil_reach):
    rows, cells = velocity.shape[1:]
    width = 2 * LANES
    blocks = cells // width - 1
    ends = 2 * HMAX
    shape = jax.ShapeDtypeStruct
    heights = cell_height.reshape(1, rows)
    near, far, wall_near, wall_far, velocity, strain, pair, both_ends = first_call(velocity, strain)
    zfar = lax.ppermute(far, "gz", far_pairs("gz", True))
    znear = lax.ppermute(near, "gz", near_pairs("gz"))
    yfar = lax.ppermute(wall_far, "gy", far_pairs("gy", False))
    ynear = lax.ppermute(wall_near, "gy", near_pairs("gy"))
    fh, fl, inner = call(
        inner_kernel,
        [
            shape((FIELDS, rows, cells), BF16),
            shape((WIDE, rows, cells), BF16),
            shape((blocks, FIELDS, rows, width), F32),
        ],
        [],
        LARGE_VMEM,
        velocity,
        strain,
        pair,
    )
    near, far = corner_call(heights, znear, zfar)
    corner_far = lax.ppermute(far, "gy", far_pairs("gy", False))
    corner_near = lax.ppermute(near, "gy", near_pairs("gy"))
    acc, part, hh, hl, halo_inner = call(
        outer_kernel,
        [
            shape((2, rows, LANES), F32),
            shape((blocks + 1, FIELDS, ends, width), F32),
            shape((FIELDS, ends, cells), BF16),
            shape((WIDE, ends, cells), BF16),
            shape((blocks, FIELDS, ends, width), F32),
        ],
        [
            pltpu.VMEM((FIELDS, rows, LANES), BF16),
            pltpu.VMEM((WIDE, rows, LANES), BF16),
            pltpu.VMEM((blocks + 1, 2 * rows, FIELDS * width), BF16),
        ],
        LARGE_VMEM,
        heights,
        stencil_reach,
        fh,
        fl,
        inner,
        znear,
        zfar,
        ynear,
        yfar,
        pair,
        both_ends,
    )
    sums = call(
        last_kernel,
        shape((lax.axis_size("gz"), 2, rows), F32),
        [
            pltpu.VMEM((FIELDS, ends, LANES), BF16),
            pltpu.VMEM((WIDE, ends, LANES), BF16),
            pltpu.VMEM((blocks + 1, 2 * ends, FIELDS * width), BF16),
            pltpu.VMEM((rows, LANES), F32),
        ],
        LARGE_VMEM,
        heights,
        stencil_reach,
        corner_near,
        corner_far,
        acc,
        part,
        hh,
        hl,
        halo_inner,
        both_ends,
    )
    sums = jnp.sum(lax.all_to_all(sums, "gz", 0, 0), axis=0)
    total = lax.axis_size("gz") * cells
    return sums[0] / total / (sums[1] / total + 1e-06)


def near_pairs(axis):
    return [(i, i ^ 1) for i in range(lax.axis_size(axis))]


def far_pairs(axis, closed):
    n = lax.axis_size(axis)
    pairs = []
    for i in range(1, n if closed else n - 1, 2):
        pairs += [(i, (i + 1) % n), ((i + 1) % n, i)]
    return pairs


def solution(mesh):
    in_specs = (P(None, "gy", "gz"), P(None, "gy", "gz"), P("gy"), P(None, "gy"))
    return jax.shard_map(local, mesh=mesh, in_specs=in_specs, out_specs=P("gy"), check_vma=False)
```

```python
import jax
import jax.numpy as jnp
from jax import lax
from jax.experimental import pallas as pl
from jax.experimental.pallas import tpu as pltpu
from jax.sharding import PartitionSpec as P

NX = 8
HMAX = 8
LANES = 128
FIELDS = 21
WIDE = 15
FIRST_VMEM = 51 * 1024 * 1024
SMALL_VMEM = 24 * 1024 * 1024
LARGE_VMEM = 24 * 1024 * 1024
LEAD_INDEX = (0, 1, 2, 0, 0, 1)
TAIL_INDEX = (0, 1, 2, 1, 2, 2)
TENSOR_WEIGHTS = (1.0, 1.0, 1.0, 2.0, 2.0, 2.0)
F32 = jnp.float32
BF16 = jnp.bfloat16


def strain_rate(s):
    squares = 2.0 * (s[0] * s[0] + s[1] * s[1] + s[2] * s[2])
    squares = squares + 4.0 * (s[3] * s[3] + s[4] * s[4] + s[5] * s[5])
    return jnp.sqrt(squares)


def lane_iota(shape):
    return lax.broadcasted_iota(jnp.int32, shape, len(shape) - 1)


def rot(x, amount):
    amount = amount % LANES
    return pltpu.roll(x, amount, x.ndim - 1) if amount else x


def cell_weights(source, target):
    turn = (source - target) & (NX - 1)
    along = jnp.where(turn == 0, 0.5, jnp.where((turn == 1) | (turn == NX - 1), 0.25, 0.0))
    step = ((source + LANES) >> 3) - ((target + LANES) >> 3)
    across = jnp.where(step == 0, 0.5, jnp.where((step == 1) | (step == -1), 0.25, 0.0))
    return along * across


def pair_filter():
    shape = (3 * LANES, 2 * LANES)
    k = lax.broadcasted_iota(jnp.int32, shape, 0)
    return cell_weights(jnp.where(k < 5 * LANES // 2, k, k - 3 * LANES), lane_iota(shape)).astype(BF16)


def ends_filter():
    shape = (3 * LANES, 2 * LANES)
    k = lax.broadcasted_iota(jnp.int32, shape, 0)
    m = lane_iota(shape)
    place = k & (LANES - 1)
    middle = LANES // 2
    outer = k >= 2 * LANES
    last = place >= LANES - NX
    after = (place >= middle - NX) & (place < middle)
    before = (place >= middle) & (place < middle + NX)
    used = (place < NX) | last | after | before
    shift = jnp.where(last, -LANES, jnp.where(after, LANES - middle + NX, jnp.where(before, -middle - NX, LANES)))
    source = jnp.where(outer, place + shift, place)
    tile = jnp.where(outer, jnp.where(last | after, 1, 0), k >> 7)
    fits = (tile == (m >> 7)) & (used | (k < 2 * LANES))
    return jnp.where(fits, cell_weights(source, m & (LANES - 1)), 0.0).astype(BF16)


def first_kernel(v_ref, s_ref, near_ref, far_ref, wall_near, wall_far, v_out, s_out, pair_ref, ends_ref, sems):
    rows, cells = v_ref.shape[1:]
    spans = ((0, LANES), (cells - LANES, LANES), (LANES, cells - 2 * LANES))
    copies = []
    for i, (start, size) in enumerate(spans):
        for j, (ref, out) in enumerate(((v_ref, v_out), (s_ref, s_out))):
            at = pl.ds(start, size)
            copies.append(pltpu.make_async_copy(ref.at[:, :, at], out.at[:, :, at], sems.at[i, j]))
    for copy in copies:
        copy.start()
    pair_ref[...] = pair_filter()
    ends_ref[...] = ends_filter()
    for copy in copies[:4]:
        copy.wait()
    lane = lane_iota((rows, LANES))
    left = jnp.zeros((rows, LANES), F32)
    right = jnp.zeros((rows, LANES), F32)
    for f in range(9):
        ref, at = (v_out, f) if f < 3 else (s_out, f - 3)
        here = (lane >= NX * f) & (lane < NX * (f + 1))
        left = jnp.where(here, rot(ref[at, :, :LANES].astype(F32), NX * f), left)
        right = jnp.where(here, rot(ref[at, :, cells - LANES :].astype(F32), NX * f + NX), right)
    odd = lax.axis_index("gz") % 2 == 1
    near_ref[...] = jnp.where(odd, left, right)
    far_ref[...] = jnp.where(odd, right, left)
    for copy in copies[4:]:
        copy.wait()
    gy_odd = lax.axis_index("gy") % 2 == 1
    for f in range(9):
        at = slice(f * cells, (f + 1) * cells)
        if f < 3:
            low, high = v_out[f, :HMAX, :], v_out[f, rows - HMAX :, :]
        else:
            low = s_out[f - 3, : 2 * HMAX, :].astype(F32)[:HMAX]
            high = s_out[f - 3, rows - 2 * HMAX :, :].astype(F32)[HMAX:]
        wall_near[:, at] = jnp.where(gy_odd, low, high)
        wall_far[:, at] = jnp.where(gy_odd, high, low)


def first_call(velocity, strain):
    rows, cells = velocity.shape[1:]
    hbm = pl.BlockSpec(memory_space=pltpu.HBM)
    vmem = pl.BlockSpec(memory_space=pltpu.VMEM)
    shape = jax.ShapeDtypeStruct
    return pl.pallas_call(
        first_kernel,
        in_specs=[hbm] * 2,
        out_specs=[vmem] * 8,
        out_shape=[shape((rows, LANES), F32)] * 2
        + [shape((HMAX, 9 * cells), F32)] * 2
        + [shape(x.shape, x.dtype) for x in (velocity, strain)]
        + [shape((3 * LANES, 2 * LANES), BF16)] * 2,
        scratch_shapes=[pltpu.SemaphoreType.DMA((3, 2))],
        compiler_params=pltpu.CompilerParams(vmem_limit_bytes=FIRST_VMEM),
    )(velocity, strain)


def corner_kernel(h_ref, znear, zfar, near_ref, far_ref):
    rows = znear.shape[0]
    gz_odd = lax.axis_index("gz") % 2 == 1
    gy_odd = lax.axis_index("gy") % 2 == 1
    lane = lane_iota((HMAX, LANES))
    row = lax.broadcasted_iota(jnp.int32, (HMAX, LANES), 0)
    stamp = (row == 0) & (lane >= 9 * NX) & (lane < 10 * NX)
    heights = jnp.broadcast_to(jnp.pad(h_ref[...], ((0, 0), (0, LANES - rows))), (HMAX, LANES))
    sides = []
    for r0 in (0, rows - HMAX):
        zn = znear[r0 : r0 + HMAX, :]
        zf = zfar[r0 : r0 + HMAX, :]
        zl = jnp.where(stamp, rot(heights, 9 * NX - r0), jnp.where(gz_odd, zn, zf))
        sides.append((zl, jnp.where(gz_odd, zf, zn)))
    (low_left, low_right), (high_left, high_right) = sides
    near_ref[:, :LANES] = jnp.where(gy_odd, low_left, high_left)
    near_ref[:, LANES:] = jnp.where(gy_odd, low_right, high_right)
    far_ref[:, :LANES] = jnp.where(gy_odd, high_left, low_left)
    far_ref[:, LANES:] = jnp.where(gy_odd, high_right, low_right)


def corner_call(heights, znear, zfar):
    vmem = pl.BlockSpec(memory_space=pltpu.VMEM)
    return pl.pallas_call(
        corner_kernel,
        in_specs=[vmem] * 3,
        out_specs=[vmem] * 2,
        out_shape=[jax.ShapeDtypeStruct((HMAX, 2 * LANES), F32)] * 2,
        compiler_params=pltpu.CompilerParams(vmem_limit_bytes=SMALL_VMEM),
    )(heights, znear, zfar)


def split2(x):
    hi = x.astype(BF16)
    return hi, (x - hi.astype(F32)).astype(BF16)


def store_fields(u, s, put_high, put_low):
    tensor = [x.astype(F32) for x in s]
    rate = strain_rate(tensor)
    wide = u + [u[a] * u[b] for a, b in zip(LEAD_INDEX, TAIL_INDEX)] + [rate * x for x in tensor]
    for f, value in enumerate(wide):
        hi, lo = split2(value)
        put_high(f, hi)
        put_low(f, lo)
    for f, value in enumerate(s):
        put_high(WIDE + f, value.astype(BF16))


def smooth(rows, operand, matrix_ref):
    wide, narrow = slice(0, WIDE), slice(WIDE, FIELDS)
    lhs = jnp.concatenate([operand(True, wide), operand(False, wide)], axis=-1).reshape(WIDE * rows, -1)
    matrix = matrix_ref[...]
    first = jnp.dot(lhs, jnp.concatenate([matrix, matrix], axis=0), preferred_element_type=F32)
    lhs = operand(True, narrow).reshape((FIELDS - WIDE) * rows, -1)
    second = jnp.dot(lhs, matrix, preferred_element_type=F32)
    return [first[f * rows : (f + 1) * rows] for f in range(WIDE)] + [
        second[f * rows : (f + 1) * rows] for f in range(FIELDS - WIDE)
    ]


def pick(after, before):
    return jnp.where(lane_iota(after.shape) < LANES // 2, after, before)


def smooth_pair(n, fh, fl, pair_ref):
    def operand(high, fields):
        ref = fh if high else fl
        tile = [ref[fields, :, (2 * n + i) * LANES : (2 * n + i + 1) * LANES] for i in range(4)]
        return jnp.concatenate([tile[1], tile[2], pick(tile[3], tile[0])], axis=-1)

    return smooth(fh.shape[1], operand, pair_ref)


def smooth_ends(fh, fl, eh, el, ends_ref):
    cells = fh.shape[2]

    def operand(high, fields):
        ref, outer = (fh, eh) if high else (fl, el)
        second = ref[fields, :, LANES : 2 * LANES]
        ahead = ref[fields, :, cells - 2 * LANES : cells - LANES]
        lane = lane_iota(second.shape)
        edge = jnp.where(lane < NX, second, jnp.where(lane >= LANES - NX, ahead, outer[fields]))
        return jnp.concatenate([ref[fields, :, :LANES], ref[fields, :, cells - LANES :], edge], axis=-1)

    return smooth(fh.shape[1], operand, ends_ref)


def contract(g, inv, num, den):
    u, p, m, s = g[0:3], g[3:9], g[9:15], g[15:21]
    rate = 4.0 * inv * strain_rate(s)
    scaled = [inv * x for x in u]
    for k in range(6):
        leonard = p[k] - scaled[LEAD_INDEX[k]] * u[TAIL_INDEX[k]]
        model = m[k] - rate * s[k]
        weighted = TENSOR_WEIGHTS[k] * model
        num = num + weighted * leonard
        den = den + weighted * model
    return num, den


def to_column(row_vector, size):
    shape = (size, LANES)
    eye = lax.broadcasted_iota(jnp.int32, shape, 0) == lane_iota(shape)
    return jnp.sum(jnp.where(eye, jnp.broadcast_to(row_vector, shape), 0.0), axis=1, keepdims=True)


def to_row(column_vector, row):
    return jnp.sum(jnp.where(row == lane_iota(row.shape), column_vector, 0.0), axis=0, keepdims=True)


def pad_lanes(x):
    return jnp.pad(x, ((0, 0), (0, LANES - x.shape[1])))


def stencil_holds(place, row, down, up, rows):
    gy = lax.axis_index("gy")
    lowest = jnp.maximum(row - down, -gy * rows)
    highest = jnp.minimum(row + up, (lax.axis_size("gy") - gy) * rows - 1)
    return (place >= lowest) & (place <= highest)


def end_rows(x):
    return jnp.concatenate([x[:HMAX], x[x.shape[0] - HMAX :]], axis=0)


def wall_block(g, mask, height, inv, stack, acc_ref, part_ref):
    rows = g[0].shape[0]
    width = 2 * LANES
    for f in range(FIELDS):
        hi, lo = split2(g[f] * height)
        stack[0:rows, f * width : (f + 1) * width] = hi
        stack[rows:, f * width : (f + 1) * width] = lo
    merged = jnp.dot(mask, stack[...], preferred_element_type=F32)
    for f in range(FIELDS):
        part_ref[f, 0:HMAX, :] = merged[0:HMAX, f * width : (f + 1) * width]
        part_ref[f, HMAX:, :] = merged[rows - HMAX :, f * width : (f + 1) * width]
    for r in range(HMAX, rows - HMAX, HMAX):
        num = acc_ref[0, r : r + HMAX, :]
        den = acc_ref[1, r : r + HMAX, :]
        scale = jnp.broadcast_to(inv[r : r + HMAX], (HMAX, LANES))
        for c in range(2):
            parts = [
                merged[r : r + HMAX, f * width + c * LANES : f * width + (c + 1) * LANES] for f in range(FIELDS)
            ]
            num, den = contract(parts, scale, num, den)
        acc_ref[0, r : r + HMAX, :] = num
        acc_ref[1, r : r + HMAX, :] = den


def inner_kernel(v_ref, s_ref, pair_ref, fh, fl, inner):
    rows, cells = v_ref.shape[1:]
    for t in range(cells // LANES):
        at = slice(t * LANES, (t + 1) * LANES)
        for r in range(0, rows, 16):
            rr = slice(r, r + 16)

            def put_high(f, x):
                fh[f, rr, at] = x

            def put_low(f, x):
                fl[f, rr, at] = x

            store_fields(
                [v_ref[f, rr, at] for f in range(3)], [s_ref[f, rr, at] for f in range(6)], put_high, put_low
            )
    for n in range(inner.shape[0]):
        g = smooth_pair(n, fh, fl, pair_ref)
        for f in range(FIELDS):
            inner[n, f] = g[f]


def outer_kernel(
    h_ref, reach_ref, fh, fl, inner, znear, zfar, ynear, yfar, pair_ref, ends_ref,
    sums_ref, part_ref, mask_ref, total_ref, hh, hl, halo_inner, eh, el, stack, acc_ref,
):
    rows, cells = fh.shape[1:]
    blocks = inner.shape[0]
    ends = 2 * HMAX
    gz_odd = lax.axis_index("gz") % 2 == 1
    gy_odd = lax.axis_index("gy") % 2 == 1
    reach = pad_lanes(reach_ref[...].astype(F32))
    down = to_column(reach[0:1], rows).astype(jnp.int32)
    up = to_column(reach[1:2], rows).astype(jnp.int32)
    column = lane_iota((rows, 2 * LANES))
    row = lax.broadcasted_iota(jnp.int32, (rows, 2 * LANES), 0)
    place = jnp.where(column < rows, column, column - rows)
    inside = stencil_holds(place, row, down, up, rows)
    mask = jnp.where(inside, 1.0, 0.0)[:, : 2 * rows].astype(BF16)
    heights = pad_lanes(h_ref[...])
    height = to_column(heights, rows)
    own = inside[:, :LANES] & (column[:, :LANES] < rows)
    total = jnp.sum(jnp.where(own, jnp.broadcast_to(heights, (rows, LANES)), 0.0), axis=1, keepdims=True)
    inv = 1.0 / total
    total_ref[...] = jnp.broadcast_to(end_rows(total), (ends, LANES))
    column = lane_iota((ends, LANES))
    row = lax.broadcasted_iota(jnp.int32, (ends, LANES), 0)
    turn = column & (ends - 1)
    place = jnp.where(turn < HMAX, turn - HMAX, turn - HMAX + rows)
    row = jnp.where(row < HMAX, row, row + rows - ends)
    inside = stencil_holds(place, row, end_rows(down), end_rows(up), rows) & (column < 2 * ends)
    mask_ref[...] = jnp.where(inside, 1.0, 0.0)
    acc_ref[...] = jnp.zeros_like(acc_ref)
    edge_fields(jnp.where(gz_odd, znear[...], zfar[...]), jnp.where(gz_odd, zfar[...], znear[...]), eh, el)
    for n in range(blocks + 1):
        if n < blocks:
            g = [inner[n, f] for f in range(FIELDS)]
        else:
            g = smooth_ends(fh, fl, eh, el, ends_ref)
        wall_block(g, mask, height, inv, stack.at[n], acc_ref, part_ref.at[n])
    for t in range(cells // LANES):
        at = slice(t * LANES, (t + 1) * LANES)

        def put_high(f, x):
            hh[f, :, at] = x

        def put_low(f, x):
            hl[f, :, at] = x

        raw = []
        for f in range(9):
            span = slice(f * cells + t * LANES, f * cells + (t + 1) * LANES)
            near, far = ynear[:, span], yfar[:, span]
            raw.append(jnp.concatenate([jnp.where(gy_odd, near, far), jnp.where(gy_odd, far, near)], axis=0))
        store_fields(raw[:3], raw[3:], put_high, put_low)
    for n in range(blocks):
        g = smooth_pair(n, hh, hl, pair_ref)
        for f in range(FIELDS):
            halo_inner[n, f] = g[f]
    for k in range(2):
        plane_sums = jnp.sum(acc_ref[k] * (inv * inv), axis=1, keepdims=True)
        sums_ref[k : k + 1, :] = to_row(plane_sums, lax.broadcasted_iota(jnp.int32, (rows, LANES), 0))


def edge_fields(zl, zr, eh, el):
    rows = zl.shape[0]
    lane = lane_iota((16, LANES))
    middle = LANES // 2
    follows = (lane >= middle - NX) & (lane < middle)
    precedes = (lane >= middle) & (lane < middle + NX)
    for r in range(0, rows, 16):
        rr = slice(r, r + 16)
        raw = [
            jnp.where(
                follows,
                rot(zr[rr], middle - NX - NX * f),
                jnp.where(precedes, rot(zl[rr], middle - NX * f), 0.0),
            )
            for f in range(9)
        ]

        def put_high(f, x):
            eh[f, rr, :] = x

        def put_low(f, x):
            el[f, rr, :] = x

        store_fields(raw[:3], raw[3:], put_high, put_low)


def last_kernel(near_ref, far_ref, sums_in, part, mask_ref, total_ref, hh, hl, halo_inner, ends_ref, out_ref, eh, el, stack):
    rows = out_ref.shape[2]
    width = 2 * LANES
    gy_odd = lax.axis_index("gy") % 2 == 1
    both_rows = 2 * HMAX

    def halo(at):
        near, far = near_ref[:, at], far_ref[:, at]
        return jnp.concatenate([jnp.where(gy_odd, near, far), jnp.where(gy_odd, far, near)], axis=0)

    zl = halo(slice(0, LANES))
    zr = halo(slice(LANES, 2 * LANES))
    below = rot(zl[:HMAX], -9 * NX)[0:1]
    above = rot(zl[HMAX:], -9 * NX)[0:1]
    height = jnp.concatenate([to_column(below, HMAX), to_column(above, HMAX)], axis=0)
    lane = lane_iota((both_rows, LANES))
    heights = jnp.where(lane[0:1] < HMAX, below, rot(above, HMAX))
    outside = jnp.where(lane < both_rows, mask_ref[...] * heights, 0.0)
    inv = 1.0 / (total_ref[...] + jnp.sum(outside, axis=1, keepdims=True))
    scale = [inv[:HMAX], inv[HMAX:]]
    mask = mask_ref[:, : 2 * both_rows].astype(BF16)

    edge_fields(zl, zr, eh, el)
    zero = jnp.zeros((HMAX, LANES), F32)
    sums = [[zero, zero], [zero, zero]]
    blocks = halo_inner.shape[0]
    for n in range(blocks + 1):
        if n < blocks:
            g = [halo_inner[n, f] for f in range(FIELDS)]
        else:
            g = smooth_ends(hh, hl, eh, el, ends_ref)
        for f in range(FIELDS):
            hi, lo = split2(g[f] * height)
            stack[n, 0:both_rows, f * width : (f + 1) * width] = hi
            stack[n, both_rows:, f * width : (f + 1) * width] = lo
        merged = jnp.dot(mask, stack[n], preferred_element_type=F32)
        for i in range(2):
            rr = slice(i * HMAX, (i + 1) * HMAX)
            for c in range(2):
                at = slice(c * LANES, (c + 1) * LANES)
                values = [
                    part[n, f, rr, at] + merged[rr, f * width + c * LANES : f * width + (c + 1) * LANES]
                    for f in range(FIELDS)
                ]
                sums[i] = list(contract(values, scale[i], *sums[i]))
    row = lax.broadcasted_iota(jnp.int32, (both_rows, LANES), 0)
    row = jnp.where(row < HMAX, row, row + rows - both_rows)
    for k in range(2):
        values = jnp.concatenate([sums[0][k], sums[1][k]], axis=0) * (inv * inv)
        total = sums_in[k : k + 1, :] + to_row(jnp.sum(values, axis=1, keepdims=True), row)
        out_ref[:, k : k + 1, :] = jnp.broadcast_to(total[None, :, :rows], (out_ref.shape[0], 1, rows))


def call(kernel, out_shape, scratch, limit, *operands):
    vmem = pl.BlockSpec(memory_space=pltpu.VMEM)
    return pl.pallas_call(
        kernel,
        in_specs=[vmem] * len(operands),
        out_specs=jax.tree.map(lambda _: vmem, out_shape),
        out_shape=out_shape,
        scratch_shapes=scratch,
        compiler_params=pltpu.CompilerParams(vmem_limit_bytes=limit),
        cost_estimate=pl.CostEstimate(flops=4 * 10**9, bytes_accessed=2**20, transcendentals=0),
    )(*operands)


def local(velocity, strain, cell_height, stencil_reach):
    rows, cells = velocity.shape[1:]
    width = 2 * LANES
    blocks = cells // width - 1
    ends = 2 * HMAX
    shape = jax.ShapeDtypeStruct
    heights = cell_height.reshape(1, rows)
    near, far, wall_near, wall_far, velocity, strain, pair, both_ends = first_call(velocity, strain)
    zfar = lax.ppermute(far, "gz", far_pairs("gz", True))
    znear = lax.ppermute(near, "gz", near_pairs("gz"))
    yfar = lax.ppermute(wall_far, "gy", far_pairs("gy", False))
    ynear = lax.ppermute(wall_near, "gy", near_pairs("gy"))
    fh, fl, inner = call(
        inner_kernel,
        [
            shape((FIELDS, rows, cells), BF16),
            shape((WIDE, rows, cells), BF16),
            shape((blocks, FIELDS, rows, width), F32),
        ],
        [],
        LARGE_VMEM,
        velocity,
        strain,
        pair,
    )
    near, far = corner_call(heights, znear, zfar)
    corner_far = lax.ppermute(far, "gy", far_pairs("gy", False))
    corner_near = lax.ppermute(near, "gy", near_pairs("gy"))
    sums, part, mask, totals, hh, hl, halo_inner = call(
        outer_kernel,
        [
            shape((2, LANES), F32),
            shape((blocks + 1, FIELDS, ends, width), F32),
            shape((ends, LANES), F32),
            shape((ends, LANES), F32),
            shape((FIELDS, ends, cells), BF16),
            shape((WIDE, ends, cells), BF16),
            shape((blocks, FIELDS, ends, width), F32),
        ],
        [
            pltpu.VMEM((FIELDS, rows, LANES), BF16),
            pltpu.VMEM((WIDE, rows, LANES), BF16),
            pltpu.VMEM((blocks + 1, 2 * rows, FIELDS * width), BF16),
            pltpu.VMEM((2, rows, LANES), F32),
        ],
        LARGE_VMEM,
        heights,
        stencil_reach,
        fh,
        fl,
        inner,
        znear,
        zfar,
        ynear,
        yfar,
        pair,
        both_ends,
    )
    sums = call(
        last_kernel,
        shape((lax.axis_size("gz"), 2, rows), F32),
        [
            pltpu.VMEM((FIELDS, ends, LANES), BF16),
            pltpu.VMEM((WIDE, ends, LANES), BF16),
            pltpu.VMEM((blocks + 1, 2 * ends, FIELDS * width), BF16),
        ],
        LARGE_VMEM,
        corner_near,
        corner_far,
        sums,
        part,
        mask,
        totals,
        hh,
        hl,
        halo_inner,
        both_ends,
    )
    sums = jnp.sum(lax.all_to_all(sums, "gz", 0, 0), axis=0)
    total = lax.axis_size("gz") * cells
    return sums[0] / total / (sums[1] / total + 1e-06)


def near_pairs(axis):
    return [(i, i ^ 1) for i in range(lax.axis_size(axis))]


def far_pairs(axis, closed):
    n = lax.axis_size(axis)
    pairs = []
    for i in range(1, n if closed else n - 1, 2):
        pairs += [(i, (i + 1) % n), ((i + 1) % n, i)]
    return pairs


def solution(mesh):
    in_specs = (P(None, "gy", "gz"), P(None, "gy", "gz"), P("gy"), P(None, "gy"))
    return jax.shard_map(local, mesh=mesh, in_specs=in_specs, out_specs=P("gy"), check_vma=False)
```

```python
import jax
import jax.numpy as jnp
from jax import lax
from jax.experimental import pallas as pl
from jax.experimental.pallas import tpu as pltpu
from jax.sharding import PartitionSpec as P

NX = 8
HMAX = 8
LANES = 128
FIELDS = 21
WIDE = 15
FIRST_VMEM = 51 * 1024 * 1024
SMALL_VMEM = 24 * 1024 * 1024
LARGE_VMEM = 24 * 1024 * 1024
LEAD_INDEX = (0, 1, 2, 0, 0, 1)
TAIL_INDEX = (0, 1, 2, 1, 2, 2)
TENSOR_WEIGHTS = (1.0, 1.0, 1.0, 2.0, 2.0, 2.0)
F32 = jnp.float32
BF16 = jnp.bfloat16


def strain_rate(s):
    squares = 2.0 * (s[0] * s[0] + s[1] * s[1] + s[2] * s[2])
    squares = squares + 4.0 * (s[3] * s[3] + s[4] * s[4] + s[5] * s[5])
    return jnp.sqrt(squares)


def lane_iota(shape):
    return lax.broadcasted_iota(jnp.int32, shape, len(shape) - 1)


def rot(x, amount):
    amount = amount % LANES
    return pltpu.roll(x, amount, x.ndim - 1) if amount else x


def cell_weights(source, target):
    turn = (source - target) & (NX - 1)
    along = jnp.where(turn == 0, 0.5, jnp.where((turn == 1) | (turn == NX - 1), 0.25, 0.0))
    step = ((source + LANES) >> 3) - ((target + LANES) >> 3)
    across = jnp.where(step == 0, 0.5, jnp.where((step == 1) | (step == -1), 0.25, 0.0))
    return along * across


def pair_filter():
    shape = (3 * LANES, 2 * LANES)
    k = lax.broadcasted_iota(jnp.int32, shape, 0)
    return cell_weights(jnp.where(k < 5 * LANES // 2, k, k - 3 * LANES), lane_iota(shape)).astype(BF16)


def ends_filter():
    shape = (3 * LANES, 2 * LANES)
    k = lax.broadcasted_iota(jnp.int32, shape, 0)
    m = lane_iota(shape)
    place = k & (LANES - 1)
    middle = LANES // 2
    outer = k >= 2 * LANES
    last = place >= LANES - NX
    after = (place >= middle - NX) & (place < middle)
    before = (place >= middle) & (place < middle + NX)
    used = (place < NX) | last | after | before
    shift = jnp.where(last, -LANES, jnp.where(after, LANES - middle + NX, jnp.where(before, -middle - NX, LANES)))
    source = jnp.where(outer, place + shift, place)
    tile = jnp.where(outer, jnp.where(last | after, 1, 0), k >> 7)
    fits = (tile == (m >> 7)) & (used | (k < 2 * LANES))
    return jnp.where(fits, cell_weights(source, m & (LANES - 1)), 0.0).astype(BF16)


def first_kernel(v_ref, s_ref, near_ref, far_ref, wall_near, wall_far, v_out, s_out, pair_ref, ends_ref, sems):
    rows, cells = v_ref.shape[1:]
    spans = ((0, LANES), (cells - LANES, LANES), (LANES, cells - 2 * LANES))
    copies = []
    for i, (start, size) in enumerate(spans):
        for j, (ref, out) in enumerate(((v_ref, v_out), (s_ref, s_out))):
            at = pl.ds(start, size)
            copies.append(pltpu.make_async_copy(ref.at[:, :, at], out.at[:, :, at], sems.at[i, j]))
    for copy in copies:
        copy.start()
    pair_ref[...] = pair_filter()
    ends_ref[...] = ends_filter()
    for copy in copies[:4]:
        copy.wait()
    lane = lane_iota((rows, LANES))
    left = jnp.zeros((rows, LANES), F32)
    right = jnp.zeros((rows, LANES), F32)
    for f in range(9):
        ref, at = (v_out, f) if f < 3 else (s_out, f - 3)
        here = (lane >= NX * f) & (lane < NX * (f + 1))
        left = jnp.where(here, rot(ref[at, :, :LANES].astype(F32), NX * f), left)
        right = jnp.where(here, rot(ref[at, :, cells - LANES :].astype(F32), NX * f + NX), right)
    odd = lax.axis_index("gz") % 2 == 1
    near_ref[...] = jnp.where(odd, left, right)
    far_ref[...] = jnp.where(odd, right, left)
    for copy in copies[4:]:
        copy.wait()
    gy_odd = lax.axis_index("gy") % 2 == 1
    for f in range(9):
        at = slice(f * cells, (f + 1) * cells)
        if f < 3:
            low, high = v_out[f, :HMAX, :], v_out[f, rows - HMAX :, :]
        else:
            low = s_out[f - 3, : 2 * HMAX, :].astype(F32)[:HMAX]
            high = s_out[f - 3, rows - 2 * HMAX :, :].astype(F32)[HMAX:]
        wall_near[:, at] = jnp.where(gy_odd, low, high)
        wall_far[:, at] = jnp.where(gy_odd, high, low)


def first_call(velocity, strain):
    rows, cells = velocity.shape[1:]
    hbm = pl.BlockSpec(memory_space=pltpu.HBM)
    vmem = pl.BlockSpec(memory_space=pltpu.VMEM)
    shape = jax.ShapeDtypeStruct
    return pl.pallas_call(
        first_kernel,
        in_specs=[hbm] * 2,
        out_specs=[vmem] * 8,
        out_shape=[shape((rows, LANES), F32)] * 2
        + [shape((HMAX, 9 * cells), F32)] * 2
        + [shape(x.shape, x.dtype) for x in (velocity, strain)]
        + [shape((3 * LANES, 2 * LANES), BF16)] * 2,
        scratch_shapes=[pltpu.SemaphoreType.DMA((3, 2))],
        compiler_params=pltpu.CompilerParams(vmem_limit_bytes=FIRST_VMEM),
    )(velocity, strain)


def corner_kernel(h_ref, znear, zfar, near_ref, far_ref):
    rows = znear.shape[0]
    gz_odd = lax.axis_index("gz") % 2 == 1
    gy_odd = lax.axis_index("gy") % 2 == 1
    lane = lane_iota((HMAX, LANES))
    row = lax.broadcasted_iota(jnp.int32, (HMAX, LANES), 0)
    stamp = (row == 0) & (lane >= 9 * NX) & (lane < 10 * NX)
    heights = jnp.broadcast_to(jnp.pad(h_ref[...], ((0, 0), (0, LANES - rows))), (HMAX, LANES))
    sides = []
    for r0 in (0, rows - HMAX):
        zn = znear[r0 : r0 + HMAX, :]
        zf = zfar[r0 : r0 + HMAX, :]
        zl = jnp.where(stamp, rot(heights, 9 * NX - r0), jnp.where(gz_odd, zn, zf))
        sides.append((zl, jnp.where(gz_odd, zf, zn)))
    (low_left, low_right), (high_left, high_right) = sides
    near_ref[:, :LANES] = jnp.where(gy_odd, low_left, high_left)
    near_ref[:, LANES:] = jnp.where(gy_odd, low_right, high_right)
    far_ref[:, :LANES] = jnp.where(gy_odd, high_left, low_left)
    far_ref[:, LANES:] = jnp.where(gy_odd, high_right, low_right)


def corner_call(heights, znear, zfar):
    vmem = pl.BlockSpec(memory_space=pltpu.VMEM)
    return pl.pallas_call(
        corner_kernel,
        in_specs=[vmem] * 3,
        out_specs=[vmem] * 2,
        out_shape=[jax.ShapeDtypeStruct((HMAX, 2 * LANES), F32)] * 2,
        compiler_params=pltpu.CompilerParams(vmem_limit_bytes=SMALL_VMEM),
    )(heights, znear, zfar)


def split2(x):
    hi = x.astype(BF16)
    return hi, (x - hi.astype(F32)).astype(BF16)


def store_fields(u, s, put_high, put_low):
    tensor = [x.astype(F32) for x in s]
    rate = strain_rate(tensor)
    wide = u + [u[a] * u[b] for a, b in zip(LEAD_INDEX, TAIL_INDEX)] + [rate * x for x in tensor]
    for f, value in enumerate(wide):
        hi, lo = split2(value)
        put_high(f, hi)
        put_low(f, lo)
    for f, value in enumerate(s):
        put_high(WIDE + f, value.astype(BF16))


def smooth(rows, operand, matrix_ref):
    wide, narrow = slice(0, WIDE), slice(WIDE, FIELDS)
    lhs = jnp.concatenate([operand(True, wide), operand(False, wide)], axis=-1).reshape(WIDE * rows, -1)
    matrix = matrix_ref[...]
    first = jnp.dot(lhs, jnp.concatenate([matrix, matrix], axis=0), preferred_element_type=F32)
    lhs = operand(True, narrow).reshape((FIELDS - WIDE) * rows, -1)
    second = jnp.dot(lhs, matrix, preferred_element_type=F32)
    return [first[f * rows : (f + 1) * rows] for f in range(WIDE)] + [
        second[f * rows : (f + 1) * rows] for f in range(FIELDS - WIDE)
    ]


def pick(after, before):
    return jnp.where(lane_iota(after.shape) < LANES // 2, after, before)


def smooth_pair(n, fh, fl, pair_ref):
    def operand(high, fields):
        ref = fh if high else fl
        tile = [ref[fields, :, (2 * n + i) * LANES : (2 * n + i + 1) * LANES] for i in range(4)]
        return jnp.concatenate([tile[1], tile[2], pick(tile[3], tile[0])], axis=-1)

    return smooth(fh.shape[1], operand, pair_ref)


def smooth_ends(fh, fl, eh, el, ends_ref):
    cells = fh.shape[2]

    def operand(high, fields):
        ref, outer = (fh, eh) if high else (fl, el)
        second = ref[fields, :, LANES : 2 * LANES]
        ahead = ref[fields, :, cells - 2 * LANES : cells - LANES]
        lane = lane_iota(second.shape)
        edge = jnp.where(lane < NX, second, jnp.where(lane >= LANES - NX, ahead, outer[fields]))
        return jnp.concatenate([ref[fields, :, :LANES], ref[fields, :, cells - LANES :], edge], axis=-1)

    return smooth(fh.shape[1], operand, ends_ref)


def contract(g, inv, num, den):
    u, p, m, s = g[0:3], g[3:9], g[9:15], g[15:21]
    rate = 4.0 * inv * strain_rate(s)
    scaled = [inv * x for x in u]
    for k in range(6):
        leonard = p[k] - scaled[LEAD_INDEX[k]] * u[TAIL_INDEX[k]]
        model = m[k] - rate * s[k]
        weighted = TENSOR_WEIGHTS[k] * model
        num = num + weighted * leonard
        den = den + weighted * model
    return num, den


def to_column(row_vector, size):
    shape = (size, LANES)
    eye = lax.broadcasted_iota(jnp.int32, shape, 0) == lane_iota(shape)
    return jnp.sum(jnp.where(eye, jnp.broadcast_to(row_vector, shape), 0.0), axis=1, keepdims=True)


def to_row(column_vector, row):
    return jnp.sum(jnp.where(row == lane_iota(row.shape), column_vector, 0.0), axis=0, keepdims=True)


def pad_lanes(x):
    return jnp.pad(x, ((0, 0), (0, LANES - x.shape[1])))


def stencil_holds(place, row, down, up, rows):
    gy = lax.axis_index("gy")
    lowest = jnp.maximum(row - down, -gy * rows)
    highest = jnp.minimum(row + up, (lax.axis_size("gy") - gy) * rows - 1)
    return (place >= lowest) & (place <= highest)


def end_rows(x):
    return jnp.concatenate([x[:HMAX], x[x.shape[0] - HMAX :]], axis=0)


def wall_block(g, own_ref, height_ref, inv_ref, stack, acc_ref, part_ref):
    rows = g[0].shape[0]
    width = 2 * LANES
    height = jnp.concatenate([height_ref[...], height_ref[...]], axis=1)
    mask = own_ref[:, : 2 * rows]
    for f in range(FIELDS):
        hi, lo = split2(g[f] * height)
        stack[0:rows, f * width : (f + 1) * width] = hi
        stack[rows:, f * width : (f + 1) * width] = lo
    merged = jnp.dot(mask, stack[...], preferred_element_type=F32)
    for f in range(FIELDS):
        part_ref[f, 0:HMAX, :] = merged[0:HMAX, f * width : (f + 1) * width]
        part_ref[f, HMAX:, :] = merged[rows - HMAX :, f * width : (f + 1) * width]
    for r in range(HMAX, rows - HMAX, HMAX):
        num = acc_ref[0, r : r + HMAX, :]
        den = acc_ref[1, r : r + HMAX, :]
        scale = inv_ref[r : r + HMAX, :]
        for c in range(2):
            parts = [
                merged[r : r + HMAX, f * width + c * LANES : f * width + (c + 1) * LANES] for f in range(FIELDS)
            ]
            num, den = contract(parts, scale, num, den)
        acc_ref[0, r : r + HMAX, :] = num
        acc_ref[1, r : r + HMAX, :] = den


def leaves_early():
    gz = lax.axis_index("gz")
    y, z = gz // 4, gz % 4
    return (z == 0) | ((z == 1) & (y <= 1))


def inner_work(v_ref, s_ref, pair_ref, fh, fl, inner):
    rows, cells = v_ref.shape[1:]
    for t in range(cells // LANES):
        at = slice(t * LANES, (t + 1) * LANES)
        for r in range(0, rows, 16):
            rr = slice(r, r + 16)

            def put_high(f, x):
                fh[f, rr, at] = x

            def put_low(f, x):
                fl[f, rr, at] = x

            store_fields(
                [v_ref[f, rr, at] for f in range(3)], [s_ref[f, rr, at] for f in range(6)], put_high, put_low
            )
    for n in range(inner.shape[0]):
        g = smooth_pair(n, fh, fl, pair_ref)
        for f in range(FIELDS):
            inner[n, f] = g[f]


def early_kernel(v_ref, s_ref, pair_ref, a, b, c, d, fh, fl, inner, *same):
    @pl.when(leaves_early())
    def _():
        inner_work(v_ref, s_ref, pair_ref, fh, fl, inner)


def late_kernel(v_ref, s_ref, pair_ref, a, b, c, fh, fl, inner):
    @pl.when(jnp.logical_not(leaves_early()))
    def _():
        inner_work(v_ref, s_ref, pair_ref, fh, fl, inner)


def wall_kernel(
    h_ref, reach_ref, inner, acc_ref, part_ref, own_ref, height_ref, inv_ref, mask_ref, total_ref, stack
):
    rows = h_ref.shape[1]
    ends = 2 * HMAX
    reach = pad_lanes(reach_ref[...].astype(F32))
    down = to_column(reach[0:1], rows).astype(jnp.int32)
    up = to_column(reach[1:2], rows).astype(jnp.int32)
    column = lane_iota((rows, 2 * LANES))
    row = lax.broadcasted_iota(jnp.int32, (rows, 2 * LANES), 0)
    place = jnp.where(column < rows, column, column - rows)
    inside = stencil_holds(place, row, down, up, rows)
    own_ref[...] = jnp.where(inside, 1.0, 0.0).astype(BF16)
    heights = pad_lanes(h_ref[...])
    height_ref[...] = jnp.broadcast_to(to_column(heights, rows), (rows, LANES))
    own = inside[:, :LANES] & (column[:, :LANES] < rows)
    total = jnp.sum(jnp.where(own, jnp.broadcast_to(heights, (rows, LANES)), 0.0), axis=1, keepdims=True)
    inv_ref[...] = jnp.broadcast_to(1.0 / total, (rows, LANES))
    total_ref[...] = jnp.broadcast_to(end_rows(total), (ends, LANES))
    column = lane_iota((ends, LANES))
    row = lax.broadcasted_iota(jnp.int32, (ends, LANES), 0)
    turn = column & (ends - 1)
    place = jnp.where(turn < HMAX, turn - HMAX, turn - HMAX + rows)
    row = jnp.where(row < HMAX, row, row + rows - ends)
    inside = stencil_holds(place, row, end_rows(down), end_rows(up), rows) & (column < 2 * ends)
    mask_ref[...] = jnp.where(inside, 1.0, 0.0)
    acc_ref[...] = jnp.zeros_like(acc_ref)
    for n in range(inner.shape[0]):
        g = [inner[n, f] for f in range(FIELDS)]
        wall_block(g, own_ref, height_ref, inv_ref, stack.at[n], acc_ref, part_ref.at[n])


def outer_kernel(
    fh, fl, znear, zfar, ynear, yfar, pair_ref, ends_ref, acc_in, own_ref, height_ref, inv_ref,
    sums_ref, part_ref, hh, hl, halo_inner, eh, el, stack, acc_ref,
):
    rows, cells = fh.shape[1:]
    gz_odd = lax.axis_index("gz") % 2 == 1
    gy_odd = lax.axis_index("gy") % 2 == 1
    acc_ref[...] = acc_in[...]
    edge_fields(jnp.where(gz_odd, znear[...], zfar[...]), jnp.where(gz_odd, zfar[...], znear[...]), eh, el)
    g = smooth_ends(fh, fl, eh, el, ends_ref)
    wall_block(g, own_ref, height_ref, inv_ref, stack, acc_ref, part_ref)
    for t in range(cells // LANES):
        at = slice(t * LANES, (t + 1) * LANES)

        def put_high(f, x):
            hh[f, :, at] = x

        def put_low(f, x):
            hl[f, :, at] = x

        raw = []
        for f in range(9):
            span = slice(f * cells + t * LANES, f * cells + (t + 1) * LANES)
            near, far = ynear[:, span], yfar[:, span]
            raw.append(jnp.concatenate([jnp.where(gy_odd, near, far), jnp.where(gy_odd, far, near)], axis=0))
        store_fields(raw[:3], raw[3:], put_high, put_low)
    for n in range(halo_inner.shape[0]):
        g = smooth_pair(n, hh, hl, pair_ref)
        for f in range(FIELDS):
            halo_inner[n, f] = g[f]
    inv = inv_ref[...]
    for k in range(2):
        plane_sums = jnp.sum(acc_ref[k] * (inv * inv), axis=1, keepdims=True)
        sums_ref[k : k + 1, :] = to_row(plane_sums, lax.broadcasted_iota(jnp.int32, (rows, LANES), 0))


def edge_fields(zl, zr, eh, el):
    rows = zl.shape[0]
    lane = lane_iota((16, LANES))
    middle = LANES // 2
    follows = (lane >= middle - NX) & (lane < middle)
    precedes = (lane >= middle) & (lane < middle + NX)
    for r in range(0, rows, 16):
        rr = slice(r, r + 16)
        raw = [
            jnp.where(
                follows,
                rot(zr[rr], middle - NX - NX * f),
                jnp.where(precedes, rot(zl[rr], middle - NX * f), 0.0),
            )
            for f in range(9)
        ]

        def put_high(f, x):
            eh[f, rr, :] = x

        def put_low(f, x):
            el[f, rr, :] = x

        store_fields(raw[:3], raw[3:], put_high, put_low)


def last_kernel(near_ref, far_ref, sums_in, part_inner, part_ends, mask_ref, total_ref, hh, hl, halo_inner, ends_ref, out_ref, eh, el, stack):
    rows = out_ref.shape[2]
    width = 2 * LANES
    gy_odd = lax.axis_index("gy") % 2 == 1
    both_rows = 2 * HMAX

    def halo(at):
        near, far = near_ref[:, at], far_ref[:, at]
        return jnp.concatenate([jnp.where(gy_odd, near, far), jnp.where(gy_odd, far, near)], axis=0)

    zl = halo(slice(0, LANES))
    zr = halo(slice(LANES, 2 * LANES))
    below = rot(zl[:HMAX], -9 * NX)[0:1]
    above = rot(zl[HMAX:], -9 * NX)[0:1]
    height = jnp.concatenate([to_column(below, HMAX), to_column(above, HMAX)], axis=0)
    lane = lane_iota((both_rows, LANES))
    heights = jnp.where(lane[0:1] < HMAX, below, rot(above, HMAX))
    outside = jnp.where(lane < both_rows, mask_ref[...] * heights, 0.0)
    inv = 1.0 / (total_ref[...] + jnp.sum(outside, axis=1, keepdims=True))
    scale = [inv[:HMAX], inv[HMAX:]]
    mask = mask_ref[:, : 2 * both_rows].astype(BF16)

    edge_fields(zl, zr, eh, el)
    zero = jnp.zeros((HMAX, LANES), F32)
    sums = [[zero, zero], [zero, zero]]
    blocks = halo_inner.shape[0]
    for n in range(blocks + 1):
        if n < blocks:
            g = [halo_inner[n, f] for f in range(FIELDS)]
            part = part_inner.at[n]
        else:
            part = part_ends
            g = smooth_ends(hh, hl, eh, el, ends_ref)
        for f in range(FIELDS):
            hi, lo = split2(g[f] * height)
            stack[n, 0:both_rows, f * width : (f + 1) * width] = hi
            stack[n, both_rows:, f * width : (f + 1) * width] = lo
        merged = jnp.dot(mask, stack[n], preferred_element_type=F32)
        for i in range(2):
            rr = slice(i * HMAX, (i + 1) * HMAX)
            for c in range(2):
                at = slice(c * LANES, (c + 1) * LANES)
                values = [
                    part[f, rr, at] + merged[rr, f * width + c * LANES : f * width + (c + 1) * LANES]
                    for f in range(FIELDS)
                ]
                sums[i] = list(contract(values, scale[i], *sums[i]))
    row = lax.broadcasted_iota(jnp.int32, (both_rows, LANES), 0)
    row = jnp.where(row < HMAX, row, row + rows - both_rows)
    for k in range(2):
        values = jnp.concatenate([sums[0][k], sums[1][k]], axis=0) * (inv * inv)
        total = sums_in[k : k + 1, :] + to_row(jnp.sum(values, axis=1, keepdims=True), row)
        out_ref[:, k : k + 1, :] = jnp.broadcast_to(total[None, :, :rows], (out_ref.shape[0], 1, rows))


def call(kernel, out_shape, scratch, limit, *operands, aliases=None):
    vmem = pl.BlockSpec(memory_space=pltpu.VMEM)
    return pl.pallas_call(
        kernel,
        in_specs=[vmem] * len(operands),
        out_specs=jax.tree.map(lambda _: vmem, out_shape),
        out_shape=out_shape,
        scratch_shapes=scratch,
        input_output_aliases=aliases or {},
        compiler_params=pltpu.CompilerParams(vmem_limit_bytes=limit),
        cost_estimate=pl.CostEstimate(flops=4 * 10**9, bytes_accessed=2**20, transcendentals=0),
    )(*operands)


def local(velocity, strain, cell_height, stencil_reach):
    rows, cells = velocity.shape[1:]
    width = 2 * LANES
    blocks = cells // width - 1
    ends = 2 * HMAX
    shape = jax.ShapeDtypeStruct
    heights = cell_height.reshape(1, rows)
    near, far, wall_near, wall_far, velocity, strain, pair, both_ends = first_call(velocity, strain)
    own_work = [
        shape((FIELDS, rows, cells), BF16),
        shape((WIDE, rows, cells), BF16),
        shape((blocks, FIELDS, rows, width), F32),
    ]
    messages = (near, far, wall_near, wall_far)
    fh, fl, inner, near, far, wall_near, wall_far = call(
        early_kernel,
        own_work + [shape(x.shape, x.dtype) for x in messages],
        [],
        LARGE_VMEM,
        velocity,
        strain,
        pair,
        *messages,
        aliases={3 + i: 3 + i for i in range(4)},
    )
    znear = lax.ppermute(near, "gz", near_pairs("gz"))
    zfar = lax.ppermute(far, "gz", far_pairs("gz", True))
    yfar = lax.ppermute(wall_far, "gy", far_pairs("gy", False))
    ynear = lax.ppermute(wall_near, "gy", near_pairs("gy"))
    fh, fl, inner = call(
        late_kernel,
        own_work,
        [],
        LARGE_VMEM,
        velocity,
        strain,
        pair,
        fh,
        fl,
        inner,
        aliases={3 + i: i for i in range(3)},
    )
    acc, part_inner, own, height, inv, mask, totals = call(
        wall_kernel,
        [
            shape((2, rows, LANES), F32),
            shape((blocks, FIELDS, ends, width), F32),
            shape((rows, width), BF16),
            shape((rows, LANES), F32),
            shape((rows, LANES), F32),
            shape((ends, LANES), F32),
            shape((ends, LANES), F32),
        ],
        [pltpu.VMEM((blocks, 2 * rows, FIELDS * width), BF16)],
        LARGE_VMEM,
        heights,
        stencil_reach,
        inner,
    )
    near, far = corner_call(heights, znear, zfar)
    corner_far = lax.ppermute(far, "gy", far_pairs("gy", False))
    corner_near = lax.ppermute(near, "gy", near_pairs("gy"))
    sums, part_ends, hh, hl, halo_inner = call(
        outer_kernel,
        [
            shape((2, LANES), F32),
            shape((FIELDS, ends, width), F32),
            shape((FIELDS, ends, cells), BF16),
            shape((WIDE, ends, cells), BF16),
            shape((blocks, FIELDS, ends, width), F32),
        ],
        [
            pltpu.VMEM((FIELDS, rows, LANES), BF16),
            pltpu.VMEM((WIDE, rows, LANES), BF16),
            pltpu.VMEM((2 * rows, FIELDS * width), BF16),
            pltpu.VMEM((2, rows, LANES), F32),
        ],
        LARGE_VMEM,
        fh,
        fl,
        znear,
        zfar,
        ynear,
        yfar,
        pair,
        both_ends,
        acc,
        own,
        height,
        inv,
    )
    sums = call(
        last_kernel,
        shape((lax.axis_size("gz"), 2, rows), F32),
        [
            pltpu.VMEM((FIELDS, ends, LANES), BF16),
            pltpu.VMEM((WIDE, ends, LANES), BF16),
            pltpu.VMEM((blocks + 1, 2 * ends, FIELDS * width), BF16),
        ],
        LARGE_VMEM,
        corner_near,
        corner_far,
        sums,
        part_inner,
        part_ends,
        mask,
        totals,
        hh,
        hl,
        halo_inner,
        both_ends,
    )
    sums = jnp.sum(lax.all_to_all(sums, "gz", 0, 0), axis=0)
    total = lax.axis_size("gz") * cells
    return sums[0] / total / (sums[1] / total + 1e-06)


def near_pairs(axis):
    return [(i, i ^ 1) for i in range(lax.axis_size(axis))]


def far_pairs(axis, closed):
    n = lax.axis_size(axis)
    pairs = []
    for i in range(1, n if closed else n - 1, 2):
        pairs += [(i, (i + 1) % n), ((i + 1) % n, i)]
    return pairs


def solution(mesh):
    in_specs = (P(None, "gy", "gz"), P(None, "gy", "gz"), P("gy"), P(None, "gy"))
    return jax.shard_map(local, mesh=mesh, in_specs=in_specs, out_specs=P("gy"), check_vma=False)
```

```python
import jax
import jax.numpy as jnp
from jax import lax
from jax.experimental import pallas as pl
from jax.experimental.pallas import tpu as pltpu
from jax.sharding import PartitionSpec as P

NX = 8
HMAX = 8
LANES = 128
FIELDS = 21
WIDE = 15
FIRST_VMEM = 51 * 1024 * 1024
SMALL_VMEM = 24 * 1024 * 1024
LARGE_VMEM = 24 * 1024 * 1024
LEAD_INDEX = (0, 1, 2, 0, 0, 1)
TAIL_INDEX = (0, 1, 2, 1, 2, 2)
TENSOR_WEIGHTS = (1.0, 1.0, 1.0, 2.0, 2.0, 2.0)
F32 = jnp.float32
BF16 = jnp.bfloat16


def strain_rate(s):
    squares = 2.0 * (s[0] * s[0] + s[1] * s[1] + s[2] * s[2])
    squares = squares + 4.0 * (s[3] * s[3] + s[4] * s[4] + s[5] * s[5])
    return jnp.sqrt(squares)


def lane_iota(shape):
    return lax.broadcasted_iota(jnp.int32, shape, len(shape) - 1)


def rot(x, amount):
    amount = amount % LANES
    return pltpu.roll(x, amount, x.ndim - 1) if amount else x


def cell_weights(source, target):
    turn = (source - target) & (NX - 1)
    along = jnp.where(turn == 0, 0.5, jnp.where((turn == 1) | (turn == NX - 1), 0.25, 0.0))
    step = ((source + LANES) >> 3) - ((target + LANES) >> 3)
    across = jnp.where(step == 0, 0.5, jnp.where((step == 1) | (step == -1), 0.25, 0.0))
    return along * across


def pair_filter():
    shape = (3 * LANES, 2 * LANES)
    k = lax.broadcasted_iota(jnp.int32, shape, 0)
    return cell_weights(jnp.where(k < 5 * LANES // 2, k, k - 3 * LANES), lane_iota(shape)).astype(BF16)


def ends_filter():
    shape = (3 * LANES, 2 * LANES)
    k = lax.broadcasted_iota(jnp.int32, shape, 0)
    m = lane_iota(shape)
    place = k & (LANES - 1)
    middle = LANES // 2
    outer = k >= 2 * LANES
    last = place >= LANES - NX
    after = (place >= middle - NX) & (place < middle)
    before = (place >= middle) & (place < middle + NX)
    used = (place < NX) | last | after | before
    shift = jnp.where(last, -LANES, jnp.where(after, LANES - middle + NX, jnp.where(before, -middle - NX, LANES)))
    source = jnp.where(outer, place + shift, place)
    tile = jnp.where(outer, jnp.where(last | after, 1, 0), k >> 7)
    fits = (tile == (m >> 7)) & (used | (k < 2 * LANES))
    return jnp.where(fits, cell_weights(source, m & (LANES - 1)), 0.0).astype(BF16)


def first_kernel(v_ref, s_ref, near_ref, far_ref, wall_near, wall_far, v_out, s_out, pair_ref, ends_ref, sems):
    rows, cells = v_ref.shape[1:]
    spans = ((0, LANES), (cells - LANES, LANES), (LANES, cells - 2 * LANES))
    copies = []
    for i, (start, size) in enumerate(spans):
        for j, (ref, out) in enumerate(((v_ref, v_out), (s_ref, s_out))):
            at = pl.ds(start, size)
            copies.append(pltpu.make_async_copy(ref.at[:, :, at], out.at[:, :, at], sems.at[i, j]))
    for copy in copies:
        copy.start()
    pair_ref[...] = pair_filter()
    ends_ref[...] = ends_filter()
    for copy in copies[:4]:
        copy.wait()
    lane = lane_iota((rows, LANES))
    left = jnp.zeros((rows, LANES), F32)
    right = jnp.zeros((rows, LANES), F32)
    for f in range(9):
        ref, at = (v_out, f) if f < 3 else (s_out, f - 3)
        here = (lane >= NX * f) & (lane < NX * (f + 1))
        left = jnp.where(here, rot(ref[at, :, :LANES].astype(F32), NX * f), left)
        right = jnp.where(here, rot(ref[at, :, cells - LANES :].astype(F32), NX * f + NX), right)
    odd = lax.axis_index("gz") % 2 == 1
    near_ref[...] = jnp.where(odd, left, right)
    far_ref[...] = jnp.where(odd, right, left)
    for copy in copies[4:]:
        copy.wait()
    gy_odd = lax.axis_index("gy") % 2 == 1
    for f in range(9):
        at = slice(f * cells, (f + 1) * cells)
        if f < 3:
            low, high = v_out[f, :HMAX, :], v_out[f, rows - HMAX :, :]
        else:
            low = s_out[f - 3, : 2 * HMAX, :].astype(F32)[:HMAX]
            high = s_out[f - 3, rows - 2 * HMAX :, :].astype(F32)[HMAX:]
        wall_near[:, at] = jnp.where(gy_odd, low, high)
        wall_far[:, at] = jnp.where(gy_odd, high, low)


def first_call(velocity, strain):
    rows, cells = velocity.shape[1:]
    hbm = pl.BlockSpec(memory_space=pltpu.HBM)
    vmem = pl.BlockSpec(memory_space=pltpu.VMEM)
    shape = jax.ShapeDtypeStruct
    return pl.pallas_call(
        first_kernel,
        in_specs=[hbm] * 2,
        out_specs=[vmem] * 8,
        out_shape=[shape((rows, LANES), F32)] * 2
        + [shape((HMAX, 9 * cells), F32)] * 2
        + [shape(x.shape, x.dtype) for x in (velocity, strain)]
        + [shape((3 * LANES, 2 * LANES), BF16)] * 2,
        scratch_shapes=[pltpu.SemaphoreType.DMA((3, 2))],
        compiler_params=pltpu.CompilerParams(vmem_limit_bytes=FIRST_VMEM),
    )(velocity, strain)


def corner_kernel(h_ref, znear, zfar, near_ref, far_ref):
    rows = znear.shape[0]
    gz_odd = lax.axis_index("gz") % 2 == 1
    gy_odd = lax.axis_index("gy") % 2 == 1
    lane = lane_iota((HMAX, LANES))
    row = lax.broadcasted_iota(jnp.int32, (HMAX, LANES), 0)
    stamp = (row == 0) & (lane >= 9 * NX) & (lane < 10 * NX)
    heights = jnp.broadcast_to(jnp.pad(h_ref[...], ((0, 0), (0, LANES - rows))), (HMAX, LANES))
    sides = []
    for r0 in (0, rows - HMAX):
        zn = znear[r0 : r0 + HMAX, :]
        zf = zfar[r0 : r0 + HMAX, :]
        zl = jnp.where(stamp, rot(heights, 9 * NX - r0), jnp.where(gz_odd, zn, zf))
        sides.append((zl, jnp.where(gz_odd, zf, zn)))
    (low_left, low_right), (high_left, high_right) = sides
    near_ref[:, :LANES] = jnp.where(gy_odd, low_left, high_left)
    near_ref[:, LANES:] = jnp.where(gy_odd, low_right, high_right)
    far_ref[:, :LANES] = jnp.where(gy_odd, high_left, low_left)
    far_ref[:, LANES:] = jnp.where(gy_odd, high_right, low_right)


def corner_call(heights, znear, zfar):
    vmem = pl.BlockSpec(memory_space=pltpu.VMEM)
    return pl.pallas_call(
        corner_kernel,
        in_specs=[vmem] * 3,
        out_specs=[vmem] * 2,
        out_shape=[jax.ShapeDtypeStruct((HMAX, 2 * LANES), F32)] * 2,
        compiler_params=pltpu.CompilerParams(vmem_limit_bytes=SMALL_VMEM),
    )(heights, znear, zfar)


def split2(x):
    hi = x.astype(BF16)
    return hi, (x - hi.astype(F32)).astype(BF16)


def store_fields(u, s, put_high, put_low):
    tensor = [x.astype(F32) for x in s]
    rate = strain_rate(tensor)
    wide = u + [u[a] * u[b] for a, b in zip(LEAD_INDEX, TAIL_INDEX)] + [rate * x for x in tensor]
    for f, value in enumerate(wide):
        hi, lo = split2(value)
        put_high(f, hi)
        put_low(f, lo)
    for f, value in enumerate(s):
        put_high(WIDE + f, value.astype(BF16))


def smooth(rows, operand, matrix_ref):
    wide, narrow = slice(0, WIDE), slice(WIDE, FIELDS)
    lhs = jnp.concatenate([operand(True, wide), operand(False, wide)], axis=-1).reshape(WIDE * rows, -1)
    matrix = matrix_ref[...]
    first = jnp.dot(lhs, jnp.concatenate([matrix, matrix], axis=0), preferred_element_type=F32)
    lhs = operand(True, narrow).reshape((FIELDS - WIDE) * rows, -1)
    second = jnp.dot(lhs, matrix, preferred_element_type=F32)
    return [first[f * rows : (f + 1) * rows] for f in range(WIDE)] + [
        second[f * rows : (f + 1) * rows] for f in range(FIELDS - WIDE)
    ]


def pick(after, before):
    return jnp.where(lane_iota(after.shape) < LANES // 2, after, before)


def smooth_pair(n, fh, fl, pair_ref):
    def operand(high, fields):
        ref = fh if high else fl
        tile = [ref[fields, :, (2 * n + i) * LANES : (2 * n + i + 1) * LANES] for i in range(4)]
        return jnp.concatenate([tile[1], tile[2], pick(tile[3], tile[0])], axis=-1)

    return smooth(fh.shape[1], operand, pair_ref)


def smooth_ends(fh, fl, eh, el, ends_ref):
    cells = fh.shape[2]

    def operand(high, fields):
        ref, outer = (fh, eh) if high else (fl, el)
        second = ref[fields, :, LANES : 2 * LANES]
        ahead = ref[fields, :, cells - 2 * LANES : cells - LANES]
        lane = lane_iota(second.shape)
        edge = jnp.where(lane < NX, second, jnp.where(lane >= LANES - NX, ahead, outer[fields]))
        return jnp.concatenate([ref[fields, :, :LANES], ref[fields, :, cells - LANES :], edge], axis=-1)

    return smooth(fh.shape[1], operand, ends_ref)


def contract(g, inv, num, den):
    u, p, m, s = g[0:3], g[3:9], g[9:15], g[15:21]
    rate = 4.0 * inv * strain_rate(s)
    scaled = [inv * x for x in u]
    for k in range(6):
        leonard = p[k] - scaled[LEAD_INDEX[k]] * u[TAIL_INDEX[k]]
        model = m[k] - rate * s[k]
        weighted = TENSOR_WEIGHTS[k] * model
        num = num + weighted * leonard
        den = den + weighted * model
    return num, den


def to_column(row_vector, size):
    shape = (size, LANES)
    eye = lax.broadcasted_iota(jnp.int32, shape, 0) == lane_iota(shape)
    return jnp.sum(jnp.where(eye, jnp.broadcast_to(row_vector, shape), 0.0), axis=1, keepdims=True)


def to_row(column_vector, row):
    return jnp.sum(jnp.where(row == lane_iota(row.shape), column_vector, 0.0), axis=0, keepdims=True)


def pad_lanes(x):
    return jnp.pad(x, ((0, 0), (0, LANES - x.shape[1])))


def stencil_holds(place, row, down, up, rows):
    gy = lax.axis_index("gy")
    lowest = jnp.maximum(row - down, -gy * rows)
    highest = jnp.minimum(row + up, (lax.axis_size("gy") - gy) * rows - 1)
    return (place >= lowest) & (place <= highest)


def end_rows(x):
    return jnp.concatenate([x[:HMAX], x[x.shape[0] - HMAX :]], axis=0)


def wall_block(g, own_ref, height_ref, inv_ref, stack, acc_ref, part_ref):
    rows = g[0].shape[0]
    width = 2 * LANES
    height = jnp.concatenate([height_ref[...], height_ref[...]], axis=1)
    mask = own_ref[:, : 2 * rows]
    for f in range(FIELDS):
        hi, lo = split2(g[f] * height)
        stack[0:rows, f * width : (f + 1) * width] = hi
        stack[rows:, f * width : (f + 1) * width] = lo
    merged = jnp.dot(mask, stack[...], preferred_element_type=F32)
    for f in range(FIELDS):
        part_ref[f, 0:HMAX, :] = merged[0:HMAX, f * width : (f + 1) * width]
        part_ref[f, HMAX:, :] = merged[rows - HMAX :, f * width : (f + 1) * width]
    for r in range(HMAX, rows - HMAX, HMAX):
        num = acc_ref[0, r : r + HMAX, :]
        den = acc_ref[1, r : r + HMAX, :]
        scale = inv_ref[r : r + HMAX, :]
        for c in range(2):
            parts = [
                merged[r : r + HMAX, f * width + c * LANES : f * width + (c + 1) * LANES] for f in range(FIELDS)
            ]
            num, den = contract(parts, scale, num, den)
        acc_ref[0, r : r + HMAX, :] = num
        acc_ref[1, r : r + HMAX, :] = den


def leaves_early():
    return lax.axis_index("gz") == 0


def inner_work(v_ref, s_ref, pair_ref, fh, fl, inner):
    rows, cells = v_ref.shape[1:]
    for t in range(cells // LANES):
        at = slice(t * LANES, (t + 1) * LANES)
        for r in range(0, rows, 16):
            rr = slice(r, r + 16)

            def put_high(f, x):
                fh[f, rr, at] = x

            def put_low(f, x):
                fl[f, rr, at] = x

            store_fields(
                [v_ref[f, rr, at] for f in range(3)], [s_ref[f, rr, at] for f in range(6)], put_high, put_low
            )
    for n in range(inner.shape[0]):
        g = smooth_pair(n, fh, fl, pair_ref)
        for f in range(FIELDS):
            inner[n, f] = g[f]


def early_kernel(v_ref, s_ref, pair_ref, a, b, c, d, fh, fl, inner, *same):
    @pl.when(leaves_early())
    def _():
        inner_work(v_ref, s_ref, pair_ref, fh, fl, inner)


def late_kernel(v_ref, s_ref, pair_ref, a, b, c, fh, fl, inner):
    @pl.when(jnp.logical_not(leaves_early()))
    def _():
        inner_work(v_ref, s_ref, pair_ref, fh, fl, inner)


def wall_kernel(
    h_ref, reach_ref, inner, acc_ref, part_ref, own_ref, height_ref, inv_ref, mask_ref, total_ref, stack
):
    rows = h_ref.shape[1]
    ends = 2 * HMAX
    reach = pad_lanes(reach_ref[...].astype(F32))
    down = to_column(reach[0:1], rows).astype(jnp.int32)
    up = to_column(reach[1:2], rows).astype(jnp.int32)
    column = lane_iota((rows, 2 * LANES))
    row = lax.broadcasted_iota(jnp.int32, (rows, 2 * LANES), 0)
    place = jnp.where(column < rows, column, column - rows)
    inside = stencil_holds(place, row, down, up, rows)
    own_ref[...] = jnp.where(inside, 1.0, 0.0).astype(BF16)
    heights = pad_lanes(h_ref[...])
    height_ref[...] = jnp.broadcast_to(to_column(heights, rows), (rows, LANES))
    own = inside[:, :LANES] & (column[:, :LANES] < rows)
    total = jnp.sum(jnp.where(own, jnp.broadcast_to(heights, (rows, LANES)), 0.0), axis=1, keepdims=True)
    inv_ref[...] = jnp.broadcast_to(1.0 / total, (rows, LANES))
    total_ref[...] = jnp.broadcast_to(end_rows(total), (ends, LANES))
    column = lane_iota((ends, LANES))
    row = lax.broadcasted_iota(jnp.int32, (ends, LANES), 0)
    turn = column & (ends - 1)
    place = jnp.where(turn < HMAX, turn - HMAX, turn - HMAX + rows)
    row = jnp.where(row < HMAX, row, row + rows - ends)
    inside = stencil_holds(place, row, end_rows(down), end_rows(up), rows) & (column < 2 * ends)
    mask_ref[...] = jnp.where(inside, 1.0, 0.0)
    acc_ref[...] = jnp.zeros_like(acc_ref)
    for n in range(inner.shape[0]):
        g = [inner[n, f] for f in range(FIELDS)]
        wall_block(g, own_ref, height_ref, inv_ref, stack.at[n], acc_ref, part_ref.at[n])


def outer_kernel(
    fh, fl, znear, zfar, ynear, yfar, pair_ref, ends_ref, acc_in, own_ref, height_ref, inv_ref,
    sums_ref, part_ref, hh, hl, halo_inner, eh, el, stack, acc_ref,
):
    rows, cells = fh.shape[1:]
    gz_odd = lax.axis_index("gz") % 2 == 1
    gy_odd = lax.axis_index("gy") % 2 == 1
    acc_ref[...] = acc_in[...]
    edge_fields(jnp.where(gz_odd, znear[...], zfar[...]), jnp.where(gz_odd, zfar[...], znear[...]), eh, el)
    g = smooth_ends(fh, fl, eh, el, ends_ref)
    wall_block(g, own_ref, height_ref, inv_ref, stack, acc_ref, part_ref)
    for t in range(cells // LANES):
        at = slice(t * LANES, (t + 1) * LANES)

        def put_high(f, x):
            hh[f, :, at] = x

        def put_low(f, x):
            hl[f, :, at] = x

        raw = []
        for f in range(9):
            span = slice(f * cells + t * LANES, f * cells + (t + 1) * LANES)
            near, far = ynear[:, span], yfar[:, span]
            raw.append(jnp.concatenate([jnp.where(gy_odd, near, far), jnp.where(gy_odd, far, near)], axis=0))
        store_fields(raw[:3], raw[3:], put_high, put_low)
    for n in range(halo_inner.shape[0]):
        g = smooth_pair(n, hh, hl, pair_ref)
        for f in range(FIELDS):
            halo_inner[n, f] = g[f]
    inv = inv_ref[...]
    for k in range(2):
        plane_sums = jnp.sum(acc_ref[k] * (inv * inv), axis=1, keepdims=True)
        sums_ref[k : k + 1, :] = to_row(plane_sums, lax.broadcasted_iota(jnp.int32, (rows, LANES), 0))


def edge_fields(zl, zr, eh, el):
    rows = zl.shape[0]
    lane = lane_iota((16, LANES))
    middle = LANES // 2
    follows = (lane >= middle - NX) & (lane < middle)
    precedes = (lane >= middle) & (lane < middle + NX)
    for r in range(0, rows, 16):
        rr = slice(r, r + 16)
        raw = [
            jnp.where(
                follows,
                rot(zr[rr], middle - NX - NX * f),
                jnp.where(precedes, rot(zl[rr], middle - NX * f), 0.0),
            )
            for f in range(9)
        ]

        def put_high(f, x):
            eh[f, rr, :] = x

        def put_low(f, x):
            el[f, rr, :] = x

        store_fields(raw[:3], raw[3:], put_high, put_low)


def last_kernel(near_ref, far_ref, sums_in, part_inner, part_ends, mask_ref, total_ref, hh, hl, halo_inner, ends_ref, out_ref, eh, el, stack):
    rows = out_ref.shape[2]
    width = 2 * LANES
    gy_odd = lax.axis_index("gy") % 2 == 1
    both_rows = 2 * HMAX

    def halo(at):
        near, far = near_ref[:, at], far_ref[:, at]
        return jnp.concatenate([jnp.where(gy_odd, near, far), jnp.where(gy_odd, far, near)], axis=0)

    zl = halo(slice(0, LANES))
    zr = halo(slice(LANES, 2 * LANES))
    below = rot(zl[:HMAX], -9 * NX)[0:1]
    above = rot(zl[HMAX:], -9 * NX)[0:1]
    height = jnp.concatenate([to_column(below, HMAX), to_column(above, HMAX)], axis=0)
    lane = lane_iota((both_rows, LANES))
    heights = jnp.where(lane[0:1] < HMAX, below, rot(above, HMAX))
    outside = jnp.where(lane < both_rows, mask_ref[...] * heights, 0.0)
    inv = 1.0 / (total_ref[...] + jnp.sum(outside, axis=1, keepdims=True))
    scale = [inv[:HMAX], inv[HMAX:]]
    mask = mask_ref[:, : 2 * both_rows].astype(BF16)

    edge_fields(zl, zr, eh, el)
    zero = jnp.zeros((HMAX, LANES), F32)
    sums = [[zero, zero], [zero, zero]]
    blocks = halo_inner.shape[0]
    for n in range(blocks + 1):
        if n < blocks:
            g = [halo_inner[n, f] for f in range(FIELDS)]
            part = part_inner.at[n]
        else:
            part = part_ends
            g = smooth_ends(hh, hl, eh, el, ends_ref)
        for f in range(FIELDS):
            hi, lo = split2(g[f] * height)
            stack[n, 0:both_rows, f * width : (f + 1) * width] = hi
            stack[n, both_rows:, f * width : (f + 1) * width] = lo
        merged = jnp.dot(mask, stack[n], preferred_element_type=F32)
        for i in range(2):
            rr = slice(i * HMAX, (i + 1) * HMAX)
            for c in range(2):
                at = slice(c * LANES, (c + 1) * LANES)
                values = [
                    part[f, rr, at] + merged[rr, f * width + c * LANES : f * width + (c + 1) * LANES]
                    for f in range(FIELDS)
                ]
                sums[i] = list(contract(values, scale[i], *sums[i]))
    row = lax.broadcasted_iota(jnp.int32, (both_rows, LANES), 0)
    row = jnp.where(row < HMAX, row, row + rows - both_rows)
    for k in range(2):
        values = jnp.concatenate([sums[0][k], sums[1][k]], axis=0) * (inv * inv)
        total = sums_in[k : k + 1, :] + to_row(jnp.sum(values, axis=1, keepdims=True), row)
        out_ref[:, k : k + 1, :] = jnp.broadcast_to(total[None, :, :rows], (out_ref.shape[0], 1, rows))


def call(kernel, out_shape, scratch, limit, *operands, aliases=None):
    vmem = pl.BlockSpec(memory_space=pltpu.VMEM)
    return pl.pallas_call(
        kernel,
        in_specs=[vmem] * len(operands),
        out_specs=jax.tree.map(lambda _: vmem, out_shape),
        out_shape=out_shape,
        scratch_shapes=scratch,
        input_output_aliases=aliases or {},
        compiler_params=pltpu.CompilerParams(vmem_limit_bytes=limit),
        cost_estimate=pl.CostEstimate(flops=4 * 10**9, bytes_accessed=2**20, transcendentals=0),
    )(*operands)


def local(velocity, strain, cell_height, stencil_reach):
    rows, cells = velocity.shape[1:]
    width = 2 * LANES
    blocks = cells // width - 1
    ends = 2 * HMAX
    shape = jax.ShapeDtypeStruct
    heights = cell_height.reshape(1, rows)
    near, far, wall_near, wall_far, velocity, strain, pair, both_ends = first_call(velocity, strain)
    own_work = [
        shape((FIELDS, rows, cells), BF16),
        shape((WIDE, rows, cells), BF16),
        shape((blocks, FIELDS, rows, width), F32),
    ]
    messages = (near, far, wall_near, wall_far)
    fh, fl, inner, near, far, wall_near, wall_far = call(
        early_kernel,
        own_work + [shape(x.shape, x.dtype) for x in messages],
        [],
        LARGE_VMEM,
        velocity,
        strain,
        pair,
        *messages,
        aliases={3 + i: 3 + i for i in range(4)},
    )
    znear = lax.ppermute(near, "gz", near_pairs("gz"))
    zfar = lax.ppermute(far, "gz", far_pairs("gz", True))
    yfar = lax.ppermute(wall_far, "gy", far_pairs("gy", False))
    ynear = lax.ppermute(wall_near, "gy", near_pairs("gy"))
    fh, fl, inner = call(
        late_kernel,
        own_work,
        [],
        LARGE_VMEM,
        velocity,
        strain,
        pair,
        fh,
        fl,
        inner,
        aliases={3 + i: i for i in range(3)},
    )
    acc, part_inner, own, height, inv, mask, totals = call(
        wall_kernel,
        [
            shape((2, rows, LANES), F32),
            shape((blocks, FIELDS, ends, width), F32),
            shape((rows, width), BF16),
            shape((rows, LANES), F32),
            shape((rows, LANES), F32),
            shape((ends, LANES), F32),
            shape((ends, LANES), F32),
        ],
        [pltpu.VMEM((blocks, 2 * rows, FIELDS * width), BF16)],
        LARGE_VMEM,
        heights,
        stencil_reach,
        inner,
    )
    near, far = corner_call(heights, znear, zfar)
    corner_far = lax.ppermute(far, "gy", far_pairs("gy", False))
    corner_near = lax.ppermute(near, "gy", near_pairs("gy"))
    sums, part_ends, hh, hl, halo_inner = call(
        outer_kernel,
        [
            shape((2, LANES), F32),
            shape((FIELDS, ends, width), F32),
            shape((FIELDS, ends, cells), BF16),
            shape((WIDE, ends, cells), BF16),
            shape((blocks, FIELDS, ends, width), F32),
        ],
        [
            pltpu.VMEM((FIELDS, rows, LANES), BF16),
            pltpu.VMEM((WIDE, rows, LANES), BF16),
            pltpu.VMEM((2 * rows, FIELDS * width), BF16),
            pltpu.VMEM((2, rows, LANES), F32),
        ],
        LARGE_VMEM,
        fh,
        fl,
        znear,
        zfar,
        ynear,
        yfar,
        pair,
        both_ends,
        acc,
        own,
        height,
        inv,
    )
    sums = call(
        last_kernel,
        shape((lax.axis_size("gz"), 2, rows), F32),
        [
            pltpu.VMEM((FIELDS, ends, LANES), BF16),
            pltpu.VMEM((WIDE, ends, LANES), BF16),
            pltpu.VMEM((blocks + 1, 2 * ends, FIELDS * width), BF16),
        ],
        LARGE_VMEM,
        corner_near,
        corner_far,
        sums,
        part_inner,
        part_ends,
        mask,
        totals,
        hh,
        hl,
        halo_inner,
        both_ends,
    )
    sums = jnp.sum(lax.all_to_all(sums, "gz", 0, 0), axis=0)
    total = lax.axis_size("gz") * cells
    return sums[0] / total / (sums[1] / total + 1e-06)


def near_pairs(axis):
    return [(i, i ^ 1) for i in range(lax.axis_size(axis))]


def far_pairs(axis, closed):
    n = lax.axis_size(axis)
    pairs = []
    for i in range(1, n if closed else n - 1, 2):
        pairs += [(i, (i + 1) % n), ((i + 1) % n, i)]
    return pairs


def solution(mesh):
    in_specs = (P(None, "gy", "gz"), P(None, "gy", "gz"), P("gy"), P(None, "gy"))
    return jax.shard_map(local, mesh=mesh, in_specs=in_specs, out_specs=P("gy"), check_vma=False)
```

```python
import jax
import jax.numpy as jnp
from jax import lax
from jax.experimental import pallas as pl
from jax.experimental.pallas import tpu as pltpu
from jax.sharding import PartitionSpec as P

NX = 8
HMAX = 8
LANES = 128
FIELDS = 21
WIDE = 15
FIRST_VMEM = 51 * 1024 * 1024
SMALL_VMEM = 24 * 1024 * 1024
LARGE_VMEM = 24 * 1024 * 1024
LEAD_INDEX = (0, 1, 2, 0, 0, 1)
TAIL_INDEX = (0, 1, 2, 1, 2, 2)
TENSOR_WEIGHTS = (1.0, 1.0, 1.0, 2.0, 2.0, 2.0)
F32 = jnp.float32
BF16 = jnp.bfloat16


def strain_rate(s):
    squares = 2.0 * (s[0] * s[0] + s[1] * s[1] + s[2] * s[2])
    squares = squares + 4.0 * (s[3] * s[3] + s[4] * s[4] + s[5] * s[5])
    return jnp.sqrt(squares)


def lane_iota(shape):
    return lax.broadcasted_iota(jnp.int32, shape, len(shape) - 1)


def rot(x, amount):
    amount = amount % LANES
    return pltpu.roll(x, amount, x.ndim - 1) if amount else x


def cell_weights(source, target):
    turn = (source - target) & (NX - 1)
    along = jnp.where(turn == 0, 0.5, jnp.where((turn == 1) | (turn == NX - 1), 0.25, 0.0))
    step = ((source + LANES) >> 3) - ((target + LANES) >> 3)
    across = jnp.where(step == 0, 0.5, jnp.where((step == 1) | (step == -1), 0.25, 0.0))
    return along * across


def pair_filter():
    shape = (3 * LANES, 2 * LANES)
    k = lax.broadcasted_iota(jnp.int32, shape, 0)
    return cell_weights(jnp.where(k < 5 * LANES // 2, k, k - 3 * LANES), lane_iota(shape)).astype(BF16)


def ends_filter():
    shape = (3 * LANES, 2 * LANES)
    k = lax.broadcasted_iota(jnp.int32, shape, 0)
    m = lane_iota(shape)
    place = k & (LANES - 1)
    middle = LANES // 2
    outer = k >= 2 * LANES
    last = place >= LANES - NX
    after = (place >= middle - NX) & (place < middle)
    before = (place >= middle) & (place < middle + NX)
    used = (place < NX) | last | after | before
    shift = jnp.where(last, -LANES, jnp.where(after, LANES - middle + NX, jnp.where(before, -middle - NX, LANES)))
    source = jnp.where(outer, place + shift, place)
    tile = jnp.where(outer, jnp.where(last | after, 1, 0), k >> 7)
    fits = (tile == (m >> 7)) & (used | (k < 2 * LANES))
    return jnp.where(fits, cell_weights(source, m & (LANES - 1)), 0.0).astype(BF16)


def first_kernel(v_ref, s_ref, near_ref, far_ref, wall_near, wall_far, v_out, s_out, pair_ref, ends_ref, sems):
    rows, cells = v_ref.shape[1:]
    spans = ((0, LANES), (cells - LANES, LANES), (LANES, cells - 2 * LANES))
    copies = []
    for i, (start, size) in enumerate(spans):
        for j, (ref, out) in enumerate(((v_ref, v_out), (s_ref, s_out))):
            at = pl.ds(start, size)
            copies.append(pltpu.make_async_copy(ref.at[:, :, at], out.at[:, :, at], sems.at[i, j]))
    for copy in copies:
        copy.start()
    pair_ref[...] = pair_filter()
    ends_ref[...] = ends_filter()
    for copy in copies[:4]:
        copy.wait()
    lane = lane_iota((rows, LANES))
    left = jnp.zeros((rows, LANES), F32)
    right = jnp.zeros((rows, LANES), F32)
    for f in range(9):
        ref, at = (v_out, f) if f < 3 else (s_out, f - 3)
        here = (lane >= NX * f) & (lane < NX * (f + 1))
        left = jnp.where(here, rot(ref[at, :, :LANES].astype(F32), NX * f), left)
        right = jnp.where(here, rot(ref[at, :, cells - LANES :].astype(F32), NX * f + NX), right)
    odd = lax.axis_index("gz") % 2 == 1
    near_ref[...] = jnp.where(odd, left, right)
    far_ref[...] = jnp.where(odd, right, left)
    for copy in copies[4:]:
        copy.wait()
    gy_odd = lax.axis_index("gy") % 2 == 1
    for f in range(9):
        at = slice(f * cells, (f + 1) * cells)
        if f < 3:
            low, high = v_out[f, :HMAX, :], v_out[f, rows - HMAX :, :]
        else:
            low = s_out[f - 3, : 2 * HMAX, :].astype(F32)[:HMAX]
            high = s_out[f - 3, rows - 2 * HMAX :, :].astype(F32)[HMAX:]
        wall_near[:, at] = jnp.where(gy_odd, low, high)
        wall_far[:, at] = jnp.where(gy_odd, high, low)


def first_call(velocity, strain):
    rows, cells = velocity.shape[1:]
    hbm = pl.BlockSpec(memory_space=pltpu.HBM)
    vmem = pl.BlockSpec(memory_space=pltpu.VMEM)
    shape = jax.ShapeDtypeStruct
    return pl.pallas_call(
        first_kernel,
        in_specs=[hbm] * 2,
        out_specs=[vmem] * 8,
        out_shape=[shape((rows, LANES), F32)] * 2
        + [shape((HMAX, 9 * cells), F32)] * 2
        + [shape(x.shape, x.dtype) for x in (velocity, strain)]
        + [shape((3 * LANES, 2 * LANES), BF16)] * 2,
        scratch_shapes=[pltpu.SemaphoreType.DMA((3, 2))],
        compiler_params=pltpu.CompilerParams(vmem_limit_bytes=FIRST_VMEM),
    )(velocity, strain)


def corner_kernel(h_ref, zfar, znear, near_ref, far_ref):
    rows = znear.shape[0]
    gz_odd = lax.axis_index("gz") % 2 == 1
    gy_odd = lax.axis_index("gy") % 2 == 1
    lane = lane_iota((HMAX, LANES))
    row = lax.broadcasted_iota(jnp.int32, (HMAX, LANES), 0)
    stamp = (row == 0) & (lane >= 9 * NX) & (lane < 10 * NX)
    heights = jnp.broadcast_to(jnp.pad(h_ref[...], ((0, 0), (0, LANES - rows))), (HMAX, LANES))
    sides = []
    for r0 in (0, rows - HMAX):
        zn = znear[r0 : r0 + HMAX, :]
        zf = zfar[r0 : r0 + HMAX, :]
        zl = jnp.where(stamp, rot(heights, 9 * NX - r0), jnp.where(gz_odd, zn, zf))
        sides.append((zl, jnp.where(gz_odd, zf, zn)))
    (low_left, low_right), (high_left, high_right) = sides
    near_ref[:, :LANES] = jnp.where(gy_odd, low_left, high_left)
    near_ref[:, LANES:] = jnp.where(gy_odd, low_right, high_right)
    far_ref[:, :LANES] = jnp.where(gy_odd, high_left, low_left)
    far_ref[:, LANES:] = jnp.where(gy_odd, high_right, low_right)


def corner_call(heights, zfar, znear):
    vmem = pl.BlockSpec(memory_space=pltpu.VMEM)
    return pl.pallas_call(
        corner_kernel,
        in_specs=[vmem] * 3,
        out_specs=[vmem] * 2,
        out_shape=[jax.ShapeDtypeStruct((HMAX, 2 * LANES), F32)] * 2,
        compiler_params=pltpu.CompilerParams(vmem_limit_bytes=SMALL_VMEM),
    )(heights, zfar, znear)


def split2(x):
    hi = x.astype(BF16)
    return hi, (x - hi.astype(F32)).astype(BF16)


def store_fields(u, s, put_high, put_low):
    tensor = [x.astype(F32) for x in s]
    rate = strain_rate(tensor)
    wide = u + [u[a] * u[b] for a, b in zip(LEAD_INDEX, TAIL_INDEX)] + [rate * x for x in tensor]
    for f, value in enumerate(wide):
        hi, lo = split2(value)
        put_high(f, hi)
        put_low(f, lo)
    for f, value in enumerate(s):
        put_high(WIDE + f, value.astype(BF16))


def smooth(rows, operand, matrix_ref):
    wide, narrow = slice(0, WIDE), slice(WIDE, FIELDS)
    lhs = jnp.concatenate([operand(True, wide), operand(False, wide)], axis=-1).reshape(WIDE * rows, -1)
    matrix = matrix_ref[...]
    first = jnp.dot(lhs, jnp.concatenate([matrix, matrix], axis=0), preferred_element_type=F32)
    lhs = operand(True, narrow).reshape((FIELDS - WIDE) * rows, -1)
    second = jnp.dot(lhs, matrix, preferred_element_type=F32)
    return [first[f * rows : (f + 1) * rows] for f in range(WIDE)] + [
        second[f * rows : (f + 1) * rows] for f in range(FIELDS - WIDE)
    ]


def pick(after, before):
    return jnp.where(lane_iota(after.shape) < LANES // 2, after, before)


def smooth_pair(n, fh, fl, pair_ref):
    def operand(high, fields):
        ref = fh if high else fl
        tile = [ref[fields, :, (2 * n + i) * LANES : (2 * n + i + 1) * LANES] for i in range(4)]
        return jnp.concatenate([tile[1], tile[2], pick(tile[3], tile[0])], axis=-1)

    return smooth(fh.shape[1], operand, pair_ref)


def smooth_ends(fh, fl, eh, el, ends_ref):
    cells = fh.shape[2]

    def operand(high, fields):
        ref, outer = (fh, eh) if high else (fl, el)
        second = ref[fields, :, LANES : 2 * LANES]
        ahead = ref[fields, :, cells - 2 * LANES : cells - LANES]
        lane = lane_iota(second.shape)
        edge = jnp.where(lane < NX, second, jnp.where(lane >= LANES - NX, ahead, outer[fields]))
        return jnp.concatenate([ref[fields, :, :LANES], ref[fields, :, cells - LANES :], edge], axis=-1)

    return smooth(fh.shape[1], operand, ends_ref)


def contract(g, inv, num, den):
    u, p, m, s = g[0:3], g[3:9], g[9:15], g[15:21]
    rate = 4.0 * inv * strain_rate(s)
    scaled = [inv * x for x in u]
    for k in range(6):
        leonard = p[k] - scaled[LEAD_INDEX[k]] * u[TAIL_INDEX[k]]
        model = m[k] - rate * s[k]
        weighted = TENSOR_WEIGHTS[k] * model
        num = num + weighted * leonard
        den = den + weighted * model
    return num, den


def to_column(row_vector, size):
    shape = (size, LANES)
    eye = lax.broadcasted_iota(jnp.int32, shape, 0) == lane_iota(shape)
    return jnp.sum(jnp.where(eye, jnp.broadcast_to(row_vector, shape), 0.0), axis=1, keepdims=True)


def to_row(column_vector, row):
    return jnp.sum(jnp.where(row == lane_iota(row.shape), column_vector, 0.0), axis=0, keepdims=True)


def pad_lanes(x):
    return jnp.pad(x, ((0, 0), (0, LANES - x.shape[1])))


def stencil_holds(place, row, down, up, rows):
    gy = lax.axis_index("gy")
    lowest = jnp.maximum(row - down, -gy * rows)
    highest = jnp.minimum(row + up, (lax.axis_size("gy") - gy) * rows - 1)
    return (place >= lowest) & (place <= highest)


def end_rows(x):
    return jnp.concatenate([x[:HMAX], x[x.shape[0] - HMAX :]], axis=0)


def wall_block(g, own_ref, height_ref, inv_ref, stack, acc_ref, part_ref):
    rows = g[0].shape[0]
    width = 2 * LANES
    height = jnp.concatenate([height_ref[...], height_ref[...]], axis=1)
    mask = own_ref[:, : 2 * rows]
    for f in range(FIELDS):
        hi, lo = split2(g[f] * height)
        stack[0:rows, f * width : (f + 1) * width] = hi
        stack[rows:, f * width : (f + 1) * width] = lo
    merged = jnp.dot(mask, stack[...], preferred_element_type=F32)
    for f in range(FIELDS):
        part_ref[f, 0:HMAX, :] = merged[0:HMAX, f * width : (f + 1) * width]
        part_ref[f, HMAX:, :] = merged[rows - HMAX :, f * width : (f + 1) * width]
    for r in range(HMAX, rows - HMAX, HMAX):
        num = acc_ref[0, r : r + HMAX, :]
        den = acc_ref[1, r : r + HMAX, :]
        scale = inv_ref[r : r + HMAX, :]
        for c in range(2):
            parts = [
                merged[r : r + HMAX, f * width + c * LANES : f * width + (c + 1) * LANES] for f in range(FIELDS)
            ]
            num, den = contract(parts, scale, num, den)
        acc_ref[0, r : r + HMAX, :] = num
        acc_ref[1, r : r + HMAX, :] = den


def leaves_early():
    return lax.axis_index("gz") == 0


def inner_work(v_ref, s_ref, pair_ref, fh, fl, inner):
    rows, cells = v_ref.shape[1:]
    for t in range(cells // LANES):
        at = slice(t * LANES, (t + 1) * LANES)
        for r in range(0, rows, 16):
            rr = slice(r, r + 16)

            def put_high(f, x):
                fh[f, rr, at] = x

            def put_low(f, x):
                fl[f, rr, at] = x

            store_fields(
                [v_ref[f, rr, at] for f in range(3)], [s_ref[f, rr, at] for f in range(6)], put_high, put_low
            )
    for n in range(inner.shape[0]):
        g = smooth_pair(n, fh, fl, pair_ref)
        for f in range(FIELDS):
            inner[n, f] = g[f]


def early_kernel(v_ref, s_ref, pair_ref, a, b, c, d, fh, fl, inner, *same):
    @pl.when(leaves_early())
    def _():
        inner_work(v_ref, s_ref, pair_ref, fh, fl, inner)


def late_kernel(v_ref, s_ref, pair_ref, a, b, c, fh, fl, inner):
    @pl.when(jnp.logical_not(leaves_early()))
    def _():
        inner_work(v_ref, s_ref, pair_ref, fh, fl, inner)


def wall_kernel(
    h_ref, reach_ref, inner, acc_ref, part_ref, own_ref, height_ref, inv_ref, mask_ref, total_ref, stack
):
    rows = h_ref.shape[1]
    ends = 2 * HMAX
    reach = pad_lanes(reach_ref[...].astype(F32))
    down = to_column(reach[0:1], rows).astype(jnp.int32)
    up = to_column(reach[1:2], rows).astype(jnp.int32)
    column = lane_iota((rows, 2 * LANES))
    row = lax.broadcasted_iota(jnp.int32, (rows, 2 * LANES), 0)
    place = jnp.where(column < rows, column, column - rows)
    inside = stencil_holds(place, row, down, up, rows)
    own_ref[...] = jnp.where(inside, 1.0, 0.0).astype(BF16)
    heights = pad_lanes(h_ref[...])
    height_ref[...] = jnp.broadcast_to(to_column(heights, rows), (rows, LANES))
    own = inside[:, :LANES] & (column[:, :LANES] < rows)
    total = jnp.sum(jnp.where(own, jnp.broadcast_to(heights, (rows, LANES)), 0.0), axis=1, keepdims=True)
    inv_ref[...] = jnp.broadcast_to(1.0 / total, (rows, LANES))
    total_ref[...] = jnp.broadcast_to(end_rows(total), (ends, LANES))
    column = lane_iota((ends, LANES))
    row = lax.broadcasted_iota(jnp.int32, (ends, LANES), 0)
    turn = column & (ends - 1)
    place = jnp.where(turn < HMAX, turn - HMAX, turn - HMAX + rows)
    row = jnp.where(row < HMAX, row, row + rows - ends)
    inside = stencil_holds(place, row, end_rows(down), end_rows(up), rows) & (column < 2 * ends)
    mask_ref[...] = jnp.where(inside, 1.0, 0.0)
    acc_ref[...] = jnp.zeros_like(acc_ref)
    for n in range(inner.shape[0]):
        g = [inner[n, f] for f in range(FIELDS)]
        wall_block(g, own_ref, height_ref, inv_ref, stack.at[n], acc_ref, part_ref.at[n])


def outer_kernel(
    fh, fl, zfar, znear, ynear, yfar, pair_ref, ends_ref, acc_in, own_ref, height_ref, inv_ref,
    sums_ref, part_ref, hh, hl, halo_inner, eh, el, stack, acc_ref,
):
    rows, cells = fh.shape[1:]
    gz_odd = lax.axis_index("gz") % 2 == 1
    gy_odd = lax.axis_index("gy") % 2 == 1
    acc_ref[...] = acc_in[...]
    edge_fields(jnp.where(gz_odd, znear[...], zfar[...]), jnp.where(gz_odd, zfar[...], znear[...]), eh, el)
    g = smooth_ends(fh, fl, eh, el, ends_ref)
    wall_block(g, own_ref, height_ref, inv_ref, stack, acc_ref, part_ref)
    for t in range(cells // LANES):
        at = slice(t * LANES, (t + 1) * LANES)

        def put_high(f, x):
            hh[f, :, at] = x

        def put_low(f, x):
            hl[f, :, at] = x

        raw = []
        for f in range(9):
            span = slice(f * cells + t * LANES, f * cells + (t + 1) * LANES)
            near, far = ynear[:, span], yfar[:, span]
            raw.append(jnp.concatenate([jnp.where(gy_odd, near, far), jnp.where(gy_odd, far, near)], axis=0))
        store_fields(raw[:3], raw[3:], put_high, put_low)
    for n in range(halo_inner.shape[0]):
        g = smooth_pair(n, hh, hl, pair_ref)
        for f in range(FIELDS):
            halo_inner[n, f] = g[f]
    inv = inv_ref[...]
    for k in range(2):
        plane_sums = jnp.sum(acc_ref[k] * (inv * inv), axis=1, keepdims=True)
        sums_ref[k : k + 1, :] = to_row(plane_sums, lax.broadcasted_iota(jnp.int32, (rows, LANES), 0))


def edge_fields(zl, zr, eh, el):
    rows = zl.shape[0]
    lane = lane_iota((16, LANES))
    middle = LANES // 2
    follows = (lane >= middle - NX) & (lane < middle)
    precedes = (lane >= middle) & (lane < middle + NX)
    for r in range(0, rows, 16):
        rr = slice(r, r + 16)
        raw = [
            jnp.where(
                follows,
                rot(zr[rr], middle - NX - NX * f),
                jnp.where(precedes, rot(zl[rr], middle - NX * f), 0.0),
            )
            for f in range(9)
        ]

        def put_high(f, x):
            eh[f, rr, :] = x

        def put_low(f, x):
            el[f, rr, :] = x

        store_fields(raw[:3], raw[3:], put_high, put_low)


def last_kernel(near_ref, far_ref, sums_in, part_inner, part_ends, mask_ref, total_ref, hh, hl, halo_inner, ends_ref, out_ref, eh, el, stack):
    rows = out_ref.shape[2]
    width = 2 * LANES
    gy_odd = lax.axis_index("gy") % 2 == 1
    both_rows = 2 * HMAX

    def halo(at):
        near, far = near_ref[:, at], far_ref[:, at]
        return jnp.concatenate([jnp.where(gy_odd, near, far), jnp.where(gy_odd, far, near)], axis=0)

    zl = halo(slice(0, LANES))
    zr = halo(slice(LANES, 2 * LANES))
    below = rot(zl[:HMAX], -9 * NX)[0:1]
    above = rot(zl[HMAX:], -9 * NX)[0:1]
    height = jnp.concatenate([to_column(below, HMAX), to_column(above, HMAX)], axis=0)
    lane = lane_iota((both_rows, LANES))
    heights = jnp.where(lane[0:1] < HMAX, below, rot(above, HMAX))
    outside = jnp.where(lane < both_rows, mask_ref[...] * heights, 0.0)
    inv = 1.0 / (total_ref[...] + jnp.sum(outside, axis=1, keepdims=True))
    scale = [inv[:HMAX], inv[HMAX:]]
    mask = mask_ref[:, : 2 * both_rows].astype(BF16)

    edge_fields(zl, zr, eh, el)
    zero = jnp.zeros((HMAX, LANES), F32)
    sums = [[zero, zero], [zero, zero]]
    blocks = halo_inner.shape[0]
    for n in range(blocks + 1):
        if n < blocks:
            g = [halo_inner[n, f] for f in range(FIELDS)]
            part = part_inner.at[n]
        else:
            part = part_ends
            g = smooth_ends(hh, hl, eh, el, ends_ref)
        for f in range(FIELDS):
            hi, lo = split2(g[f] * height)
            stack[n, 0:both_rows, f * width : (f + 1) * width] = hi
            stack[n, both_rows:, f * width : (f + 1) * width] = lo
        merged = jnp.dot(mask, stack[n], preferred_element_type=F32)
        for i in range(2):
            rr = slice(i * HMAX, (i + 1) * HMAX)
            for c in range(2):
                at = slice(c * LANES, (c + 1) * LANES)
                values = [
                    part[f, rr, at] + merged[rr, f * width + c * LANES : f * width + (c + 1) * LANES]
                    for f in range(FIELDS)
                ]
                sums[i] = list(contract(values, scale[i], *sums[i]))
    row = lax.broadcasted_iota(jnp.int32, (both_rows, LANES), 0)
    row = jnp.where(row < HMAX, row, row + rows - both_rows)
    for k in range(2):
        values = jnp.concatenate([sums[0][k], sums[1][k]], axis=0) * (inv * inv)
        total = sums_in[k : k + 1, :] + to_row(jnp.sum(values, axis=1, keepdims=True), row)
        out_ref[:, k : k + 1, :] = jnp.broadcast_to(total[None, :, :rows], (out_ref.shape[0], 1, rows))


def call(kernel, out_shape, scratch, limit, *operands, aliases=None):
    vmem = pl.BlockSpec(memory_space=pltpu.VMEM)
    return pl.pallas_call(
        kernel,
        in_specs=[vmem] * len(operands),
        out_specs=jax.tree.map(lambda _: vmem, out_shape),
        out_shape=out_shape,
        scratch_shapes=scratch,
        input_output_aliases=aliases or {},
        compiler_params=pltpu.CompilerParams(vmem_limit_bytes=limit),
        cost_estimate=pl.CostEstimate(flops=4 * 10**9, bytes_accessed=2**20, transcendentals=0),
    )(*operands)


def local(velocity, strain, cell_height, stencil_reach):
    rows, cells = velocity.shape[1:]
    width = 2 * LANES
    blocks = cells // width - 1
    ends = 2 * HMAX
    shape = jax.ShapeDtypeStruct
    heights = cell_height.reshape(1, rows)
    near, far, wall_near, wall_far, velocity, strain, pair, both_ends = first_call(velocity, strain)
    own_work = [
        shape((FIELDS, rows, cells), BF16),
        shape((WIDE, rows, cells), BF16),
        shape((blocks, FIELDS, rows, width), F32),
    ]
    messages = (near, far, wall_near, wall_far)
    fh, fl, inner, near, far, wall_near, wall_far = call(
        early_kernel,
        own_work + [shape(x.shape, x.dtype) for x in messages],
        [],
        LARGE_VMEM,
        velocity,
        strain,
        pair,
        *messages,
        aliases={3 + i: 3 + i for i in range(4)},
    )
    znear = lax.ppermute(near, "gz", near_pairs("gz"))
    zfar = lax.ppermute(far, "gz", far_pairs("gz", True))
    yfar = lax.ppermute(wall_far, "gy", far_pairs("gy", False))
    ynear = lax.ppermute(wall_near, "gy", near_pairs("gy"))
    fh, fl, inner = call(
        late_kernel,
        own_work,
        [],
        LARGE_VMEM,
        velocity,
        strain,
        pair,
        fh,
        fl,
        inner,
        aliases={3 + i: i for i in range(3)},
    )
    acc, part_inner, own, height, inv, mask, totals = call(
        wall_kernel,
        [
            shape((2, rows, LANES), F32),
            shape((blocks, FIELDS, ends, width), F32),
            shape((rows, width), BF16),
            shape((rows, LANES), F32),
            shape((rows, LANES), F32),
            shape((ends, LANES), F32),
            shape((ends, LANES), F32),
        ],
        [pltpu.VMEM((blocks, 2 * rows, FIELDS * width), BF16)],
        LARGE_VMEM,
        heights,
        stencil_reach,
        inner,
    )
    near, far = corner_call(heights, zfar, znear)
    corner_far = lax.ppermute(far, "gy", far_pairs("gy", False))
    corner_near = lax.ppermute(near, "gy", near_pairs("gy"))
    sums, part_ends, hh, hl, halo_inner = call(
        outer_kernel,
        [
            shape((2, LANES), F32),
            shape((FIELDS, ends, width), F32),
            shape((FIELDS, ends, cells), BF16),
            shape((WIDE, ends, cells), BF16),
            shape((blocks, FIELDS, ends, width), F32),
        ],
        [
            pltpu.VMEM((FIELDS, rows, LANES), BF16),
            pltpu.VMEM((WIDE, rows, LANES), BF16),
            pltpu.VMEM((2 * rows, FIELDS * width), BF16),
            pltpu.VMEM((2, rows, LANES), F32),
        ],
        LARGE_VMEM,
        fh,
        fl,
        zfar,
        znear,
        ynear,
        yfar,
        pair,
        both_ends,
        acc,
        own,
        height,
        inv,
    )
    sums = call(
        last_kernel,
        shape((lax.axis_size("gz"), 2, rows), F32),
        [
            pltpu.VMEM((FIELDS, ends, LANES), BF16),
            pltpu.VMEM((WIDE, ends, LANES), BF16),
            pltpu.VMEM((blocks + 1, 2 * ends, FIELDS * width), BF16),
        ],
        LARGE_VMEM,
        corner_near,
        corner_far,
        sums,
        part_inner,
        part_ends,
        mask,
        totals,
        hh,
        hl,
        halo_inner,
        both_ends,
    )
    sums = jnp.sum(lax.all_to_all(sums, "gz", 0, 0), axis=0)
    total = lax.axis_size("gz") * cells
    return sums[0] / total / (sums[1] / total + 1e-06)


def near_pairs(axis):
    return [(i, i ^ 1) for i in range(lax.axis_size(axis))]


def far_pairs(axis, closed):
    n = lax.axis_size(axis)
    pairs = []
    for i in range(1, n if closed else n - 1, 2):
        pairs += [(i, (i + 1) % n), ((i + 1) % n, i)]
    return pairs


def solution(mesh):
    in_specs = (P(None, "gy", "gz"), P(None, "gy", "gz"), P("gy"), P(None, "gy"))
    return jax.shard_map(local, mesh=mesh, in_specs=in_specs, out_specs=P("gy"), check_vma=False)
```

```python
import jax
import jax.numpy as jnp
from jax import lax
from jax.experimental import pallas as pl
from jax.experimental.pallas import tpu as pltpu
from jax.sharding import PartitionSpec as P

NX = 8
HMAX = 8
LANES = 128
FIELDS = 21
WIDE = 15
FIRST_VMEM = 51 * 1024 * 1024
SMALL_VMEM = 24 * 1024 * 1024
LARGE_VMEM = 24 * 1024 * 1024
LEAD_INDEX = (0, 1, 2, 0, 0, 1)
TAIL_INDEX = (0, 1, 2, 1, 2, 2)
TENSOR_WEIGHTS = (1.0, 1.0, 1.0, 2.0, 2.0, 2.0)
F32 = jnp.float32
BF16 = jnp.bfloat16


def strain_rate(s):
    squares = 2.0 * (s[0] * s[0] + s[1] * s[1] + s[2] * s[2])
    squares = squares + 4.0 * (s[3] * s[3] + s[4] * s[4] + s[5] * s[5])
    return jnp.sqrt(squares)


def lane_iota(shape):
    return lax.broadcasted_iota(jnp.int32, shape, len(shape) - 1)


def rot(x, amount):
    amount = amount % LANES
    return pltpu.roll(x, amount, x.ndim - 1) if amount else x


def cell_weights(source, target):
    turn = (source - target) & (NX - 1)
    along = jnp.where(turn == 0, 0.5, jnp.where((turn == 1) | (turn == NX - 1), 0.25, 0.0))
    step = ((source + LANES) >> 3) - ((target + LANES) >> 3)
    across = jnp.where(step == 0, 0.5, jnp.where((step == 1) | (step == -1), 0.25, 0.0))
    return along * across


def pair_filter():
    shape = (3 * LANES, 2 * LANES)
    k = lax.broadcasted_iota(jnp.int32, shape, 0)
    return cell_weights(jnp.where(k < 5 * LANES // 2, k, k - 3 * LANES), lane_iota(shape)).astype(BF16)


def ends_filter():
    shape = (3 * LANES, 2 * LANES)
    k = lax.broadcasted_iota(jnp.int32, shape, 0)
    m = lane_iota(shape)
    place = k & (LANES - 1)
    middle = LANES // 2
    outer = k >= 2 * LANES
    last = place >= LANES - NX
    after = (place >= middle - NX) & (place < middle)
    before = (place >= middle) & (place < middle + NX)
    used = (place < NX) | last | after | before
    shift = jnp.where(last, -LANES, jnp.where(after, LANES - middle + NX, jnp.where(before, -middle - NX, LANES)))
    source = jnp.where(outer, place + shift, place)
    tile = jnp.where(outer, jnp.where(last | after, 1, 0), k >> 7)
    fits = (tile == (m >> 7)) & (used | (k < 2 * LANES))
    return jnp.where(fits, cell_weights(source, m & (LANES - 1)), 0.0).astype(BF16)


def first_kernel(v_ref, s_ref, near_ref, far_ref, wall_near, wall_far, v_out, s_out, pair_ref, ends_ref, sems):
    rows, cells = v_ref.shape[1:]
    spans = ((0, LANES), (cells - LANES, LANES), (LANES, cells - 2 * LANES))
    copies = []
    for i, (start, size) in enumerate(spans):
        for j, (ref, out) in enumerate(((v_ref, v_out), (s_ref, s_out))):
            at = pl.ds(start, size)
            copies.append(pltpu.make_async_copy(ref.at[:, :, at], out.at[:, :, at], sems.at[i, j]))
    for copy in copies:
        copy.start()
    pair_ref[...] = pair_filter()
    ends_ref[...] = ends_filter()
    for copy in copies[:4]:
        copy.wait()
    lane = lane_iota((rows, LANES))
    left = jnp.zeros((rows, LANES), F32)
    right = jnp.zeros((rows, LANES), F32)
    for f in range(9):
        ref, at = (v_out, f) if f < 3 else (s_out, f - 3)
        here = (lane >= NX * f) & (lane < NX * (f + 1))
        left = jnp.where(here, rot(ref[at, :, :LANES].astype(F32), NX * f), left)
        right = jnp.where(here, rot(ref[at, :, cells - LANES :].astype(F32), NX * f + NX), right)
    odd = lax.axis_index("gz") % 2 == 1
    near_ref[...] = jnp.where(odd, left, right)
    far_ref[...] = jnp.where(odd, right, left)
    for copy in copies[4:]:
        copy.wait()
    gy_odd = lax.axis_index("gy") % 2 == 1
    for f in range(9):
        at = slice(f * cells, (f + 1) * cells)
        if f < 3:
            low, high = v_out[f, :HMAX, :], v_out[f, rows - HMAX :, :]
        else:
            low = s_out[f - 3, : 2 * HMAX, :].astype(F32)[:HMAX]
            high = s_out[f - 3, rows - 2 * HMAX :, :].astype(F32)[HMAX:]
        wall_near[:, at] = jnp.where(gy_odd, low, high)
        wall_far[:, at] = jnp.where(gy_odd, high, low)


def first_call(velocity, strain):
    rows, cells = velocity.shape[1:]
    hbm = pl.BlockSpec(memory_space=pltpu.HBM)
    vmem = pl.BlockSpec(memory_space=pltpu.VMEM)
    shape = jax.ShapeDtypeStruct
    return pl.pallas_call(
        first_kernel,
        in_specs=[hbm] * 2,
        out_specs=[vmem] * 8,
        out_shape=[shape((rows, LANES), F32)] * 2
        + [shape((HMAX, 9 * cells), F32)] * 2
        + [shape(x.shape, x.dtype) for x in (velocity, strain)]
        + [shape((3 * LANES, 2 * LANES), BF16)] * 2,
        scratch_shapes=[pltpu.SemaphoreType.DMA((3, 2))],
        compiler_params=pltpu.CompilerParams(vmem_limit_bytes=FIRST_VMEM),
    )(velocity, strain)


def corner_kernel(h_ref, znear, zfar, near_ref, far_ref):
    rows = znear.shape[0]
    gz_odd = lax.axis_index("gz") % 2 == 1
    gy_odd = lax.axis_index("gy") % 2 == 1
    lane = lane_iota((HMAX, LANES))
    row = lax.broadcasted_iota(jnp.int32, (HMAX, LANES), 0)
    stamp = (row == 0) & (lane >= 9 * NX) & (lane < 10 * NX)
    heights = jnp.broadcast_to(jnp.pad(h_ref[...], ((0, 0), (0, LANES - rows))), (HMAX, LANES))
    sides = []
    for r0 in (0, rows - HMAX):
        zn = znear[r0 : r0 + HMAX, :]
        zf = zfar[r0 : r0 + HMAX, :]
        zl = jnp.where(stamp, rot(heights, 9 * NX - r0), jnp.where(gz_odd, zn, zf))
        sides.append((zl, jnp.where(gz_odd, zf, zn)))
    (low_left, low_right), (high_left, high_right) = sides
    near_ref[:, :LANES] = jnp.where(gy_odd, low_left, high_left)
    near_ref[:, LANES:] = jnp.where(gy_odd, low_right, high_right)
    far_ref[:, :LANES] = jnp.where(gy_odd, high_left, low_left)
    far_ref[:, LANES:] = jnp.where(gy_odd, high_right, low_right)


def corner_call(heights, znear, zfar):
    vmem = pl.BlockSpec(memory_space=pltpu.VMEM)
    return pl.pallas_call(
        corner_kernel,
        in_specs=[vmem] * 3,
        out_specs=[vmem] * 2,
        out_shape=[jax.ShapeDtypeStruct((HMAX, 2 * LANES), F32)] * 2,
        compiler_params=pltpu.CompilerParams(vmem_limit_bytes=SMALL_VMEM),
    )(heights, znear, zfar)


def split2(x):
    hi = x.astype(BF16)
    return hi, (x - hi.astype(F32)).astype(BF16)


def store_fields(u, s, put_high, put_low):
    tensor = [x.astype(F32) for x in s]
    rate = strain_rate(tensor)
    wide = u + [u[a] * u[b] for a, b in zip(LEAD_INDEX, TAIL_INDEX)] + [rate * x for x in tensor]
    for f, value in enumerate(wide):
        hi, lo = split2(value)
        put_high(f, hi)
        put_low(f, lo)
    for f, value in enumerate(s):
        put_high(WIDE + f, value.astype(BF16))


def smooth(rows, operand, matrix_ref):
    wide, narrow = slice(0, WIDE), slice(WIDE, FIELDS)
    lhs = jnp.concatenate([operand(True, wide), operand(False, wide)], axis=-1).reshape(WIDE * rows, -1)
    matrix = matrix_ref[...]
    first = jnp.dot(lhs, jnp.concatenate([matrix, matrix], axis=0), preferred_element_type=F32)
    lhs = operand(True, narrow).reshape((FIELDS - WIDE) * rows, -1)
    second = jnp.dot(lhs, matrix, preferred_element_type=F32)
    return [first[f * rows : (f + 1) * rows] for f in range(WIDE)] + [
        second[f * rows : (f + 1) * rows] for f in range(FIELDS - WIDE)
    ]


def pick(after, before):
    return jnp.where(lane_iota(after.shape) < LANES // 2, after, before)


def smooth_pair(n, fh, fl, pair_ref):
    def operand(high, fields):
        ref = fh if high else fl
        tile = [ref[fields, :, (2 * n + i) * LANES : (2 * n + i + 1) * LANES] for i in range(4)]
        return jnp.concatenate([tile[1], tile[2], pick(tile[3], tile[0])], axis=-1)

    return smooth(fh.shape[1], operand, pair_ref)


def smooth_ends(fh, fl, eh, el, ends_ref):
    cells = fh.shape[2]

    def operand(high, fields):
        ref, outer = (fh, eh) if high else (fl, el)
        second = ref[fields, :, LANES : 2 * LANES]
        ahead = ref[fields, :, cells - 2 * LANES : cells - LANES]
        lane = lane_iota(second.shape)
        edge = jnp.where(lane < NX, second, jnp.where(lane >= LANES - NX, ahead, outer[fields]))
        return jnp.concatenate([ref[fields, :, :LANES], ref[fields, :, cells - LANES :], edge], axis=-1)

    return smooth(fh.shape[1], operand, ends_ref)


def contract(g, inv, num, den):
    u, p, m, s = g[0:3], g[3:9], g[9:15], g[15:21]
    rate = 4.0 * inv * strain_rate(s)
    scaled = [inv * x for x in u]
    for k in range(6):
        leonard = p[k] - scaled[LEAD_INDEX[k]] * u[TAIL_INDEX[k]]
        model = m[k] - rate * s[k]
        weighted = TENSOR_WEIGHTS[k] * model
        num = num + weighted * leonard
        den = den + weighted * model
    return num, den


def to_column(row_vector, size):
    shape = (size, LANES)
    eye = lax.broadcasted_iota(jnp.int32, shape, 0) == lane_iota(shape)
    return jnp.sum(jnp.where(eye, jnp.broadcast_to(row_vector, shape), 0.0), axis=1, keepdims=True)


def to_row(column_vector, row):
    return jnp.sum(jnp.where(row == lane_iota(row.shape), column_vector, 0.0), axis=0, keepdims=True)


def pad_lanes(x):
    return jnp.pad(x, ((0, 0), (0, LANES - x.shape[1])))


def stencil_holds(place, row, down, up, rows):
    gy = lax.axis_index("gy")
    lowest = jnp.maximum(row - down, -gy * rows)
    highest = jnp.minimum(row + up, (lax.axis_size("gy") - gy) * rows - 1)
    return (place >= lowest) & (place <= highest)


def end_rows(x):
    return jnp.concatenate([x[:HMAX], x[x.shape[0] - HMAX :]], axis=0)


def wall_block(g, own_ref, height_ref, inv_ref, stack, acc_ref, part_ref):
    rows = g[0].shape[0]
    width = 2 * LANES
    height = jnp.concatenate([height_ref[...], height_ref[...]], axis=1)
    mask = own_ref[:, : 2 * rows]
    for f in range(FIELDS):
        hi, lo = split2(g[f] * height)
        stack[0:rows, f * width : (f + 1) * width] = hi
        stack[rows:, f * width : (f + 1) * width] = lo
    merged = jnp.dot(mask, stack[...], preferred_element_type=F32)
    for f in range(FIELDS):
        part_ref[f, 0:HMAX, :] = merged[0:HMAX, f * width : (f + 1) * width]
        part_ref[f, HMAX:, :] = merged[rows - HMAX :, f * width : (f + 1) * width]
    for r in range(HMAX, rows - HMAX, HMAX):
        num = acc_ref[0, r : r + HMAX, :]
        den = acc_ref[1, r : r + HMAX, :]
        scale = inv_ref[r : r + HMAX, :]
        for c in range(2):
            parts = [
                merged[r : r + HMAX, f * width + c * LANES : f * width + (c + 1) * LANES] for f in range(FIELDS)
            ]
            num, den = contract(parts, scale, num, den)
        acc_ref[0, r : r + HMAX, :] = num
        acc_ref[1, r : r + HMAX, :] = den


def leaves_early():
    return lax.axis_index("gz") == 0


def inner_work(v_ref, s_ref, pair_ref, fh, fl, inner):
    rows, cells = v_ref.shape[1:]
    for t in range(cells // LANES):
        at = slice(t * LANES, (t + 1) * LANES)
        for r in range(0, rows, 16):
            rr = slice(r, r + 16)

            def put_high(f, x):
                fh[f, rr, at] = x

            def put_low(f, x):
                fl[f, rr, at] = x

            store_fields(
                [v_ref[f, rr, at] for f in range(3)], [s_ref[f, rr, at] for f in range(6)], put_high, put_low
            )
    for n in range(inner.shape[0]):
        g = smooth_pair(n, fh, fl, pair_ref)
        for f in range(FIELDS):
            inner[n, f] = g[f]


def early_kernel(v_ref, s_ref, pair_ref, a, b, c, d, fh, fl, inner, *same):
    @pl.when(leaves_early())
    def _():
        inner_work(v_ref, s_ref, pair_ref, fh, fl, inner)


def late_kernel(v_ref, s_ref, pair_ref, a, b, c, fh, fl, inner):
    @pl.when(jnp.logical_not(leaves_early()))
    def _():
        inner_work(v_ref, s_ref, pair_ref, fh, fl, inner)


def wall_kernel(
    h_ref, reach_ref, inner, acc_ref, part_ref, own_ref, height_ref, inv_ref, mask_ref, total_ref, stack
):
    rows = h_ref.shape[1]
    ends = 2 * HMAX
    reach = pad_lanes(reach_ref[...].astype(F32))
    down = to_column(reach[0:1], rows).astype(jnp.int32)
    up = to_column(reach[1:2], rows).astype(jnp.int32)
    column = lane_iota((rows, 2 * LANES))
    row = lax.broadcasted_iota(jnp.int32, (rows, 2 * LANES), 0)
    place = jnp.where(column < rows, column, column - rows)
    inside = stencil_holds(place, row, down, up, rows)
    own_ref[...] = jnp.where(inside, 1.0, 0.0).astype(BF16)
    heights = pad_lanes(h_ref[...])
    height_ref[...] = jnp.broadcast_to(to_column(heights, rows), (rows, LANES))
    own = inside[:, :LANES] & (column[:, :LANES] < rows)
    total = jnp.sum(jnp.where(own, jnp.broadcast_to(heights, (rows, LANES)), 0.0), axis=1, keepdims=True)
    inv_ref[...] = jnp.broadcast_to(1.0 / total, (rows, LANES))
    total_ref[...] = jnp.broadcast_to(end_rows(total), (ends, LANES))
    column = lane_iota((ends, LANES))
    row = lax.broadcasted_iota(jnp.int32, (ends, LANES), 0)
    turn = column & (ends - 1)
    place = jnp.where(turn < HMAX, turn - HMAX, turn - HMAX + rows)
    row = jnp.where(row < HMAX, row, row + rows - ends)
    inside = stencil_holds(place, row, end_rows(down), end_rows(up), rows) & (column < 2 * ends)
    mask_ref[...] = jnp.where(inside, 1.0, 0.0)
    acc_ref[...] = jnp.zeros_like(acc_ref)
    for n in range(inner.shape[0]):
        g = [inner[n, f] for f in range(FIELDS)]
        wall_block(g, own_ref, height_ref, inv_ref, stack.at[n], acc_ref, part_ref.at[n])


def outer_kernel(
    fh, fl, znear, zfar, ynear, yfar, pair_ref, ends_ref, acc_in, own_ref, height_ref, inv_ref,
    sums_ref, part_ref, hh, hl, halo_inner, eh, el, stack, acc_ref,
):
    rows, cells = fh.shape[1:]
    gz_odd = lax.axis_index("gz") % 2 == 1
    gy_odd = lax.axis_index("gy") % 2 == 1
    acc_ref[...] = acc_in[...]
    edge_fields(jnp.where(gz_odd, znear[...], zfar[...]), jnp.where(gz_odd, zfar[...], znear[...]), eh, el)
    g_ends = smooth_ends(fh, fl, eh, el, ends_ref)
    for t in range(cells // LANES):
        at = slice(t * LANES, (t + 1) * LANES)

        def put_high(f, x):
            hh[f, :, at] = x

        def put_low(f, x):
            hl[f, :, at] = x

        raw = []
        for f in range(9):
            span = slice(f * cells + t * LANES, f * cells + (t + 1) * LANES)
            near, far = ynear[:, span], yfar[:, span]
            raw.append(jnp.concatenate([jnp.where(gy_odd, near, far), jnp.where(gy_odd, far, near)], axis=0))
        store_fields(raw[:3], raw[3:], put_high, put_low)
    for n in range(halo_inner.shape[0]):
        g = smooth_pair(n, hh, hl, pair_ref)
        for f in range(FIELDS):
            halo_inner[n, f] = g[f]
    wall_block(g_ends, own_ref, height_ref, inv_ref, stack, acc_ref, part_ref)
    inv = inv_ref[...]
    for k in range(2):
        plane_sums = jnp.sum(acc_ref[k] * (inv * inv), axis=1, keepdims=True)
        sums_ref[k : k + 1, :] = to_row(plane_sums, lax.broadcasted_iota(jnp.int32, (rows, LANES), 0))


def edge_fields(zl, zr, eh, el):
    rows = zl.shape[0]
    lane = lane_iota((16, LANES))
    middle = LANES // 2
    follows = (lane >= middle - NX) & (lane < middle)
    precedes = (lane >= middle) & (lane < middle + NX)
    for r in range(0, rows, 16):
        rr = slice(r, r + 16)
        raw = [
            jnp.where(
                follows,
                rot(zr[rr], middle - NX - NX * f),
                jnp.where(precedes, rot(zl[rr], middle - NX * f), 0.0),
            )
            for f in range(9)
        ]

        def put_high(f, x):
            eh[f, rr, :] = x

        def put_low(f, x):
            el[f, rr, :] = x

        store_fields(raw[:3], raw[3:], put_high, put_low)


def last_kernel(near_ref, far_ref, sums_in, part_inner, part_ends, mask_ref, total_ref, hh, hl, halo_inner, ends_ref, out_ref, eh, el, stack):
    rows = out_ref.shape[2]
    width = 2 * LANES
    gy_odd = lax.axis_index("gy") % 2 == 1
    both_rows = 2 * HMAX

    def halo(at):
        near, far = near_ref[:, at], far_ref[:, at]
        return jnp.concatenate([jnp.where(gy_odd, near, far), jnp.where(gy_odd, far, near)], axis=0)

    zl = halo(slice(0, LANES))
    zr = halo(slice(LANES, 2 * LANES))
    below = rot(zl[:HMAX], -9 * NX)[0:1]
    above = rot(zl[HMAX:], -9 * NX)[0:1]
    height = jnp.concatenate([to_column(below, HMAX), to_column(above, HMAX)], axis=0)
    lane = lane_iota((both_rows, LANES))
    heights = jnp.where(lane[0:1] < HMAX, below, rot(above, HMAX))
    outside = jnp.where(lane < both_rows, mask_ref[...] * heights, 0.0)
    inv = 1.0 / (total_ref[...] + jnp.sum(outside, axis=1, keepdims=True))
    scale = [inv[:HMAX], inv[HMAX:]]
    mask = mask_ref[:, : 2 * both_rows].astype(BF16)

    edge_fields(zl, zr, eh, el)
    zero = jnp.zeros((HMAX, LANES), F32)
    sums = [[zero, zero], [zero, zero]]
    blocks = halo_inner.shape[0]
    g_ends = smooth_ends(hh, hl, eh, el, ends_ref)
    for n in range(blocks + 1):
        if n < blocks:
            g = [halo_inner[n, f] for f in range(FIELDS)]
            part = part_inner.at[n]
        else:
            part = part_ends
            g = g_ends
        for f in range(FIELDS):
            hi, lo = split2(g[f] * height)
            stack[n, 0:both_rows, f * width : (f + 1) * width] = hi
            stack[n, both_rows:, f * width : (f + 1) * width] = lo
        merged = jnp.dot(mask, stack[n], preferred_element_type=F32)
        for i in range(2):
            rr = slice(i * HMAX, (i + 1) * HMAX)
            for c in range(2):
                at = slice(c * LANES, (c + 1) * LANES)
                values = [
                    part[f, rr, at] + merged[rr, f * width + c * LANES : f * width + (c + 1) * LANES]
                    for f in range(FIELDS)
                ]
                sums[i] = list(contract(values, scale[i], *sums[i]))
    row = lax.broadcasted_iota(jnp.int32, (both_rows, LANES), 0)
    row = jnp.where(row < HMAX, row, row + rows - both_rows)
    for k in range(2):
        values = jnp.concatenate([sums[0][k], sums[1][k]], axis=0) * (inv * inv)
        total = sums_in[k : k + 1, :] + to_row(jnp.sum(values, axis=1, keepdims=True), row)
        out_ref[:, k : k + 1, :] = jnp.broadcast_to(total[None, :, :rows], (out_ref.shape[0], 1, rows))


def call(kernel, out_shape, scratch, limit, *operands, aliases=None):
    vmem = pl.BlockSpec(memory_space=pltpu.VMEM)
    return pl.pallas_call(
        kernel,
        in_specs=[vmem] * len(operands),
        out_specs=jax.tree.map(lambda _: vmem, out_shape),
        out_shape=out_shape,
        scratch_shapes=scratch,
        input_output_aliases=aliases or {},
        compiler_params=pltpu.CompilerParams(vmem_limit_bytes=limit),
        cost_estimate=pl.CostEstimate(flops=4 * 10**9, bytes_accessed=2**20, transcendentals=0),
    )(*operands)


def local(velocity, strain, cell_height, stencil_reach):
    rows, cells = velocity.shape[1:]
    width = 2 * LANES
    blocks = cells // width - 1
    ends = 2 * HMAX
    shape = jax.ShapeDtypeStruct
    heights = cell_height.reshape(1, rows)
    near, far, wall_near, wall_far, velocity, strain, pair, both_ends = first_call(velocity, strain)
    own_work = [
        shape((FIELDS, rows, cells), BF16),
        shape((WIDE, rows, cells), BF16),
        shape((blocks, FIELDS, rows, width), F32),
    ]
    messages = (near, far, wall_near, wall_far)
    fh, fl, inner, near, far, wall_near, wall_far = call(
        early_kernel,
        own_work + [shape(x.shape, x.dtype) for x in messages],
        [],
        LARGE_VMEM,
        velocity,
        strain,
        pair,
        *messages,
        aliases={3 + i: 3 + i for i in range(4)},
    )
    znear = lax.ppermute(near, "gz", near_pairs("gz"))
    zfar = lax.ppermute(far, "gz", far_pairs("gz", True))
    yfar = lax.ppermute(wall_far, "gy", far_pairs("gy", False))
    ynear = lax.ppermute(wall_near, "gy", near_pairs("gy"))
    fh, fl, inner = call(
        late_kernel,
        own_work,
        [],
        LARGE_VMEM,
        velocity,
        strain,
        pair,
        fh,
        fl,
        inner,
        aliases={3 + i: i for i in range(3)},
    )
    acc, part_inner, own, height, inv, mask, totals = call(
        wall_kernel,
        [
            shape((2, rows, LANES), F32),
            shape((blocks, FIELDS, ends, width), F32),
            shape((rows, width), BF16),
            shape((rows, LANES), F32),
            shape((rows, LANES), F32),
            shape((ends, LANES), F32),
            shape((ends, LANES), F32),
        ],
        [pltpu.VMEM((blocks, 2 * rows, FIELDS * width), BF16)],
        LARGE_VMEM,
        heights,
        stencil_reach,
        inner,
    )
    near, far = corner_call(heights, znear, zfar)
    corner_far = lax.ppermute(far, "gy", far_pairs("gy", False))
    corner_near = lax.ppermute(near, "gy", near_pairs("gy"))
    sums, part_ends, hh, hl, halo_inner = call(
        outer_kernel,
        [
            shape((2, LANES), F32),
            shape((FIELDS, ends, width), F32),
            shape((FIELDS, ends, cells), BF16),
            shape((WIDE, ends, cells), BF16),
            shape((blocks, FIELDS, ends, width), F32),
        ],
        [
            pltpu.VMEM((FIELDS, rows, LANES), BF16),
            pltpu.VMEM((WIDE, rows, LANES), BF16),
            pltpu.VMEM((2 * rows, FIELDS * width), BF16),
            pltpu.VMEM((2, rows, LANES), F32),
        ],
        LARGE_VMEM,
        fh,
        fl,
        znear,
        zfar,
        ynear,
        yfar,
        pair,
        both_ends,
        acc,
        own,
        height,
        inv,
    )
    sums = call(
        last_kernel,
        shape((lax.axis_size("gz"), 2, rows), F32),
        [
            pltpu.VMEM((FIELDS, ends, LANES), BF16),
            pltpu.VMEM((WIDE, ends, LANES), BF16),
            pltpu.VMEM((blocks + 1, 2 * ends, FIELDS * width), BF16),
        ],
        LARGE_VMEM,
        corner_near,
        corner_far,
        sums,
        part_inner,
        part_ends,
        mask,
        totals,
        hh,
        hl,
        halo_inner,
        both_ends,
    )
    sums = jnp.sum(lax.all_to_all(sums, "gz", 0, 0), axis=0)
    total = lax.axis_size("gz") * cells
    return sums[0] / total / (sums[1] / total + 1e-06)


def near_pairs(axis):
    return [(i, i ^ 1) for i in range(lax.axis_size(axis))]


def far_pairs(axis, closed):
    n = lax.axis_size(axis)
    pairs = []
    for i in range(1, n if closed else n - 1, 2):
        pairs += [(i, (i + 1) % n), ((i + 1) % n, i)]
    return pairs


def solution(mesh):
    in_specs = (P(None, "gy", "gz"), P(None, "gy", "gz"), P("gy"), P(None, "gy"))
    return jax.shard_map(local, mesh=mesh, in_specs=in_specs, out_specs=P("gy"), check_vma=False)
```

```python
import jax
import jax.numpy as jnp
from jax import lax
from jax.experimental import pallas as pl
from jax.experimental.pallas import tpu as pltpu
from jax.sharding import PartitionSpec as P

NX = 8
HMAX = 8
LANES = 128
FIELDS = 21
WIDE = 15
FIRST_VMEM = 51 * 1024 * 1024
SMALL_VMEM = 24 * 1024 * 1024
LARGE_VMEM = 24 * 1024 * 1024
LEAD_INDEX = (0, 1, 2, 0, 0, 1)
TAIL_INDEX = (0, 1, 2, 1, 2, 2)
TENSOR_WEIGHTS = (1.0, 1.0, 1.0, 2.0, 2.0, 2.0)
F32 = jnp.float32
BF16 = jnp.bfloat16


def strain_rate(s):
    squares = 2.0 * (s[0] * s[0] + s[1] * s[1] + s[2] * s[2])
    squares = squares + 4.0 * (s[3] * s[3] + s[4] * s[4] + s[5] * s[5])
    return jnp.sqrt(squares)


def lane_iota(shape):
    return lax.broadcasted_iota(jnp.int32, shape, len(shape) - 1)


def rot(x, amount):
    amount = amount % LANES
    return pltpu.roll(x, amount, x.ndim - 1) if amount else x


def cell_weights(source, target):
    turn = (source - target) & (NX - 1)
    along = jnp.where(turn == 0, 0.5, jnp.where((turn == 1) | (turn == NX - 1), 0.25, 0.0))
    step = ((source + LANES) >> 3) - ((target + LANES) >> 3)
    across = jnp.where(step == 0, 0.5, jnp.where((step == 1) | (step == -1), 0.25, 0.0))
    return along * across


def pair_filter():
    shape = (3 * LANES, 2 * LANES)
    k = lax.broadcasted_iota(jnp.int32, shape, 0)
    return cell_weights(jnp.where(k < 5 * LANES // 2, k, k - 3 * LANES), lane_iota(shape)).astype(BF16)


def ends_filter():
    shape = (3 * LANES, 2 * LANES)
    k = lax.broadcasted_iota(jnp.int32, shape, 0)
    m = lane_iota(shape)
    place = k & (LANES - 1)
    middle = LANES // 2
    outer = k >= 2 * LANES
    last = place >= LANES - NX
    after = (place >= middle - NX) & (place < middle)
    before = (place >= middle) & (place < middle + NX)
    used = (place < NX) | last | after | before
    shift = jnp.where(last, -LANES, jnp.where(after, LANES - middle + NX, jnp.where(before, -middle - NX, LANES)))
    source = jnp.where(outer, place + shift, place)
    tile = jnp.where(outer, jnp.where(last | after, 1, 0), k >> 7)
    fits = (tile == (m >> 7)) & (used | (k < 2 * LANES))
    return jnp.where(fits, cell_weights(source, m & (LANES - 1)), 0.0).astype(BF16)


def first_kernel(v_ref, s_ref, near_ref, far_ref, wall_near, wall_far, v_out, s_out, pair_ref, ends_ref, sems):
    rows, cells = v_ref.shape[1:]
    spans = ((0, LANES), (cells - LANES, LANES), (LANES, cells - 2 * LANES))
    copies = []
    for i, (start, size) in enumerate(spans):
        for j, (ref, out) in enumerate(((v_ref, v_out), (s_ref, s_out))):
            at = pl.ds(start, size)
            copies.append(pltpu.make_async_copy(ref.at[:, :, at], out.at[:, :, at], sems.at[i, j]))
    for copy in copies:
        copy.start()
    pair_ref[...] = pair_filter()
    ends_ref[...] = ends_filter()
    for copy in copies[:4]:
        copy.wait()
    lane = lane_iota((rows, LANES))
    left = jnp.zeros((rows, LANES), F32)
    right = jnp.zeros((rows, LANES), F32)
    for f in range(9):
        ref, at = (v_out, f) if f < 3 else (s_out, f - 3)
        here = (lane >= NX * f) & (lane < NX * (f + 1))
        left = jnp.where(here, rot(ref[at, :, :LANES].astype(F32), NX * f), left)
        right = jnp.where(here, rot(ref[at, :, cells - LANES :].astype(F32), NX * f + NX), right)
    odd = lax.axis_index("gz") % 2 == 1
    near_ref[...] = jnp.where(odd, left, right)
    far_ref[...] = jnp.where(odd, right, left)
    for copy in copies[4:]:
        copy.wait()
    gy_odd = lax.axis_index("gy") % 2 == 1
    for f in range(9):
        at = slice(f * cells, (f + 1) * cells)
        if f < 3:
            low, high = v_out[f, :HMAX, :], v_out[f, rows - HMAX :, :]
        else:
            low = s_out[f - 3, : 2 * HMAX, :].astype(F32)[:HMAX]
            high = s_out[f - 3, rows - 2 * HMAX :, :].astype(F32)[HMAX:]
        wall_near[:, at] = jnp.where(gy_odd, low, high)
        wall_far[:, at] = jnp.where(gy_odd, high, low)


def first_call(velocity, strain):
    rows, cells = velocity.shape[1:]
    hbm = pl.BlockSpec(memory_space=pltpu.HBM)
    vmem = pl.BlockSpec(memory_space=pltpu.VMEM)
    shape = jax.ShapeDtypeStruct
    return pl.pallas_call(
        first_kernel,
        in_specs=[hbm] * 2,
        out_specs=[vmem] * 8,
        out_shape=[shape((rows, LANES), F32)] * 2
        + [shape((HMAX, 9 * cells), F32)] * 2
        + [shape(x.shape, x.dtype) for x in (velocity, strain)]
        + [shape((3 * LANES, 2 * LANES), BF16)] * 2,
        scratch_shapes=[pltpu.SemaphoreType.DMA((3, 2))],
        compiler_params=pltpu.CompilerParams(vmem_limit_bytes=FIRST_VMEM),
    )(velocity, strain)


def corner_kernel(h_ref, znear, zfar, near_ref, far_ref):
    rows = znear.shape[0]
    gz_odd = lax.axis_index("gz") % 2 == 1
    gy_odd = lax.axis_index("gy") % 2 == 1
    lane = lane_iota((HMAX, LANES))
    row = lax.broadcasted_iota(jnp.int32, (HMAX, LANES), 0)
    stamp = (row == 0) & (lane >= 9 * NX) & (lane < 10 * NX)
    heights = jnp.broadcast_to(jnp.pad(h_ref[...], ((0, 0), (0, LANES - rows))), (HMAX, LANES))
    sides = []
    for r0 in (0, rows - HMAX):
        zn = znear[r0 : r0 + HMAX, :]
        zf = zfar[r0 : r0 + HMAX, :]
        zl = jnp.where(stamp, rot(heights, 9 * NX - r0), jnp.where(gz_odd, zn, zf))
        sides.append((zl, jnp.where(gz_odd, zf, zn)))
    (low_left, low_right), (high_left, high_right) = sides
    near_ref[:, :LANES] = jnp.where(gy_odd, low_left, high_left)
    near_ref[:, LANES:] = jnp.where(gy_odd, low_right, high_right)
    far_ref[:, :LANES] = jnp.where(gy_odd, high_left, low_left)
    far_ref[:, LANES:] = jnp.where(gy_odd, high_right, low_right)


def corner_call(heights, znear, zfar):
    vmem = pl.BlockSpec(memory_space=pltpu.VMEM)
    return pl.pallas_call(
        corner_kernel,
        in_specs=[vmem] * 3,
        out_specs=[vmem] * 2,
        out_shape=[jax.ShapeDtypeStruct((HMAX, 2 * LANES), F32)] * 2,
        compiler_params=pltpu.CompilerParams(vmem_limit_bytes=SMALL_VMEM),
    )(heights, znear, zfar)


def split2(x):
    hi = x.astype(BF16)
    return hi, (x - hi.astype(F32)).astype(BF16)


def store_fields(u, s, put_high, put_low):
    tensor = [x.astype(F32) for x in s]
    rate = strain_rate(tensor)
    wide = u + [u[a] * u[b] for a, b in zip(LEAD_INDEX, TAIL_INDEX)] + [rate * x for x in tensor]
    for f, value in enumerate(wide):
        hi, lo = split2(value)
        put_high(f, hi)
        put_low(f, lo)
    for f, value in enumerate(s):
        put_high(WIDE + f, value.astype(BF16))


def smooth(rows, operand, matrix_ref):
    wide, narrow = slice(0, WIDE), slice(WIDE, FIELDS)
    lhs = jnp.concatenate([operand(True, wide), operand(False, wide)], axis=-1).reshape(WIDE * rows, -1)
    matrix = matrix_ref[...]
    first = jnp.dot(lhs, jnp.concatenate([matrix, matrix], axis=0), preferred_element_type=F32)
    lhs = operand(True, narrow).reshape((FIELDS - WIDE) * rows, -1)
    second = jnp.dot(lhs, matrix, preferred_element_type=F32)
    return [first[f * rows : (f + 1) * rows] for f in range(WIDE)] + [
        second[f * rows : (f + 1) * rows] for f in range(FIELDS - WIDE)
    ]


def pick(after, before):
    return jnp.where(lane_iota(after.shape) < LANES // 2, after, before)


def smooth_pair(n, fh, fl, pair_ref):
    def operand(high, fields):
        ref = fh if high else fl
        tile = [ref[fields, :, (2 * n + i) * LANES : (2 * n + i + 1) * LANES] for i in range(4)]
        return jnp.concatenate([tile[1], tile[2], pick(tile[3], tile[0])], axis=-1)

    return smooth(fh.shape[1], operand, pair_ref)


def smooth_ends(fh, fl, eh, el, ends_ref):
    cells = fh.shape[2]

    def operand(high, fields):
        ref, outer = (fh, eh) if high else (fl, el)
        second = ref[fields, :, LANES : 2 * LANES]
        ahead = ref[fields, :, cells - 2 * LANES : cells - LANES]
        lane = lane_iota(second.shape)
        edge = jnp.where(lane < NX, second, jnp.where(lane >= LANES - NX, ahead, outer[fields]))
        return jnp.concatenate([ref[fields, :, :LANES], ref[fields, :, cells - LANES :], edge], axis=-1)

    return smooth(fh.shape[1], operand, ends_ref)


def contract(g, inv, num, den):
    u, p, m, s = g[0:3], g[3:9], g[9:15], g[15:21]
    rate = 4.0 * inv * strain_rate(s)
    scaled = [inv * x for x in u]
    for k in range(6):
        leonard = p[k] - scaled[LEAD_INDEX[k]] * u[TAIL_INDEX[k]]
        model = m[k] - rate * s[k]
        weighted = TENSOR_WEIGHTS[k] * model
        num = num + weighted * leonard
        den = den + weighted * model
    return num, den


def to_column(row_vector, size):
    shape = (size, LANES)
    eye = lax.broadcasted_iota(jnp.int32, shape, 0) == lane_iota(shape)
    return jnp.sum(jnp.where(eye, jnp.broadcast_to(row_vector, shape), 0.0), axis=1, keepdims=True)


def to_row(column_vector, row):
    return jnp.sum(jnp.where(row == lane_iota(row.shape), column_vector, 0.0), axis=0, keepdims=True)


def pad_lanes(x):
    return jnp.pad(x, ((0, 0), (0, LANES - x.shape[1])))


def stencil_holds(place, row, down, up, rows):
    gy = lax.axis_index("gy")
    lowest = jnp.maximum(row - down, -gy * rows)
    highest = jnp.minimum(row + up, (lax.axis_size("gy") - gy) * rows - 1)
    return (place >= lowest) & (place <= highest)


def end_rows(x):
    return jnp.concatenate([x[:HMAX], x[x.shape[0] - HMAX :]], axis=0)


def wall_block(g, own_ref, height_ref, inv_ref, stack, acc_ref, part_ref):
    rows = g[0].shape[0]
    width = 2 * LANES
    height = jnp.concatenate([height_ref[...], height_ref[...]], axis=1)
    mask = own_ref[:, : 2 * rows]
    for f in range(FIELDS):
        hi, lo = split2(g[f] * height)
        stack[0:rows, f * width : (f + 1) * width] = hi
        stack[rows:, f * width : (f + 1) * width] = lo
    merged = jnp.dot(mask, stack[...], preferred_element_type=F32)
    for f in range(FIELDS):
        part_ref[f, 0:HMAX, :] = merged[0:HMAX, f * width : (f + 1) * width]
        part_ref[f, HMAX:, :] = merged[rows - HMAX :, f * width : (f + 1) * width]
    for r in range(HMAX, rows - HMAX, HMAX):
        num = acc_ref[0, r : r + HMAX, :]
        den = acc_ref[1, r : r + HMAX, :]
        scale = inv_ref[r : r + HMAX, :]
        for c in range(2):
            parts = [
                merged[r : r + HMAX, f * width + c * LANES : f * width + (c + 1) * LANES] for f in range(FIELDS)
            ]
            num, den = contract(parts, scale, num, den)
        acc_ref[0, r : r + HMAX, :] = num
        acc_ref[1, r : r + HMAX, :] = den


def leaves_early():
    return lax.axis_index("gz") == 0


def inner_work(v_ref, s_ref, pair_ref, fh, fl, inner):
    rows, cells = v_ref.shape[1:]
    for t in range(cells // LANES):
        at = slice(t * LANES, (t + 1) * LANES)
        for r in range(0, rows, 16):
            rr = slice(r, r + 16)

            def put_high(f, x):
                fh[f, rr, at] = x

            def put_low(f, x):
                fl[f, rr, at] = x

            store_fields(
                [v_ref[f, rr, at] for f in range(3)], [s_ref[f, rr, at] for f in range(6)], put_high, put_low
            )
    for n in range(inner.shape[0]):
        g = smooth_pair(n, fh, fl, pair_ref)
        for f in range(FIELDS):
            inner[n, f] = g[f]


def early_kernel(v_ref, s_ref, pair_ref, a, b, c, d, fh, fl, inner, *same):
    @pl.when(leaves_early())
    def _():
        inner_work(v_ref, s_ref, pair_ref, fh, fl, inner)


def late_kernel(v_ref, s_ref, pair_ref, a, b, c, fh, fl, inner):
    @pl.when(jnp.logical_not(leaves_early()))
    def _():
        inner_work(v_ref, s_ref, pair_ref, fh, fl, inner)


def wall_kernel(
    h_ref, reach_ref, inner, acc_ref, part_ref, own_ref, height_ref, inv_ref, mask_ref, total_ref, stack
):
    rows = h_ref.shape[1]
    ends = 2 * HMAX
    reach = pad_lanes(reach_ref[...].astype(F32))
    down = to_column(reach[0:1], rows).astype(jnp.int32)
    up = to_column(reach[1:2], rows).astype(jnp.int32)
    column = lane_iota((rows, 2 * LANES))
    row = lax.broadcasted_iota(jnp.int32, (rows, 2 * LANES), 0)
    place = jnp.where(column < rows, column, column - rows)
    inside = stencil_holds(place, row, down, up, rows)
    own_ref[...] = jnp.where(inside, 1.0, 0.0).astype(BF16)
    heights = pad_lanes(h_ref[...])
    height_ref[...] = jnp.broadcast_to(to_column(heights, rows), (rows, LANES))
    own = inside[:, :LANES] & (column[:, :LANES] < rows)
    total = jnp.sum(jnp.where(own, jnp.broadcast_to(heights, (rows, LANES)), 0.0), axis=1, keepdims=True)
    inv_ref[...] = jnp.broadcast_to(1.0 / total, (rows, LANES))
    total_ref[...] = jnp.broadcast_to(end_rows(total), (ends, LANES))
    column = lane_iota((ends, LANES))
    row = lax.broadcasted_iota(jnp.int32, (ends, LANES), 0)
    turn = column & (ends - 1)
    place = jnp.where(turn < HMAX, turn - HMAX, turn - HMAX + rows)
    row = jnp.where(row < HMAX, row, row + rows - ends)
    inside = stencil_holds(place, row, end_rows(down), end_rows(up), rows) & (column < 2 * ends)
    mask_ref[...] = jnp.where(inside, 1.0, 0.0)
    acc_ref[...] = jnp.zeros_like(acc_ref)
    for n in range(inner.shape[0]):
        g = [inner[n, f] for f in range(FIELDS)]
        wall_block(g, own_ref, height_ref, inv_ref, stack.at[n], acc_ref, part_ref.at[n])


def outer_kernel(
    fh, fl, znear, zfar, yfar, ynear, pair_ref, ends_ref, acc_in, own_ref, height_ref, inv_ref,
    sums_ref, part_ref, hh, hl, halo_inner, eh, el, stack, acc_ref,
):
    rows, cells = fh.shape[1:]
    gz_odd = lax.axis_index("gz") % 2 == 1
    gy_odd = lax.axis_index("gy") % 2 == 1
    acc_ref[...] = acc_in[...]
    edge_fields(jnp.where(gz_odd, znear[...], zfar[...]), jnp.where(gz_odd, zfar[...], znear[...]), eh, el)
    g_ends = smooth_ends(fh, fl, eh, el, ends_ref)
    for t in range(cells // LANES):
        at = slice(t * LANES, (t + 1) * LANES)

        def put_high(f, x):
            hh[f, :, at] = x

        def put_low(f, x):
            hl[f, :, at] = x

        raw = []
        for f in range(9):
            span = slice(f * cells + t * LANES, f * cells + (t + 1) * LANES)
            near, far = ynear[:, span], yfar[:, span]
            raw.append(jnp.concatenate([jnp.where(gy_odd, near, far), jnp.where(gy_odd, far, near)], axis=0))
        store_fields(raw[:3], raw[3:], put_high, put_low)
    for n in range(halo_inner.shape[0]):
        g = smooth_pair(n, hh, hl, pair_ref)
        for f in range(FIELDS):
            halo_inner[n, f] = g[f]
    wall_block(g_ends, own_ref, height_ref, inv_ref, stack, acc_ref, part_ref)
    inv = inv_ref[...]
    for k in range(2):
        plane_sums = jnp.sum(acc_ref[k] * (inv * inv), axis=1, keepdims=True)
        sums_ref[k : k + 1, :] = to_row(plane_sums, lax.broadcasted_iota(jnp.int32, (rows, LANES), 0))


def edge_fields(zl, zr, eh, el):
    rows = zl.shape[0]
    lane = lane_iota((16, LANES))
    middle = LANES // 2
    follows = (lane >= middle - NX) & (lane < middle)
    precedes = (lane >= middle) & (lane < middle + NX)
    for r in range(0, rows, 16):
        rr = slice(r, r + 16)
        raw = [
            jnp.where(
                follows,
                rot(zr[rr], middle - NX - NX * f),
                jnp.where(precedes, rot(zl[rr], middle - NX * f), 0.0),
            )
            for f in range(9)
        ]

        def put_high(f, x):
            eh[f, rr, :] = x

        def put_low(f, x):
            el[f, rr, :] = x

        store_fields(raw[:3], raw[3:], put_high, put_low)


def last_kernel(far_ref, near_ref, sums_in, part_inner, part_ends, mask_ref, total_ref, hh, hl, halo_inner, ends_ref, out_ref, eh, el, stack):
    rows = out_ref.shape[2]
    width = 2 * LANES
    gy_odd = lax.axis_index("gy") % 2 == 1
    both_rows = 2 * HMAX

    def halo(at):
        near, far = near_ref[:, at], far_ref[:, at]
        return jnp.concatenate([jnp.where(gy_odd, near, far), jnp.where(gy_odd, far, near)], axis=0)

    zl = halo(slice(0, LANES))
    zr = halo(slice(LANES, 2 * LANES))
    below = rot(zl[:HMAX], -9 * NX)[0:1]
    above = rot(zl[HMAX:], -9 * NX)[0:1]
    height = jnp.concatenate([to_column(below, HMAX), to_column(above, HMAX)], axis=0)
    lane = lane_iota((both_rows, LANES))
    heights = jnp.where(lane[0:1] < HMAX, below, rot(above, HMAX))
    outside = jnp.where(lane < both_rows, mask_ref[...] * heights, 0.0)
    inv = 1.0 / (total_ref[...] + jnp.sum(outside, axis=1, keepdims=True))
    scale = [inv[:HMAX], inv[HMAX:]]
    mask = mask_ref[:, : 2 * both_rows].astype(BF16)

    edge_fields(zl, zr, eh, el)
    zero = jnp.zeros((HMAX, LANES), F32)
    sums = [[zero, zero], [zero, zero]]
    blocks = halo_inner.shape[0]
    g_ends = smooth_ends(hh, hl, eh, el, ends_ref)
    for n in range(blocks + 1):
        if n < blocks:
            g = [halo_inner[n, f] for f in range(FIELDS)]
            part = part_inner.at[n]
        else:
            part = part_ends
            g = g_ends
        for f in range(FIELDS):
            hi, lo = split2(g[f] * height)
            stack[n, 0:both_rows, f * width : (f + 1) * width] = hi
            stack[n, both_rows:, f * width : (f + 1) * width] = lo
        merged = jnp.dot(mask, stack[n], preferred_element_type=F32)
        for i in range(2):
            rr = slice(i * HMAX, (i + 1) * HMAX)
            for c in range(2):
                at = slice(c * LANES, (c + 1) * LANES)
                values = [
                    part[f, rr, at] + merged[rr, f * width + c * LANES : f * width + (c + 1) * LANES]
                    for f in range(FIELDS)
                ]
                sums[i] = list(contract(values, scale[i], *sums[i]))
    row = lax.broadcasted_iota(jnp.int32, (both_rows, LANES), 0)
    row = jnp.where(row < HMAX, row, row + rows - both_rows)
    for k in range(2):
        values = jnp.concatenate([sums[0][k], sums[1][k]], axis=0) * (inv * inv)
        total = sums_in[k : k + 1, :] + to_row(jnp.sum(values, axis=1, keepdims=True), row)
        out_ref[:, k : k + 1, :] = jnp.broadcast_to(total[None, :, :rows], (out_ref.shape[0], 1, rows))


def call(kernel, out_shape, scratch, limit, *operands, aliases=None):
    vmem = pl.BlockSpec(memory_space=pltpu.VMEM)
    return pl.pallas_call(
        kernel,
        in_specs=[vmem] * len(operands),
        out_specs=jax.tree.map(lambda _: vmem, out_shape),
        out_shape=out_shape,
        scratch_shapes=scratch,
        input_output_aliases=aliases or {},
        compiler_params=pltpu.CompilerParams(vmem_limit_bytes=limit),
        cost_estimate=pl.CostEstimate(flops=4 * 10**9, bytes_accessed=2**20, transcendentals=0),
    )(*operands)


def local(velocity, strain, cell_height, stencil_reach):
    rows, cells = velocity.shape[1:]
    width = 2 * LANES
    blocks = cells // width - 1
    ends = 2 * HMAX
    shape = jax.ShapeDtypeStruct
    heights = cell_height.reshape(1, rows)
    near, far, wall_near, wall_far, velocity, strain, pair, both_ends = first_call(velocity, strain)
    own_work = [
        shape((FIELDS, rows, cells), BF16),
        shape((WIDE, rows, cells), BF16),
        shape((blocks, FIELDS, rows, width), F32),
    ]
    messages = (near, far, wall_near, wall_far)
    fh, fl, inner, near, far, wall_near, wall_far = call(
        early_kernel,
        own_work + [shape(x.shape, x.dtype) for x in messages],
        [],
        LARGE_VMEM,
        velocity,
        strain,
        pair,
        *messages,
        aliases={3 + i: 3 + i for i in range(4)},
    )
    znear = lax.ppermute(near, "gz", near_pairs("gz"))
    zfar = lax.ppermute(far, "gz", far_pairs("gz", True))
    yfar = lax.ppermute(wall_far, "gy", far_pairs("gy", False))
    ynear = lax.ppermute(wall_near, "gy", near_pairs("gy"))
    fh, fl, inner = call(
        late_kernel,
        own_work,
        [],
        LARGE_VMEM,
        velocity,
        strain,
        pair,
        fh,
        fl,
        inner,
        aliases={3 + i: i for i in range(3)},
    )
    acc, part_inner, own, height, inv, mask, totals = call(
        wall_kernel,
        [
            shape((2, rows, LANES), F32),
            shape((blocks, FIELDS, ends, width), F32),
            shape((rows, width), BF16),
            shape((rows, LANES), F32),
            shape((rows, LANES), F32),
            shape((ends, LANES), F32),
            shape((ends, LANES), F32),
        ],
        [pltpu.VMEM((blocks, 2 * rows, FIELDS * width), BF16)],
        LARGE_VMEM,
        heights,
        stencil_reach,
        inner,
    )
    near, far = corner_call(heights, znear, zfar)
    corner_far = lax.ppermute(far, "gy", far_pairs("gy", False))
    corner_near = lax.ppermute(near, "gy", near_pairs("gy"))
    sums, part_ends, hh, hl, halo_inner = call(
        outer_kernel,
        [
            shape((2, LANES), F32),
            shape((FIELDS, ends, width), F32),
            shape((FIELDS, ends, cells), BF16),
            shape((WIDE, ends, cells), BF16),
            shape((blocks, FIELDS, ends, width), F32),
        ],
        [
            pltpu.VMEM((FIELDS, rows, LANES), BF16),
            pltpu.VMEM((WIDE, rows, LANES), BF16),
            pltpu.VMEM((2 * rows, FIELDS * width), BF16),
            pltpu.VMEM((2, rows, LANES), F32),
        ],
        LARGE_VMEM,
        fh,
        fl,
        znear,
        zfar,
        yfar,
        ynear,
        pair,
        both_ends,
        acc,
        own,
        height,
        inv,
    )
    sums = call(
        last_kernel,
        shape((lax.axis_size("gz"), 2, rows), F32),
        [
            pltpu.VMEM((FIELDS, ends, LANES), BF16),
            pltpu.VMEM((WIDE, ends, LANES), BF16),
            pltpu.VMEM((blocks + 1, 2 * ends, FIELDS * width), BF16),
        ],
        LARGE_VMEM,
        corner_far,
        corner_near,
        sums,
        part_inner,
        part_ends,
        mask,
        totals,
        hh,
        hl,
        halo_inner,
        both_ends,
    )
    sums = jnp.sum(lax.all_to_all(sums, "gz", 0, 0), axis=0)
    total = lax.axis_size("gz") * cells
    return sums[0] / total / (sums[1] / total + 1e-06)


def near_pairs(axis):
    return [(i, i ^ 1) for i in range(lax.axis_size(axis))]


def far_pairs(axis, closed):
    n = lax.axis_size(axis)
    pairs = []
    for i in range(1, n if closed else n - 1, 2):
        pairs += [(i, (i + 1) % n), ((i + 1) % n, i)]
    return pairs


def solution(mesh):
    in_specs = (P(None, "gy", "gz"), P(None, "gy", "gz"), P("gy"), P(None, "gy"))
    return jax.shard_map(local, mesh=mesh, in_specs=in_specs, out_specs=P("gy"), check_vma=False)
```

```python
import jax
import jax.numpy as jnp
from jax import lax
from jax.experimental import pallas as pl
from jax.experimental.pallas import tpu as pltpu
from jax.sharding import PartitionSpec as P

NX = 8
HMAX = 8
LANES = 128
FIELDS = 21
WIDE = 15
FIRST_VMEM = 51 * 1024 * 1024
SMALL_VMEM = 24 * 1024 * 1024
LARGE_VMEM = 24 * 1024 * 1024
LEAD_INDEX = (0, 1, 2, 0, 0, 1)
TAIL_INDEX = (0, 1, 2, 1, 2, 2)
TENSOR_WEIGHTS = (1.0, 1.0, 1.0, 2.0, 2.0, 2.0)
F32 = jnp.float32
BF16 = jnp.bfloat16


def strain_rate(s):
    squares = 2.0 * (s[0] * s[0] + s[1] * s[1] + s[2] * s[2])
    squares = squares + 4.0 * (s[3] * s[3] + s[4] * s[4] + s[5] * s[5])
    return jnp.sqrt(squares)


def lane_iota(shape):
    return lax.broadcasted_iota(jnp.int32, shape, len(shape) - 1)


def rot(x, amount):
    amount = amount % LANES
    return pltpu.roll(x, amount, x.ndim - 1) if amount else x


def cell_weights(source, target):
    turn = (source - target) & (NX - 1)
    along = jnp.where(turn == 0, 0.5, jnp.where((turn == 1) | (turn == NX - 1), 0.25, 0.0))
    step = ((source + LANES) >> 3) - ((target + LANES) >> 3)
    across = jnp.where(step == 0, 0.5, jnp.where((step == 1) | (step == -1), 0.25, 0.0))
    return along * across


def pair_filter():
    shape = (3 * LANES, 2 * LANES)
    k = lax.broadcasted_iota(jnp.int32, shape, 0)
    return cell_weights(jnp.where(k < 5 * LANES // 2, k, k - 3 * LANES), lane_iota(shape)).astype(BF16)


def ends_filter():
    shape = (3 * LANES, 2 * LANES)
    k = lax.broadcasted_iota(jnp.int32, shape, 0)
    m = lane_iota(shape)
    place = k & (LANES - 1)
    middle = LANES // 2
    outer = k >= 2 * LANES
    last = place >= LANES - NX
    after = (place >= middle - NX) & (place < middle)
    before = (place >= middle) & (place < middle + NX)
    used = (place < NX) | last | after | before
    shift = jnp.where(last, -LANES, jnp.where(after, LANES - middle + NX, jnp.where(before, -middle - NX, LANES)))
    source = jnp.where(outer, place + shift, place)
    tile = jnp.where(outer, jnp.where(last | after, 1, 0), k >> 7)
    fits = (tile == (m >> 7)) & (used | (k < 2 * LANES))
    return jnp.where(fits, cell_weights(source, m & (LANES - 1)), 0.0).astype(BF16)


def first_kernel(v_ref, s_ref, near_ref, far_ref, wall_near, wall_far, v_out, s_out, pair_ref, ends_ref, sems):
    rows, cells = v_ref.shape[1:]
    spans = ((0, LANES), (cells - LANES, LANES), (LANES, cells - 2 * LANES))
    copies = []
    for i, (start, size) in enumerate(spans):
        for j, (ref, out) in enumerate(((v_ref, v_out), (s_ref, s_out))):
            at = pl.ds(start, size)
            copies.append(pltpu.make_async_copy(ref.at[:, :, at], out.at[:, :, at], sems.at[i, j]))
    for copy in copies:
        copy.start()
    pair_ref[...] = pair_filter()
    ends_ref[...] = ends_filter()
    for copy in copies[:4]:
        copy.wait()
    lane = lane_iota((rows, LANES))
    left = jnp.zeros((rows, LANES), F32)
    right = jnp.zeros((rows, LANES), F32)
    for f in range(9):
        ref, at = (v_out, f) if f < 3 else (s_out, f - 3)
        here = (lane >= NX * f) & (lane < NX * (f + 1))
        left = jnp.where(here, rot(ref[at, :, :LANES].astype(F32), NX * f), left)
        right = jnp.where(here, rot(ref[at, :, cells - LANES :].astype(F32), NX * f + NX), right)
    odd = lax.axis_index("gz") % 2 == 1
    near_ref[...] = jnp.where(odd, left, right)
    far_ref[...] = jnp.where(odd, right, left)
    for copy in copies[4:]:
        copy.wait()
    gy_odd = lax.axis_index("gy") % 2 == 1
    for f in range(9):
        at = slice(f * cells, (f + 1) * cells)
        if f < 3:
            low, high = v_out[f, :HMAX, :], v_out[f, rows - HMAX :, :]
        else:
            low = s_out[f - 3, : 2 * HMAX, :].astype(F32)[:HMAX]
            high = s_out[f - 3, rows - 2 * HMAX :, :].astype(F32)[HMAX:]
        wall_near[:, at] = jnp.where(gy_odd, low, high)
        wall_far[:, at] = jnp.where(gy_odd, high, low)


def first_call(velocity, strain):
    rows, cells = velocity.shape[1:]
    hbm = pl.BlockSpec(memory_space=pltpu.HBM)
    vmem = pl.BlockSpec(memory_space=pltpu.VMEM)
    shape = jax.ShapeDtypeStruct
    return pl.pallas_call(
        first_kernel,
        in_specs=[hbm] * 2,
        out_specs=[vmem] * 8,
        out_shape=[shape((rows, LANES), F32)] * 2
        + [shape((HMAX, 9 * cells), F32)] * 2
        + [shape(x.shape, x.dtype) for x in (velocity, strain)]
        + [shape((3 * LANES, 2 * LANES), BF16)] * 2,
        scratch_shapes=[pltpu.SemaphoreType.DMA((3, 2))],
        compiler_params=pltpu.CompilerParams(vmem_limit_bytes=FIRST_VMEM),
    )(velocity, strain)


def corner_kernel(h_ref, znear, zfar, near_ref, far_ref):
    rows = znear.shape[0]
    gz_odd = lax.axis_index("gz") % 2 == 1
    gy_odd = lax.axis_index("gy") % 2 == 1
    lane = lane_iota((HMAX, LANES))
    row = lax.broadcasted_iota(jnp.int32, (HMAX, LANES), 0)
    stamp = (row == 0) & (lane >= 9 * NX) & (lane < 10 * NX)
    heights = jnp.broadcast_to(jnp.pad(h_ref[...], ((0, 0), (0, LANES - rows))), (HMAX, LANES))
    sides = []
    for r0 in (0, rows - HMAX):
        zn = znear[r0 : r0 + HMAX, :]
        zf = zfar[r0 : r0 + HMAX, :]
        zl = jnp.where(stamp, rot(heights, 9 * NX - r0), jnp.where(gz_odd, zn, zf))
        sides.append((zl, jnp.where(gz_odd, zf, zn)))
    (low_left, low_right), (high_left, high_right) = sides
    near_ref[:, :LANES] = jnp.where(gy_odd, low_left, high_left)
    near_ref[:, LANES:] = jnp.where(gy_odd, low_right, high_right)
    far_ref[:, :LANES] = jnp.where(gy_odd, high_left, low_left)
    far_ref[:, LANES:] = jnp.where(gy_odd, high_right, low_right)


def corner_call(heights, znear, zfar):
    vmem = pl.BlockSpec(memory_space=pltpu.VMEM)
    return pl.pallas_call(
        corner_kernel,
        in_specs=[vmem] * 3,
        out_specs=[vmem] * 2,
        out_shape=[jax.ShapeDtypeStruct((HMAX, 2 * LANES), F32)] * 2,
        compiler_params=pltpu.CompilerParams(vmem_limit_bytes=SMALL_VMEM),
    )(heights, znear, zfar)


def split2(x):
    hi = x.astype(BF16)
    return hi, (x - hi.astype(F32)).astype(BF16)


def store_fields(u, s, put_high, put_low):
    tensor = [x.astype(F32) for x in s]
    rate = strain_rate(tensor)
    wide = u + [u[a] * u[b] for a, b in zip(LEAD_INDEX, TAIL_INDEX)] + [rate * x for x in tensor]
    for f, value in enumerate(wide):
        hi, lo = split2(value)
        put_high(f, hi)
        put_low(f, lo)
    for f, value in enumerate(s):
        put_high(WIDE + f, value.astype(BF16))


def smooth(rows, operand, matrix_ref):
    wide, narrow = slice(0, WIDE), slice(WIDE, FIELDS)
    lhs = jnp.concatenate([operand(True, wide), operand(False, wide)], axis=-1).reshape(WIDE * rows, -1)
    matrix = matrix_ref[...]
    first = jnp.dot(lhs, jnp.concatenate([matrix, matrix], axis=0), preferred_element_type=F32)
    lhs = operand(True, narrow).reshape((FIELDS - WIDE) * rows, -1)
    second = jnp.dot(lhs, matrix, preferred_element_type=F32)
    return [first[f * rows : (f + 1) * rows] for f in range(WIDE)] + [
        second[f * rows : (f + 1) * rows] for f in range(FIELDS - WIDE)
    ]


def pick(after, before):
    return jnp.where(lane_iota(after.shape) < LANES // 2, after, before)


def smooth_pair(n, fh, fl, pair_ref):
    def operand(high, fields):
        ref = fh if high else fl
        tile = [ref[fields, :, (2 * n + i) * LANES : (2 * n + i + 1) * LANES] for i in range(4)]
        return jnp.concatenate([tile[1], tile[2], pick(tile[3], tile[0])], axis=-1)

    return smooth(fh.shape[1], operand, pair_ref)


def smooth_ends(fh, fl, eh, el, ends_ref):
    cells = fh.shape[2]

    def operand(high, fields):
        ref, outer = (fh, eh) if high else (fl, el)
        second = ref[fields, :, LANES : 2 * LANES]
        ahead = ref[fields, :, cells - 2 * LANES : cells - LANES]
        lane = lane_iota(second.shape)
        edge = jnp.where(lane < NX, second, jnp.where(lane >= LANES - NX, ahead, outer[fields]))
        return jnp.concatenate([ref[fields, :, :LANES], ref[fields, :, cells - LANES :], edge], axis=-1)

    return smooth(fh.shape[1], operand, ends_ref)


def contract(g, inv, num, den):
    u, p, m, s = g[0:3], g[3:9], g[9:15], g[15:21]
    rate = 4.0 * inv * strain_rate(s)
    scaled = [inv * x for x in u]
    for k in range(6):
        leonard = p[k] - scaled[LEAD_INDEX[k]] * u[TAIL_INDEX[k]]
        model = m[k] - rate * s[k]
        weighted = TENSOR_WEIGHTS[k] * model
        num = num + weighted * leonard
        den = den + weighted * model
    return num, den


def to_column(row_vector, size):
    shape = (size, LANES)
    eye = lax.broadcasted_iota(jnp.int32, shape, 0) == lane_iota(shape)
    return jnp.sum(jnp.where(eye, jnp.broadcast_to(row_vector, shape), 0.0), axis=1, keepdims=True)


def to_row(column_vector, row):
    return jnp.sum(jnp.where(row == lane_iota(row.shape), column_vector, 0.0), axis=0, keepdims=True)


def pad_lanes(x):
    return jnp.pad(x, ((0, 0), (0, LANES - x.shape[1])))


def stencil_holds(place, row, down, up, rows):
    gy = lax.axis_index("gy")
    lowest = jnp.maximum(row - down, -gy * rows)
    highest = jnp.minimum(row + up, (lax.axis_size("gy") - gy) * rows - 1)
    return (place >= lowest) & (place <= highest)


def end_rows(x):
    return jnp.concatenate([x[:HMAX], x[x.shape[0] - HMAX :]], axis=0)


def wall_block(g, own_ref, height_ref, inv_ref, stack, acc_ref, part_ref):
    rows = g[0].shape[0]
    width = 2 * LANES
    height = jnp.concatenate([height_ref[...], height_ref[...]], axis=1)
    mask = own_ref[:, : 2 * rows]
    for f in range(FIELDS):
        hi, lo = split2(g[f] * height)
        stack[0:rows, f * width : (f + 1) * width] = hi
        stack[rows:, f * width : (f + 1) * width] = lo
    merged = jnp.dot(mask, stack[...], preferred_element_type=F32)
    for f in range(FIELDS):
        part_ref[f, 0:HMAX, :] = merged[0:HMAX, f * width : (f + 1) * width]
        part_ref[f, HMAX:, :] = merged[rows - HMAX :, f * width : (f + 1) * width]
    for r in range(HMAX, rows - HMAX, HMAX):
        num = acc_ref[0, r : r + HMAX, :]
        den = acc_ref[1, r : r + HMAX, :]
        scale = inv_ref[r : r + HMAX, :]
        for c in range(2):
            parts = [
                merged[r : r + HMAX, f * width + c * LANES : f * width + (c + 1) * LANES] for f in range(FIELDS)
            ]
            num, den = contract(parts, scale, num, den)
        acc_ref[0, r : r + HMAX, :] = num
        acc_ref[1, r : r + HMAX, :] = den


def fields_early():
    gz = lax.axis_index("gz")
    return (gz == 0) | ((gz >= 8) & (gz % 4 < 2))


def filters_early():
    return lax.axis_index("gz") == 0


def own_fields(v_ref, s_ref, fh, fl):
    rows, cells = v_ref.shape[1:]
    for t in range(cells // LANES):
        at = slice(t * LANES, (t + 1) * LANES)
        for r in range(0, rows, 16):
            rr = slice(r, r + 16)

            def put_high(f, x):
                fh[f, rr, at] = x

            def put_low(f, x):
                fl[f, rr, at] = x

            store_fields(
                [v_ref[f, rr, at] for f in range(3)], [s_ref[f, rr, at] for f in range(6)], put_high, put_low
            )


def own_filters(pair_ref, fh, fl, inner):
    for n in range(inner.shape[0]):
        g = smooth_pair(n, fh, fl, pair_ref)
        for f in range(FIELDS):
            inner[n, f] = g[f]


def early_kernel(v_ref, s_ref, pair_ref, a, b, c, d, fh, fl, inner, *same):
    @pl.when(fields_early())
    def _():
        own_fields(v_ref, s_ref, fh, fl)

    @pl.when(filters_early())
    def _():
        own_filters(pair_ref, fh, fl, inner)


def late_kernel(v_ref, s_ref, pair_ref, a, b, c, fh, fl, inner):
    @pl.when(jnp.logical_not(fields_early()))
    def _():
        own_fields(v_ref, s_ref, fh, fl)

    @pl.when(jnp.logical_not(filters_early()))
    def _():
        own_filters(pair_ref, fh, fl, inner)


def wall_kernel(
    h_ref, reach_ref, inner, acc_ref, part_ref, own_ref, height_ref, inv_ref, mask_ref, total_ref, stack
):
    rows = h_ref.shape[1]
    ends = 2 * HMAX
    reach = pad_lanes(reach_ref[...].astype(F32))
    down = to_column(reach[0:1], rows).astype(jnp.int32)
    up = to_column(reach[1:2], rows).astype(jnp.int32)
    column = lane_iota((rows, 2 * LANES))
    row = lax.broadcasted_iota(jnp.int32, (rows, 2 * LANES), 0)
    place = jnp.where(column < rows, column, column - rows)
    inside = stencil_holds(place, row, down, up, rows)
    own_ref[...] = jnp.where(inside, 1.0, 0.0).astype(BF16)
    heights = pad_lanes(h_ref[...])
    height_ref[...] = jnp.broadcast_to(to_column(heights, rows), (rows, LANES))
    own = inside[:, :LANES] & (column[:, :LANES] < rows)
    total = jnp.sum(jnp.where(own, jnp.broadcast_to(heights, (rows, LANES)), 0.0), axis=1, keepdims=True)
    inv_ref[...] = jnp.broadcast_to(1.0 / total, (rows, LANES))
    total_ref[...] = jnp.broadcast_to(end_rows(total), (ends, LANES))
    column = lane_iota((ends, LANES))
    row = lax.broadcasted_iota(jnp.int32, (ends, LANES), 0)
    turn = column & (ends - 1)
    place = jnp.where(turn < HMAX, turn - HMAX, turn - HMAX + rows)
    row = jnp.where(row < HMAX, row, row + rows - ends)
    inside = stencil_holds(place, row, end_rows(down), end_rows(up), rows) & (column < 2 * ends)
    mask_ref[...] = jnp.where(inside, 1.0, 0.0)
    acc_ref[...] = jnp.zeros_like(acc_ref)
    for n in range(inner.shape[0]):
        g = [inner[n, f] for f in range(FIELDS)]
        wall_block(g, own_ref, height_ref, inv_ref, stack.at[n], acc_ref, part_ref.at[n])


def outer_kernel(
    fh, fl, znear, zfar, ynear, yfar, pair_ref, ends_ref, acc_in, own_ref, height_ref, inv_ref,
    sums_ref, part_ref, hh, hl, halo_inner, eh, el, stack, acc_ref,
):
    rows, cells = fh.shape[1:]
    gz_odd = lax.axis_index("gz") % 2 == 1
    gy_odd = lax.axis_index("gy") % 2 == 1
    acc_ref[...] = acc_in[...]
    edge_fields(jnp.where(gz_odd, znear[...], zfar[...]), jnp.where(gz_odd, zfar[...], znear[...]), eh, el)
    g_ends = smooth_ends(fh, fl, eh, el, ends_ref)
    for t in range(cells // LANES):
        at = slice(t * LANES, (t + 1) * LANES)

        def put_high(f, x):
            hh[f, :, at] = x

        def put_low(f, x):
            hl[f, :, at] = x

        raw = []
        for f in range(9):
            span = slice(f * cells + t * LANES, f * cells + (t + 1) * LANES)
            near, far = ynear[:, span], yfar[:, span]
            raw.append(jnp.concatenate([jnp.where(gy_odd, near, far), jnp.where(gy_odd, far, near)], axis=0))
        store_fields(raw[:3], raw[3:], put_high, put_low)
    for n in range(halo_inner.shape[0]):
        g = smooth_pair(n, hh, hl, pair_ref)
        for f in range(FIELDS):
            halo_inner[n, f] = g[f]
    wall_block(g_ends, own_ref, height_ref, inv_ref, stack, acc_ref, part_ref)
    inv = inv_ref[...]
    for k in range(2):
        plane_sums = jnp.sum(acc_ref[k] * (inv * inv), axis=1, keepdims=True)
        sums_ref[k : k + 1, :] = to_row(plane_sums, lax.broadcasted_iota(jnp.int32, (rows, LANES), 0))


def edge_fields(zl, zr, eh, el):
    rows = zl.shape[0]
    lane = lane_iota((16, LANES))
    middle = LANES // 2
    follows = (lane >= middle - NX) & (lane < middle)
    precedes = (lane >= middle) & (lane < middle + NX)
    for r in range(0, rows, 16):
        rr = slice(r, r + 16)
        raw = [
            jnp.where(
                follows,
                rot(zr[rr], middle - NX - NX * f),
                jnp.where(precedes, rot(zl[rr], middle - NX * f), 0.0),
            )
            for f in range(9)
        ]

        def put_high(f, x):
            eh[f, rr, :] = x

        def put_low(f, x):
            el[f, rr, :] = x

        store_fields(raw[:3], raw[3:], put_high, put_low)


def last_kernel(near_ref, far_ref, sums_in, part_inner, part_ends, mask_ref, total_ref, hh, hl, halo_inner, ends_ref, out_ref, eh, el, stack):
    rows = out_ref.shape[2]
    width = 2 * LANES
    gy_odd = lax.axis_index("gy") % 2 == 1
    both_rows = 2 * HMAX

    def halo(at):
        near, far = near_ref[:, at], far_ref[:, at]
        return jnp.concatenate([jnp.where(gy_odd, near, far), jnp.where(gy_odd, far, near)], axis=0)

    zl = halo(slice(0, LANES))
    zr = halo(slice(LANES, 2 * LANES))
    below = rot(zl[:HMAX], -9 * NX)[0:1]
    above = rot(zl[HMAX:], -9 * NX)[0:1]
    height = jnp.concatenate([to_column(below, HMAX), to_column(above, HMAX)], axis=0)
    lane = lane_iota((both_rows, LANES))
    heights = jnp.where(lane[0:1] < HMAX, below, rot(above, HMAX))
    outside = jnp.where(lane < both_rows, mask_ref[...] * heights, 0.0)
    inv = 1.0 / (total_ref[...] + jnp.sum(outside, axis=1, keepdims=True))
    scale = [inv[:HMAX], inv[HMAX:]]
    mask = mask_ref[:, : 2 * both_rows].astype(BF16)

    edge_fields(zl, zr, eh, el)
    zero = jnp.zeros((HMAX, LANES), F32)
    sums = [[zero, zero], [zero, zero]]
    blocks = halo_inner.shape[0]
    g_ends = smooth_ends(hh, hl, eh, el, ends_ref)
    for n in range(blocks + 1):
        if n < blocks:
            g = [halo_inner[n, f] for f in range(FIELDS)]
            part = part_inner.at[n]
        else:
            part = part_ends
            g = g_ends
        for f in range(FIELDS):
            hi, lo = split2(g[f] * height)
            stack[n, 0:both_rows, f * width : (f + 1) * width] = hi
            stack[n, both_rows:, f * width : (f + 1) * width] = lo
        merged = jnp.dot(mask, stack[n], preferred_element_type=F32)
        for i in range(2):
            rr = slice(i * HMAX, (i + 1) * HMAX)
            for c in range(2):
                at = slice(c * LANES, (c + 1) * LANES)
                values = [
                    part[f, rr, at] + merged[rr, f * width + c * LANES : f * width + (c + 1) * LANES]
                    for f in range(FIELDS)
                ]
                sums[i] = list(contract(values, scale[i], *sums[i]))
    row = lax.broadcasted_iota(jnp.int32, (both_rows, LANES), 0)
    row = jnp.where(row < HMAX, row, row + rows - both_rows)
    for k in range(2):
        values = jnp.concatenate([sums[0][k], sums[1][k]], axis=0) * (inv * inv)
        total = sums_in[k : k + 1, :] + to_row(jnp.sum(values, axis=1, keepdims=True), row)
        out_ref[:, k : k + 1, :] = jnp.broadcast_to(total[None, :, :rows], (out_ref.shape[0], 1, rows))


def call(kernel, out_shape, scratch, limit, *operands, aliases=None):
    vmem = pl.BlockSpec(memory_space=pltpu.VMEM)
    return pl.pallas_call(
        kernel,
        in_specs=[vmem] * len(operands),
        out_specs=jax.tree.map(lambda _: vmem, out_shape),
        out_shape=out_shape,
        scratch_shapes=scratch,
        input_output_aliases=aliases or {},
        compiler_params=pltpu.CompilerParams(vmem_limit_bytes=limit),
        cost_estimate=pl.CostEstimate(flops=4 * 10**9, bytes_accessed=2**20, transcendentals=0),
    )(*operands)


def local(velocity, strain, cell_height, stencil_reach):
    rows, cells = velocity.shape[1:]
    width = 2 * LANES
    blocks = cells // width - 1
    ends = 2 * HMAX
    shape = jax.ShapeDtypeStruct
    heights = cell_height.reshape(1, rows)
    near, far, wall_near, wall_far, velocity, strain, pair, both_ends = first_call(velocity, strain)
    own_work = [
        shape((FIELDS, rows, cells), BF16),
        shape((WIDE, rows, cells), BF16),
        shape((blocks, FIELDS, rows, width), F32),
    ]
    messages = (near, far, wall_near, wall_far)
    fh, fl, inner, near, far, wall_near, wall_far = call(
        early_kernel,
        own_work + [shape(x.shape, x.dtype) for x in messages],
        [],
        LARGE_VMEM,
        velocity,
        strain,
        pair,
        *messages,
        aliases={3 + i: 3 + i for i in range(4)},
    )
    znear = lax.ppermute(near, "gz", near_pairs("gz"))
    zfar = lax.ppermute(far, "gz", far_pairs("gz", True))
    yfar = lax.ppermute(wall_far, "gy", far_pairs("gy", False))
    ynear = lax.ppermute(wall_near, "gy", near_pairs("gy"))
    fh, fl, inner = call(
        late_kernel,
        own_work,
        [],
        LARGE_VMEM,
        velocity,
        strain,
        pair,
        fh,
        fl,
        inner,
        aliases={3 + i: i for i in range(3)},
    )
    acc, part_inner, own, height, inv, mask, totals = call(
        wall_kernel,
        [
            shape((2, rows, LANES), F32),
            shape((blocks, FIELDS, ends, width), F32),
            shape((rows, width), BF16),
            shape((rows, LANES), F32),
            shape((rows, LANES), F32),
            shape((ends, LANES), F32),
            shape((ends, LANES), F32),
        ],
        [pltpu.VMEM((blocks, 2 * rows, FIELDS * width), BF16)],
        LARGE_VMEM,
        heights,
        stencil_reach,
        inner,
    )
    near, far = corner_call(heights, znear, zfar)
    corner_far = lax.ppermute(far, "gy", far_pairs("gy", False))
    corner_near = lax.ppermute(near, "gy", near_pairs("gy"))
    sums, part_ends, hh, hl, halo_inner = call(
        outer_kernel,
        [
            shape((2, LANES), F32),
            shape((FIELDS, ends, width), F32),
            shape((FIELDS, ends, cells), BF16),
            shape((WIDE, ends, cells), BF16),
            shape((blocks, FIELDS, ends, width), F32),
        ],
        [
            pltpu.VMEM((FIELDS, rows, LANES), BF16),
            pltpu.VMEM((WIDE, rows, LANES), BF16),
            pltpu.VMEM((2 * rows, FIELDS * width), BF16),
            pltpu.VMEM((2, rows, LANES), F32),
        ],
        LARGE_VMEM,
        fh,
        fl,
        znear,
        zfar,
        ynear,
        yfar,
        pair,
        both_ends,
        acc,
        own,
        height,
        inv,
    )
    sums = call(
        last_kernel,
        shape((lax.axis_size("gz"), 2, rows), F32),
        [
            pltpu.VMEM((FIELDS, ends, LANES), BF16),
            pltpu.VMEM((WIDE, ends, LANES), BF16),
            pltpu.VMEM((blocks + 1, 2 * ends, FIELDS * width), BF16),
        ],
        LARGE_VMEM,
        corner_near,
        corner_far,
        sums,
        part_inner,
        part_ends,
        mask,
        totals,
        hh,
        hl,
        halo_inner,
        both_ends,
    )
    sums = jnp.sum(lax.all_to_all(sums, "gz", 0, 0), axis=0)
    total = lax.axis_size("gz") * cells
    return sums[0] / total / (sums[1] / total + 1e-06)


def near_pairs(axis):
    return [(i, i ^ 1) for i in range(lax.axis_size(axis))]


def far_pairs(axis, closed):
    n = lax.axis_size(axis)
    pairs = []
    for i in range(1, n if closed else n - 1, 2):
        pairs += [(i, (i + 1) % n), ((i + 1) % n, i)]
    return pairs


def solution(mesh):
    in_specs = (P(None, "gy", "gz"), P(None, "gy", "gz"), P("gy"), P(None, "gy"))
    return jax.shard_map(local, mesh=mesh, in_specs=in_specs, out_specs=P("gy"), check_vma=False)
```

```python
import jax
import jax.numpy as jnp
from jax import lax
from jax.experimental import pallas as pl
from jax.experimental.pallas import tpu as pltpu
from jax.sharding import PartitionSpec as P

NX = 8
HMAX = 8
LANES = 128
FIELDS = 21
WIDE = 15
FIRST_VMEM = 51 * 1024 * 1024
SMALL_VMEM = 24 * 1024 * 1024
LARGE_VMEM = 24 * 1024 * 1024
LEAD_INDEX = (0, 1, 2, 0, 0, 1)
TAIL_INDEX = (0, 1, 2, 1, 2, 2)
TENSOR_WEIGHTS = (1.0, 1.0, 1.0, 2.0, 2.0, 2.0)
F32 = jnp.float32
BF16 = jnp.bfloat16


def strain_rate(s):
    squares = 2.0 * (s[0] * s[0] + s[1] * s[1] + s[2] * s[2])
    squares = squares + 4.0 * (s[3] * s[3] + s[4] * s[4] + s[5] * s[5])
    return jnp.sqrt(squares)


def lane_iota(shape):
    return lax.broadcasted_iota(jnp.int32, shape, len(shape) - 1)


def rot(x, amount):
    amount = amount % LANES
    return pltpu.roll(x, amount, x.ndim - 1) if amount else x


def cell_weights(source, target):
    turn = (source - target) & (NX - 1)
    along = jnp.where(turn == 0, 0.5, jnp.where((turn == 1) | (turn == NX - 1), 0.25, 0.0))
    step = ((source + LANES) >> 3) - ((target + LANES) >> 3)
    across = jnp.where(step == 0, 0.5, jnp.where((step == 1) | (step == -1), 0.25, 0.0))
    return along * across


def pair_filter():
    shape = (3 * LANES, 2 * LANES)
    k = lax.broadcasted_iota(jnp.int32, shape, 0)
    return cell_weights(jnp.where(k < 5 * LANES // 2, k, k - 3 * LANES), lane_iota(shape)).astype(BF16)


def ends_filter():
    shape = (3 * LANES, 2 * LANES)
    k = lax.broadcasted_iota(jnp.int32, shape, 0)
    m = lane_iota(shape)
    place = k & (LANES - 1)
    middle = LANES // 2
    outer = k >= 2 * LANES
    last = place >= LANES - NX
    after = (place >= middle - NX) & (place < middle)
    before = (place >= middle) & (place < middle + NX)
    used = (place < NX) | last | after | before
    shift = jnp.where(last, -LANES, jnp.where(after, LANES - middle + NX, jnp.where(before, -middle - NX, LANES)))
    source = jnp.where(outer, place + shift, place)
    tile = jnp.where(outer, jnp.where(last | after, 1, 0), k >> 7)
    fits = (tile == (m >> 7)) & (used | (k < 2 * LANES))
    return jnp.where(fits, cell_weights(source, m & (LANES - 1)), 0.0).astype(BF16)


def first_kernel(v_ref, s_ref, near_ref, far_ref, wall_near, wall_far, v_out, s_out, pair_ref, ends_ref, sems):
    rows, cells = v_ref.shape[1:]
    spans = ((0, LANES), (cells - LANES, LANES), (LANES, cells - 2 * LANES))
    copies = []
    for i, (start, size) in enumerate(spans):
        for j, (ref, out) in enumerate(((v_ref, v_out), (s_ref, s_out))):
            at = pl.ds(start, size)
            copies.append(pltpu.make_async_copy(ref.at[:, :, at], out.at[:, :, at], sems.at[i, j]))
    for copy in copies:
        copy.start()
    pair_ref[...] = pair_filter()
    ends_ref[...] = ends_filter()
    for copy in copies[:4]:
        copy.wait()
    lane = lane_iota((rows, LANES))
    left = jnp.zeros((rows, LANES), F32)
    right = jnp.zeros((rows, LANES), F32)
    for f in range(9):
        ref, at = (v_out, f) if f < 3 else (s_out, f - 3)
        here = (lane >= NX * f) & (lane < NX * (f + 1))
        left = jnp.where(here, rot(ref[at, :, :LANES].astype(F32), NX * f), left)
        right = jnp.where(here, rot(ref[at, :, cells - LANES :].astype(F32), NX * f + NX), right)
    odd = lax.axis_index("gz") % 2 == 1
    near_ref[...] = jnp.where(odd, left, right)
    far_ref[...] = jnp.where(odd, right, left)
    for copy in copies[4:]:
        copy.wait()
    gy_odd = lax.axis_index("gy") % 2 == 1
    for f in range(9):
        at = slice(f * cells, (f + 1) * cells)
        if f < 3:
            low, high = v_out[f, :HMAX, :], v_out[f, rows - HMAX :, :]
        else:
            low = s_out[f - 3, : 2 * HMAX, :].astype(F32)[:HMAX]
            high = s_out[f - 3, rows - 2 * HMAX :, :].astype(F32)[HMAX:]
        wall_near[:, at] = jnp.where(gy_odd, low, high)
        wall_far[:, at] = jnp.where(gy_odd, high, low)


def first_call(velocity, strain):
    rows, cells = velocity.shape[1:]
    hbm = pl.BlockSpec(memory_space=pltpu.HBM)
    vmem = pl.BlockSpec(memory_space=pltpu.VMEM)
    shape = jax.ShapeDtypeStruct
    return pl.pallas_call(
        first_kernel,
        in_specs=[hbm] * 2,
        out_specs=[vmem] * 8,
        out_shape=[shape((rows, LANES), F32)] * 2
        + [shape((HMAX, 9 * cells), F32)] * 2
        + [shape(x.shape, x.dtype) for x in (velocity, strain)]
        + [shape((3 * LANES, 2 * LANES), BF16)] * 2,
        scratch_shapes=[pltpu.SemaphoreType.DMA((3, 2))],
        compiler_params=pltpu.CompilerParams(vmem_limit_bytes=FIRST_VMEM),
    )(velocity, strain)


def corner_kernel(h_ref, znear, zfar, near_ref, far_ref):
    rows = znear.shape[0]
    gz_odd = lax.axis_index("gz") % 2 == 1
    gy_odd = lax.axis_index("gy") % 2 == 1
    lane = lane_iota((HMAX, LANES))
    row = lax.broadcasted_iota(jnp.int32, (HMAX, LANES), 0)
    stamp = (row == 0) & (lane >= 9 * NX) & (lane < 10 * NX)
    heights = jnp.broadcast_to(jnp.pad(h_ref[...], ((0, 0), (0, LANES - rows))), (HMAX, LANES))
    sides = []
    for r0 in (0, rows - HMAX):
        zn = znear[r0 : r0 + HMAX, :]
        zf = zfar[r0 : r0 + HMAX, :]
        zl = jnp.where(stamp, rot(heights, 9 * NX - r0), jnp.where(gz_odd, zn, zf))
        sides.append((zl, jnp.where(gz_odd, zf, zn)))
    (low_left, low_right), (high_left, high_right) = sides
    near_ref[:, :LANES] = jnp.where(gy_odd, low_left, high_left)
    near_ref[:, LANES:] = jnp.where(gy_odd, low_right, high_right)
    far_ref[:, :LANES] = jnp.where(gy_odd, high_left, low_left)
    far_ref[:, LANES:] = jnp.where(gy_odd, high_right, low_right)


def corner_call(heights, znear, zfar):
    vmem = pl.BlockSpec(memory_space=pltpu.VMEM)
    return pl.pallas_call(
        corner_kernel,
        in_specs=[vmem] * 3,
        out_specs=[vmem] * 2,
        out_shape=[jax.ShapeDtypeStruct((HMAX, 2 * LANES), F32)] * 2,
        compiler_params=pltpu.CompilerParams(vmem_limit_bytes=SMALL_VMEM),
    )(heights, znear, zfar)


def split2(x):
    hi = x.astype(BF16)
    return hi, (x - hi.astype(F32)).astype(BF16)


def store_fields(u, s, put_high, put_low):
    tensor = [x.astype(F32) for x in s]
    rate = strain_rate(tensor)
    wide = u + [u[a] * u[b] for a, b in zip(LEAD_INDEX, TAIL_INDEX)] + [rate * x for x in tensor]
    for f, value in enumerate(wide):
        hi, lo = split2(value)
        put_high(f, hi)
        put_low(f, lo)
    for f, value in enumerate(s):
        put_high(WIDE + f, value.astype(BF16))


def smooth(rows, operand, matrix_ref):
    wide, narrow = slice(0, WIDE), slice(WIDE, FIELDS)
    lhs = jnp.concatenate([operand(True, wide), operand(False, wide)], axis=-1).reshape(WIDE * rows, -1)
    matrix = matrix_ref[...]
    first = jnp.dot(lhs, jnp.concatenate([matrix, matrix], axis=0), preferred_element_type=F32)
    lhs = operand(True, narrow).reshape((FIELDS - WIDE) * rows, -1)
    second = jnp.dot(lhs, matrix, preferred_element_type=F32)
    return [first[f * rows : (f + 1) * rows] for f in range(WIDE)] + [
        second[f * rows : (f + 1) * rows] for f in range(FIELDS - WIDE)
    ]


def pick(after, before):
    return jnp.where(lane_iota(after.shape) < LANES // 2, after, before)


def smooth_pair(n, fh, fl, pair_ref):
    def operand(high, fields):
        ref = fh if high else fl
        tile = [ref[fields, :, (2 * n + i) * LANES : (2 * n + i + 1) * LANES] for i in range(4)]
        return jnp.concatenate([tile[1], tile[2], pick(tile[3], tile[0])], axis=-1)

    return smooth(fh.shape[1], operand, pair_ref)


def smooth_ends(fh, fl, eh, el, ends_ref):
    cells = fh.shape[2]

    def operand(high, fields):
        ref, outer = (fh, eh) if high else (fl, el)
        second = ref[fields, :, LANES : 2 * LANES]
        ahead = ref[fields, :, cells - 2 * LANES : cells - LANES]
        lane = lane_iota(second.shape)
        edge = jnp.where(lane < NX, second, jnp.where(lane >= LANES - NX, ahead, outer[fields]))
        return jnp.concatenate([ref[fields, :, :LANES], ref[fields, :, cells - LANES :], edge], axis=-1)

    return smooth(fh.shape[1], operand, ends_ref)


def contract(g, inv, num, den):
    u, p, m, s = g[0:3], g[3:9], g[9:15], g[15:21]
    rate = 4.0 * inv * strain_rate(s)
    scaled = [inv * x for x in u]
    for k in range(6):
        leonard = p[k] - scaled[LEAD_INDEX[k]] * u[TAIL_INDEX[k]]
        model = m[k] - rate * s[k]
        weighted = TENSOR_WEIGHTS[k] * model
        num = num + weighted * leonard
        den = den + weighted * model
    return num, den


def to_column(row_vector, size):
    shape = (size, LANES)
    eye = lax.broadcasted_iota(jnp.int32, shape, 0) == lane_iota(shape)
    return jnp.sum(jnp.where(eye, jnp.broadcast_to(row_vector, shape), 0.0), axis=1, keepdims=True)


def to_row(column_vector, row):
    return jnp.sum(jnp.where(row == lane_iota(row.shape), column_vector, 0.0), axis=0, keepdims=True)


def pad_lanes(x):
    return jnp.pad(x, ((0, 0), (0, LANES - x.shape[1])))


def stencil_holds(place, row, down, up, rows):
    gy = lax.axis_index("gy")
    lowest = jnp.maximum(row - down, -gy * rows)
    highest = jnp.minimum(row + up, (lax.axis_size("gy") - gy) * rows - 1)
    return (place >= lowest) & (place <= highest)


def end_rows(x):
    return jnp.concatenate([x[:HMAX], x[x.shape[0] - HMAX :]], axis=0)


def wall_block(g, own_ref, height_ref, inv_ref, stack, acc_ref, part_ref):
    rows = g[0].shape[0]
    width = 2 * LANES
    height = jnp.concatenate([height_ref[...], height_ref[...]], axis=1)
    mask = own_ref[:, : 2 * rows]
    for f in range(FIELDS):
        hi, lo = split2(g[f] * height)
        stack[0:rows, f * width : (f + 1) * width] = hi
        stack[rows:, f * width : (f + 1) * width] = lo
    merged = jnp.dot(mask, stack[...], preferred_element_type=F32)
    for f in range(FIELDS):
        part_ref[f, 0:HMAX, :] = merged[0:HMAX, f * width : (f + 1) * width]
        part_ref[f, HMAX:, :] = merged[rows - HMAX :, f * width : (f + 1) * width]
    for r in range(HMAX, rows - HMAX, HMAX):
        num = acc_ref[0, r : r + HMAX, :]
        den = acc_ref[1, r : r + HMAX, :]
        scale = inv_ref[r : r + HMAX, :]
        for c in range(2):
            parts = [
                merged[r : r + HMAX, f * width + c * LANES : f * width + (c + 1) * LANES] for f in range(FIELDS)
            ]
            num, den = contract(parts, scale, num, den)
        acc_ref[0, r : r + HMAX, :] = num
        acc_ref[1, r : r + HMAX, :] = den


def fields_early():
    gz = lax.axis_index("gz")
    return (gz == 0) | (gz == 9)


def filters_early():
    return lax.axis_index("gz") == 0


def own_fields(v_ref, s_ref, fh, fl):
    rows, cells = v_ref.shape[1:]
    for t in range(cells // LANES):
        at = slice(t * LANES, (t + 1) * LANES)
        for r in range(0, rows, 16):
            rr = slice(r, r + 16)

            def put_high(f, x):
                fh[f, rr, at] = x

            def put_low(f, x):
                fl[f, rr, at] = x

            store_fields(
                [v_ref[f, rr, at] for f in range(3)], [s_ref[f, rr, at] for f in range(6)], put_high, put_low
            )


def own_filters(pair_ref, fh, fl, inner):
    for n in range(inner.shape[0]):
        g = smooth_pair(n, fh, fl, pair_ref)
        for f in range(FIELDS):
            inner[n, f] = g[f]


def early_kernel(v_ref, s_ref, pair_ref, a, b, c, d, fh, fl, inner, *same):
    @pl.when(fields_early())
    def _():
        own_fields(v_ref, s_ref, fh, fl)

    @pl.when(filters_early())
    def _():
        own_filters(pair_ref, fh, fl, inner)


def late_kernel(v_ref, s_ref, pair_ref, a, b, c, fh, fl, inner):
    @pl.when(jnp.logical_not(fields_early()))
    def _():
        own_fields(v_ref, s_ref, fh, fl)

    @pl.when(jnp.logical_not(filters_early()))
    def _():
        own_filters(pair_ref, fh, fl, inner)


def wall_kernel(
    h_ref, reach_ref, inner, acc_ref, part_ref, own_ref, height_ref, inv_ref, mask_ref, total_ref, stack
):
    rows = h_ref.shape[1]
    ends = 2 * HMAX
    reach = pad_lanes(reach_ref[...].astype(F32))
    down = to_column(reach[0:1], rows).astype(jnp.int32)
    up = to_column(reach[1:2], rows).astype(jnp.int32)
    column = lane_iota((rows, 2 * LANES))
    row = lax.broadcasted_iota(jnp.int32, (rows, 2 * LANES), 0)
    place = jnp.where(column < rows, column, column - rows)
    inside = stencil_holds(place, row, down, up, rows)
    own_ref[...] = jnp.where(inside, 1.0, 0.0).astype(BF16)
    heights = pad_lanes(h_ref[...])
    height_ref[...] = jnp.broadcast_to(to_column(heights, rows), (rows, LANES))
    own = inside[:, :LANES] & (column[:, :LANES] < rows)
    total = jnp.sum(jnp.where(own, jnp.broadcast_to(heights, (rows, LANES)), 0.0), axis=1, keepdims=True)
    inv_ref[...] = jnp.broadcast_to(1.0 / total, (rows, LANES))
    total_ref[...] = jnp.broadcast_to(end_rows(total), (ends, LANES))
    column = lane_iota((ends, LANES))
    row = lax.broadcasted_iota(jnp.int32, (ends, LANES), 0)
    turn = column & (ends - 1)
    place = jnp.where(turn < HMAX, turn - HMAX, turn - HMAX + rows)
    row = jnp.where(row < HMAX, row, row + rows - ends)
    inside = stencil_holds(place, row, end_rows(down), end_rows(up), rows) & (column < 2 * ends)
    mask_ref[...] = jnp.where(inside, 1.0, 0.0)
    acc_ref[...] = jnp.zeros_like(acc_ref)
    for n in range(inner.shape[0]):
        g = [inner[n, f] for f in range(FIELDS)]
        wall_block(g, own_ref, height_ref, inv_ref, stack.at[n], acc_ref, part_ref.at[n])


def outer_kernel(
    fh, fl, znear, zfar, ynear, yfar, pair_ref, ends_ref, acc_in, own_ref, height_ref, inv_ref,
    sums_ref, part_ref, hh, hl, halo_inner, eh, el, stack, acc_ref,
):
    rows, cells = fh.shape[1:]
    gz_odd = lax.axis_index("gz") % 2 == 1
    gy_odd = lax.axis_index("gy") % 2 == 1
    acc_ref[...] = acc_in[...]
    edge_fields(jnp.where(gz_odd, znear[...], zfar[...]), jnp.where(gz_odd, zfar[...], znear[...]), eh, el)
    g_ends = smooth_ends(fh, fl, eh, el, ends_ref)
    for t in range(cells // LANES):
        at = slice(t * LANES, (t + 1) * LANES)

        def put_high(f, x):
            hh[f, :, at] = x

        def put_low(f, x):
            hl[f, :, at] = x

        raw = []
        for f in range(9):
            span = slice(f * cells + t * LANES, f * cells + (t + 1) * LANES)
            near, far = ynear[:, span], yfar[:, span]
            raw.append(jnp.concatenate([jnp.where(gy_odd, near, far), jnp.where(gy_odd, far, near)], axis=0))
        store_fields(raw[:3], raw[3:], put_high, put_low)
    for n in range(halo_inner.shape[0]):
        g = smooth_pair(n, hh, hl, pair_ref)
        for f in range(FIELDS):
            halo_inner[n, f] = g[f]
    wall_block(g_ends, own_ref, height_ref, inv_ref, stack, acc_ref, part_ref)
    inv = inv_ref[...]
    for k in range(2):
        plane_sums = jnp.sum(acc_ref[k] * (inv * inv), axis=1, keepdims=True)
        sums_ref[k : k + 1, :] = to_row(plane_sums, lax.broadcasted_iota(jnp.int32, (rows, LANES), 0))


def edge_fields(zl, zr, eh, el):
    rows = zl.shape[0]
    lane = lane_iota((16, LANES))
    middle = LANES // 2
    follows = (lane >= middle - NX) & (lane < middle)
    precedes = (lane >= middle) & (lane < middle + NX)
    for r in range(0, rows, 16):
        rr = slice(r, r + 16)
        raw = [
            jnp.where(
                follows,
                rot(zr[rr], middle - NX - NX * f),
                jnp.where(precedes, rot(zl[rr], middle - NX * f), 0.0),
            )
            for f in range(9)
        ]

        def put_high(f, x):
            eh[f, rr, :] = x

        def put_low(f, x):
            el[f, rr, :] = x

        store_fields(raw[:3], raw[3:], put_high, put_low)


def last_kernel(far_ref, near_ref, sums_in, part_inner, part_ends, mask_ref, total_ref, hh, hl, halo_inner, ends_ref, out_ref, eh, el, stack):
    rows = out_ref.shape[2]
    width = 2 * LANES
    gy_odd = lax.axis_index("gy") % 2 == 1
    both_rows = 2 * HMAX

    def halo(at):
        near, far = near_ref[:, at], far_ref[:, at]
        return jnp.concatenate([jnp.where(gy_odd, near, far), jnp.where(gy_odd, far, near)], axis=0)

    zl = halo(slice(0, LANES))
    zr = halo(slice(LANES, 2 * LANES))
    below = rot(zl[:HMAX], -9 * NX)[0:1]
    above = rot(zl[HMAX:], -9 * NX)[0:1]
    height = jnp.concatenate([to_column(below, HMAX), to_column(above, HMAX)], axis=0)
    lane = lane_iota((both_rows, LANES))
    heights = jnp.where(lane[0:1] < HMAX, below, rot(above, HMAX))
    outside = jnp.where(lane < both_rows, mask_ref[...] * heights, 0.0)
    inv = 1.0 / (total_ref[...] + jnp.sum(outside, axis=1, keepdims=True))
    scale = [inv[:HMAX], inv[HMAX:]]
    mask = mask_ref[:, : 2 * both_rows].astype(BF16)

    edge_fields(zl, zr, eh, el)
    zero = jnp.zeros((HMAX, LANES), F32)
    sums = [[zero, zero], [zero, zero]]
    blocks = halo_inner.shape[0]
    g_ends = smooth_ends(hh, hl, eh, el, ends_ref)
    for n in range(blocks + 1):
        if n < blocks:
            g = [halo_inner[n, f] for f in range(FIELDS)]
            part = part_inner.at[n]
        else:
            part = part_ends
            g = g_ends
        for f in range(FIELDS):
            hi, lo = split2(g[f] * height)
            stack[n, 0:both_rows, f * width : (f + 1) * width] = hi
            stack[n, both_rows:, f * width : (f + 1) * width] = lo
        merged = jnp.dot(mask, stack[n], preferred_element_type=F32)
        for i in range(2):
            rr = slice(i * HMAX, (i + 1) * HMAX)
            for c in range(2):
                at = slice(c * LANES, (c + 1) * LANES)
                values = [
                    part[f, rr, at] + merged[rr, f * width + c * LANES : f * width + (c + 1) * LANES]
                    for f in range(FIELDS)
                ]
                sums[i] = list(contract(values, scale[i], *sums[i]))
    row = lax.broadcasted_iota(jnp.int32, (both_rows, LANES), 0)
    row = jnp.where(row < HMAX, row, row + rows - both_rows)
    for k in range(2):
        values = jnp.concatenate([sums[0][k], sums[1][k]], axis=0) * (inv * inv)
        total = sums_in[k : k + 1, :] + to_row(jnp.sum(values, axis=1, keepdims=True), row)
        out_ref[:, k : k + 1, :] = jnp.broadcast_to(total[None, :, :rows], (out_ref.shape[0], 1, rows))


def call(kernel, out_shape, scratch, limit, *operands, aliases=None):
    vmem = pl.BlockSpec(memory_space=pltpu.VMEM)
    return pl.pallas_call(
        kernel,
        in_specs=[vmem] * len(operands),
        out_specs=jax.tree.map(lambda _: vmem, out_shape),
        out_shape=out_shape,
        scratch_shapes=scratch,
        input_output_aliases=aliases or {},
        compiler_params=pltpu.CompilerParams(vmem_limit_bytes=limit),
        cost_estimate=pl.CostEstimate(flops=4 * 10**9, bytes_accessed=2**20, transcendentals=0),
    )(*operands)


def local(velocity, strain, cell_height, stencil_reach):
    rows, cells = velocity.shape[1:]
    width = 2 * LANES
    blocks = cells // width - 1
    ends = 2 * HMAX
    shape = jax.ShapeDtypeStruct
    heights = cell_height.reshape(1, rows)
    near, far, wall_near, wall_far, velocity, strain, pair, both_ends = first_call(velocity, strain)
    own_work = [
        shape((FIELDS, rows, cells), BF16),
        shape((WIDE, rows, cells), BF16),
        shape((blocks, FIELDS, rows, width), F32),
    ]
    messages = (near, far, wall_near, wall_far)
    fh, fl, inner, near, far, wall_near, wall_far = call(
        early_kernel,
        own_work + [shape(x.shape, x.dtype) for x in messages],
        [],
        LARGE_VMEM,
        velocity,
        strain,
        pair,
        *messages,
        aliases={3 + i: 3 + i for i in range(4)},
    )
    znear = lax.ppermute(near, "gz", near_pairs("gz"))
    zfar = lax.ppermute(far, "gz", far_pairs("gz", True))
    yfar = lax.ppermute(wall_far, "gy", far_pairs("gy", False))
    ynear = lax.ppermute(wall_near, "gy", near_pairs("gy"))
    fh, fl, inner = call(
        late_kernel,
        own_work,
        [],
        LARGE_VMEM,
        velocity,
        strain,
        pair,
        fh,
        fl,
        inner,
        aliases={3 + i: i for i in range(3)},
    )
    acc, part_inner, own, height, inv, mask, totals = call(
        wall_kernel,
        [
            shape((2, rows, LANES), F32),
            shape((blocks, FIELDS, ends, width), F32),
            shape((rows, width), BF16),
            shape((rows, LANES), F32),
            shape((rows, LANES), F32),
            shape((ends, LANES), F32),
            shape((ends, LANES), F32),
        ],
        [pltpu.VMEM((blocks, 2 * rows, FIELDS * width), BF16)],
        LARGE_VMEM,
        heights,
        stencil_reach,
        inner,
    )
    near, far = corner_call(heights, znear, zfar)
    corner_far = lax.ppermute(far, "gy", far_pairs("gy", False))
    corner_near = lax.ppermute(near, "gy", near_pairs("gy"))
    sums, part_ends, hh, hl, halo_inner = call(
        outer_kernel,
        [
            shape((2, LANES), F32),
            shape((FIELDS, ends, width), F32),
            shape((FIELDS, ends, cells), BF16),
            shape((WIDE, ends, cells), BF16),
            shape((blocks, FIELDS, ends, width), F32),
        ],
        [
            pltpu.VMEM((FIELDS, rows, LANES), BF16),
            pltpu.VMEM((WIDE, rows, LANES), BF16),
            pltpu.VMEM((2 * rows, FIELDS * width), BF16),
            pltpu.VMEM((2, rows, LANES), F32),
        ],
        LARGE_VMEM,
        fh,
        fl,
        znear,
        zfar,
        ynear,
        yfar,
        pair,
        both_ends,
        acc,
        own,
        height,
        inv,
    )
    sums = call(
        last_kernel,
        shape((lax.axis_size("gz"), 2, rows), F32),
        [
            pltpu.VMEM((FIELDS, ends, LANES), BF16),
            pltpu.VMEM((WIDE, ends, LANES), BF16),
            pltpu.VMEM((blocks + 1, 2 * ends, FIELDS * width), BF16),
        ],
        LARGE_VMEM,
        corner_far,
        corner_near,
        sums,
        part_inner,
        part_ends,
        mask,
        totals,
        hh,
        hl,
        halo_inner,
        both_ends,
    )
    sums = jnp.sum(lax.all_to_all(sums, "gz", 0, 0), axis=0)
    total = lax.axis_size("gz") * cells
    return sums[0] / total / (sums[1] / total + 1e-06)


def near_pairs(axis):
    return [(i, i ^ 1) for i in range(lax.axis_size(axis))]


def far_pairs(axis, closed):
    n = lax.axis_size(axis)
    pairs = []
    for i in range(1, n if closed else n - 1, 2):
        pairs += [(i, (i + 1) % n), ((i + 1) % n, i)]
    return pairs


def solution(mesh):
    in_specs = (P(None, "gy", "gz"), P(None, "gy", "gz"), P("gy"), P(None, "gy"))
    return jax.shard_map(local, mesh=mesh, in_specs=in_specs, out_specs=P("gy"), check_vma=False)
```

```python
import jax
import jax.numpy as jnp
from jax import lax
from jax.experimental import pallas as pl
from jax.experimental.pallas import tpu as pltpu
from jax.sharding import PartitionSpec as P

NX = 8
HMAX = 8
LANES = 128
FIELDS = 21
WIDE = 15
FIRST_VMEM = 51 * 1024 * 1024
SMALL_VMEM = 24 * 1024 * 1024
LARGE_VMEM = 24 * 1024 * 1024
LEAD_INDEX = (0, 1, 2, 0, 0, 1)
TAIL_INDEX = (0, 1, 2, 1, 2, 2)
TENSOR_WEIGHTS = (1.0, 1.0, 1.0, 2.0, 2.0, 2.0)
F32 = jnp.float32
BF16 = jnp.bfloat16


def strain_rate(s):
    squares = 2.0 * (s[0] * s[0] + s[1] * s[1] + s[2] * s[2])
    squares = squares + 4.0 * (s[3] * s[3] + s[4] * s[4] + s[5] * s[5])
    return jnp.sqrt(squares)


def lane_iota(shape):
    return lax.broadcasted_iota(jnp.int32, shape, len(shape) - 1)


def rot(x, amount):
    amount = amount % LANES
    return pltpu.roll(x, amount, x.ndim - 1) if amount else x


def cell_weights(source, target):
    turn = (source - target) & (NX - 1)
    along = jnp.where(turn == 0, 0.5, jnp.where((turn == 1) | (turn == NX - 1), 0.25, 0.0))
    step = ((source + LANES) >> 3) - ((target + LANES) >> 3)
    across = jnp.where(step == 0, 0.5, jnp.where((step == 1) | (step == -1), 0.25, 0.0))
    return along * across


def pair_filter():
    shape = (3 * LANES, 2 * LANES)
    k = lax.broadcasted_iota(jnp.int32, shape, 0)
    return cell_weights(jnp.where(k < 5 * LANES // 2, k, k - 3 * LANES), lane_iota(shape)).astype(BF16)


def ends_filter():
    shape = (3 * LANES, 2 * LANES)
    k = lax.broadcasted_iota(jnp.int32, shape, 0)
    m = lane_iota(shape)
    place = k & (LANES - 1)
    middle = LANES // 2
    outer = k >= 2 * LANES
    last = place >= LANES - NX
    after = (place >= middle - NX) & (place < middle)
    before = (place >= middle) & (place < middle + NX)
    used = (place < NX) | last | after | before
    shift = jnp.where(last, -LANES, jnp.where(after, LANES - middle + NX, jnp.where(before, -middle - NX, LANES)))
    source = jnp.where(outer, place + shift, place)
    tile = jnp.where(outer, jnp.where(last | after, 1, 0), k >> 7)
    fits = (tile == (m >> 7)) & (used | (k < 2 * LANES))
    return jnp.where(fits, cell_weights(source, m & (LANES - 1)), 0.0).astype(BF16)


def first_kernel(v_ref, s_ref, near_ref, far_ref, wall_near, wall_far, v_out, s_out, pair_ref, ends_ref, sems):
    rows, cells = v_ref.shape[1:]
    spans = ((0, LANES), (cells - LANES, LANES), (LANES, cells - 2 * LANES))
    copies = []
    for i, (start, size) in enumerate(spans):
        for j, (ref, out) in enumerate(((v_ref, v_out), (s_ref, s_out))):
            at = pl.ds(start, size)
            copies.append(pltpu.make_async_copy(ref.at[:, :, at], out.at[:, :, at], sems.at[i, j]))
    for copy in copies:
        copy.start()
    pair_ref[...] = pair_filter()
    ends_ref[...] = ends_filter()
    for copy in copies[:4]:
        copy.wait()
    lane = lane_iota((rows, LANES))
    left = jnp.zeros((rows, LANES), F32)
    right = jnp.zeros((rows, LANES), F32)
    for f in range(9):
        ref, at = (v_out, f) if f < 3 else (s_out, f - 3)
        here = (lane >= NX * f) & (lane < NX * (f + 1))
        left = jnp.where(here, rot(ref[at, :, :LANES].astype(F32), NX * f), left)
        right = jnp.where(here, rot(ref[at, :, cells - LANES :].astype(F32), NX * f + NX), right)
    odd = lax.axis_index("gz") % 2 == 1
    near_ref[...] = jnp.where(odd, left, right)
    far_ref[...] = jnp.where(odd, right, left)
    for copy in copies[4:]:
        copy.wait()
    gy_odd = lax.axis_index("gy") % 2 == 1
    for f in range(9):
        at = slice(f * cells, (f + 1) * cells)
        if f < 3:
            low, high = v_out[f, :HMAX, :], v_out[f, rows - HMAX :, :]
        else:
            low = s_out[f - 3, : 2 * HMAX, :].astype(F32)[:HMAX]
            high = s_out[f - 3, rows - 2 * HMAX :, :].astype(F32)[HMAX:]
        wall_near[:, at] = jnp.where(gy_odd, low, high)
        wall_far[:, at] = jnp.where(gy_odd, high, low)


def first_call(velocity, strain):
    rows, cells = velocity.shape[1:]
    hbm = pl.BlockSpec(memory_space=pltpu.HBM)
    vmem = pl.BlockSpec(memory_space=pltpu.VMEM)
    shape = jax.ShapeDtypeStruct
    return pl.pallas_call(
        first_kernel,
        in_specs=[hbm] * 2,
        out_specs=[vmem] * 8,
        out_shape=[shape((rows, LANES), F32)] * 2
        + [shape((HMAX, 9 * cells), F32)] * 2
        + [shape(x.shape, x.dtype) for x in (velocity, strain)]
        + [shape((3 * LANES, 2 * LANES), BF16)] * 2,
        scratch_shapes=[pltpu.SemaphoreType.DMA((3, 2))],
        compiler_params=pltpu.CompilerParams(vmem_limit_bytes=FIRST_VMEM),
    )(velocity, strain)


def corner_kernel(h_ref, znear, zfar, near_ref, far_ref):
    rows = znear.shape[0]
    gz_odd = lax.axis_index("gz") % 2 == 1
    gy_odd = lax.axis_index("gy") % 2 == 1
    lane = lane_iota((HMAX, LANES))
    row = lax.broadcasted_iota(jnp.int32, (HMAX, LANES), 0)
    stamp = (row == 0) & (lane >= 9 * NX) & (lane < 10 * NX)
    heights = jnp.broadcast_to(jnp.pad(h_ref[...], ((0, 0), (0, LANES - rows))), (HMAX, LANES))
    sides = []
    for r0 in (0, rows - HMAX):
        zn = znear[r0 : r0 + HMAX, :]
        zf = zfar[r0 : r0 + HMAX, :]
        zl = jnp.where(stamp, rot(heights, 9 * NX - r0), jnp.where(gz_odd, zn, zf))
        sides.append((zl, jnp.where(gz_odd, zf, zn)))
    (low_left, low_right), (high_left, high_right) = sides
    near_ref[:, :LANES] = jnp.where(gy_odd, low_left, high_left)
    near_ref[:, LANES:] = jnp.where(gy_odd, low_right, high_right)
    far_ref[:, :LANES] = jnp.where(gy_odd, high_left, low_left)
    far_ref[:, LANES:] = jnp.where(gy_odd, high_right, low_right)


def corner_call(heights, znear, zfar):
    vmem = pl.BlockSpec(memory_space=pltpu.VMEM)
    return pl.pallas_call(
        corner_kernel,
        in_specs=[vmem] * 3,
        out_specs=[vmem] * 2,
        out_shape=[jax.ShapeDtypeStruct((HMAX, 2 * LANES), F32)] * 2,
        compiler_params=pltpu.CompilerParams(vmem_limit_bytes=SMALL_VMEM),
    )(heights, znear, zfar)


def split2(x):
    hi = x.astype(BF16)
    return hi, (x - hi.astype(F32)).astype(BF16)


def store_fields(u, s, put_high, put_low):
    tensor = [x.astype(F32) for x in s]
    rate = strain_rate(tensor)
    wide = u + [u[a] * u[b] for a, b in zip(LEAD_INDEX, TAIL_INDEX)] + [rate * x for x in tensor]
    for f, value in enumerate(wide):
        hi, lo = split2(value)
        put_high(f, hi)
        put_low(f, lo)
    for f, value in enumerate(s):
        put_high(WIDE + f, value.astype(BF16))


def smooth(rows, operand, matrix_ref):
    wide, narrow = slice(0, WIDE), slice(WIDE, FIELDS)
    lhs = jnp.concatenate([operand(True, wide), operand(False, wide)], axis=-1).reshape(WIDE * rows, -1)
    matrix = matrix_ref[...]
    first = jnp.dot(lhs, jnp.concatenate([matrix, matrix], axis=0), preferred_element_type=F32)
    lhs = operand(True, narrow).reshape((FIELDS - WIDE) * rows, -1)
    second = jnp.dot(lhs, matrix, preferred_element_type=F32)
    return [first[f * rows : (f + 1) * rows] for f in range(WIDE)] + [
        second[f * rows : (f + 1) * rows] for f in range(FIELDS - WIDE)
    ]


def pick(after, before):
    return jnp.where(lane_iota(after.shape) < LANES // 2, after, before)


def smooth_pair(n, fh, fl, pair_ref):
    def operand(high, fields):
        ref = fh if high else fl
        tile = [ref[fields, :, (2 * n + i) * LANES : (2 * n + i + 1) * LANES] for i in range(4)]
        return jnp.concatenate([tile[1], tile[2], pick(tile[3], tile[0])], axis=-1)

    return smooth(fh.shape[1], operand, pair_ref)


def smooth_ends(fh, fl, eh, el, ends_ref):
    cells = fh.shape[2]

    def operand(high, fields):
        ref, outer = (fh, eh) if high else (fl, el)
        second = ref[fields, :, LANES : 2 * LANES]
        ahead = ref[fields, :, cells - 2 * LANES : cells - LANES]
        lane = lane_iota(second.shape)
        edge = jnp.where(lane < NX, second, jnp.where(lane >= LANES - NX, ahead, outer[fields]))
        return jnp.concatenate([ref[fields, :, :LANES], ref[fields, :, cells - LANES :], edge], axis=-1)

    return smooth(fh.shape[1], operand, ends_ref)


def contract(g, inv, num, den):
    u, p, m, s = g[0:3], g[3:9], g[9:15], g[15:21]
    rate = 4.0 * inv * strain_rate(s)
    scaled = [inv * x for x in u]
    for k in range(6):
        leonard = p[k] - scaled[LEAD_INDEX[k]] * u[TAIL_INDEX[k]]
        model = m[k] - rate * s[k]
        weighted = TENSOR_WEIGHTS[k] * model
        num = num + weighted * leonard
        den = den + weighted * model
    return num, den


def to_column(row_vector, size):
    shape = (size, LANES)
    eye = lax.broadcasted_iota(jnp.int32, shape, 0) == lane_iota(shape)
    return jnp.sum(jnp.where(eye, jnp.broadcast_to(row_vector, shape), 0.0), axis=1, keepdims=True)


def to_row(column_vector, row):
    return jnp.sum(jnp.where(row == lane_iota(row.shape), column_vector, 0.0), axis=0, keepdims=True)


def pad_lanes(x):
    return jnp.pad(x, ((0, 0), (0, LANES - x.shape[1])))


def stencil_holds(place, row, down, up, rows):
    gy = lax.axis_index("gy")
    lowest = jnp.maximum(row - down, -gy * rows)
    highest = jnp.minimum(row + up, (lax.axis_size("gy") - gy) * rows - 1)
    return (place >= lowest) & (place <= highest)


def end_rows(x):
    return jnp.concatenate([x[:HMAX], x[x.shape[0] - HMAX :]], axis=0)


def wall_block(g, own_ref, height_ref, inv_ref, stack, acc_ref, part_ref):
    rows = g[0].shape[0]
    width = 2 * LANES
    height = jnp.concatenate([height_ref[...], height_ref[...]], axis=1)
    mask = own_ref[:, : 2 * rows]
    for f in range(FIELDS):
        hi, lo = split2(g[f] * height)
        stack[0:rows, f * width : (f + 1) * width] = hi
        stack[rows:, f * width : (f + 1) * width] = lo
    merged = jnp.dot(mask, stack[...], preferred_element_type=F32)
    for f in range(FIELDS):
        part_ref[f, 0:HMAX, :] = merged[0:HMAX, f * width : (f + 1) * width]
        part_ref[f, HMAX:, :] = merged[rows - HMAX :, f * width : (f + 1) * width]
    for r in range(HMAX, rows - HMAX, HMAX):
        num = acc_ref[0, r : r + HMAX, :]
        den = acc_ref[1, r : r + HMAX, :]
        scale = inv_ref[r : r + HMAX, :]
        for c in range(2):
            parts = [
                merged[r : r + HMAX, f * width + c * LANES : f * width + (c + 1) * LANES] for f in range(FIELDS)
            ]
            num, den = contract(parts, scale, num, den)
        acc_ref[0, r : r + HMAX, :] = num
        acc_ref[1, r : r + HMAX, :] = den


def leaves_early():
    return lax.axis_index("gz") == 0


def inner_work(v_ref, s_ref, pair_ref, fh, fl, inner):
    rows, cells = v_ref.shape[1:]
    for t in range(cells // LANES):
        at = slice(t * LANES, (t + 1) * LANES)
        for r in range(0, rows, 16):
            rr = slice(r, r + 16)

            def put_high(f, x):
                fh[f, rr, at] = x

            def put_low(f, x):
                fl[f, rr, at] = x

            store_fields(
                [v_ref[f, rr, at] for f in range(3)], [s_ref[f, rr, at] for f in range(6)], put_high, put_low
            )
    for n in range(inner.shape[0]):
        g = smooth_pair(n, fh, fl, pair_ref)
        for f in range(FIELDS):
            inner[n, f] = g[f]


def early_kernel(v_ref, s_ref, pair_ref, a, b, c, d, fh, fl, inner, *same):
    @pl.when(leaves_early())
    def _():
        inner_work(v_ref, s_ref, pair_ref, fh, fl, inner)


def late_kernel(v_ref, s_ref, pair_ref, a, b, c, fh, fl, inner):
    @pl.when(jnp.logical_not(leaves_early()))
    def _():
        inner_work(v_ref, s_ref, pair_ref, fh, fl, inner)


def wall_kernel(
    h_ref, reach_ref, inner, acc_ref, part_ref, own_ref, height_ref, inv_ref, mask_ref, total_ref, stack
):
    rows = h_ref.shape[1]
    ends = 2 * HMAX
    reach = pad_lanes(reach_ref[...].astype(F32))
    down = to_column(reach[0:1], rows).astype(jnp.int32)
    up = to_column(reach[1:2], rows).astype(jnp.int32)
    column = lane_iota((rows, 2 * LANES))
    row = lax.broadcasted_iota(jnp.int32, (rows, 2 * LANES), 0)
    place = jnp.where(column < rows, column, column - rows)
    inside = stencil_holds(place, row, down, up, rows)
    own_ref[...] = jnp.where(inside, 1.0, 0.0).astype(BF16)
    heights = pad_lanes(h_ref[...])
    height_ref[...] = jnp.broadcast_to(to_column(heights, rows), (rows, LANES))
    own = inside[:, :LANES] & (column[:, :LANES] < rows)
    total = jnp.sum(jnp.where(own, jnp.broadcast_to(heights, (rows, LANES)), 0.0), axis=1, keepdims=True)
    inv_ref[...] = jnp.broadcast_to(1.0 / total, (rows, LANES))
    total_ref[...] = jnp.broadcast_to(end_rows(total), (ends, LANES))
    column = lane_iota((ends, LANES))
    row = lax.broadcasted_iota(jnp.int32, (ends, LANES), 0)
    turn = column & (ends - 1)
    place = jnp.where(turn < HMAX, turn - HMAX, turn - HMAX + rows)
    row = jnp.where(row < HMAX, row, row + rows - ends)
    inside = stencil_holds(place, row, end_rows(down), end_rows(up), rows) & (column < 2 * ends)
    mask_ref[...] = jnp.where(inside, 1.0, 0.0)
    acc_ref[...] = jnp.zeros_like(acc_ref)
    for n in range(inner.shape[0]):
        g = [inner[n, f] for f in range(FIELDS)]
        wall_block(g, own_ref, height_ref, inv_ref, stack.at[n], acc_ref, part_ref.at[n])


def outer_kernel(
    fh, fl, znear, zfar, ynear, yfar, pair_ref, ends_ref, acc_in, own_ref, height_ref, inv_ref,
    sums_ref, part_ref, hh, hl, halo_inner, eh, el, stack, acc_ref,
):
    rows, cells = fh.shape[1:]
    gz_odd = lax.axis_index("gz") % 2 == 1
    gy_odd = lax.axis_index("gy") % 2 == 1
    acc_ref[...] = acc_in[...]
    edge_fields(jnp.where(gz_odd, znear[...], zfar[...]), jnp.where(gz_odd, zfar[...], znear[...]), eh, el)
    g_ends = smooth_ends(fh, fl, eh, el, ends_ref)
    for t in range(cells // LANES):
        at = slice(t * LANES, (t + 1) * LANES)

        def put_high(f, x):
            hh[f, :, at] = x

        def put_low(f, x):
            hl[f, :, at] = x

        raw = []
        for f in range(9):
            span = slice(f * cells + t * LANES, f * cells + (t + 1) * LANES)
            near, far = ynear[:, span], yfar[:, span]
            raw.append(jnp.concatenate([jnp.where(gy_odd, near, far), jnp.where(gy_odd, far, near)], axis=0))
        store_fields(raw[:3], raw[3:], put_high, put_low)
    for n in range(halo_inner.shape[0]):
        g = smooth_pair(n, hh, hl, pair_ref)
        for f in range(FIELDS):
            halo_inner[n, f] = g[f]
    wall_block(g_ends, own_ref, height_ref, inv_ref, stack, acc_ref, part_ref)
    inv = inv_ref[...]
    for k in range(2):
        plane_sums = jnp.sum(acc_ref[k] * (inv * inv), axis=1, keepdims=True)
        sums_ref[k : k + 1, :] = to_row(plane_sums, lax.broadcasted_iota(jnp.int32, (rows, LANES), 0))


def edge_fields(zl, zr, eh, el):
    rows = zl.shape[0]
    lane = lane_iota((16, LANES))
    middle = LANES // 2
    follows = (lane >= middle - NX) & (lane < middle)
    precedes = (lane >= middle) & (lane < middle + NX)
    for r in range(0, rows, 16):
        rr = slice(r, r + 16)
        raw = [
            jnp.where(
                follows,
                rot(zr[rr], middle - NX - NX * f),
                jnp.where(precedes, rot(zl[rr], middle - NX * f), 0.0),
            )
            for f in range(9)
        ]

        def put_high(f, x):
            eh[f, rr, :] = x

        def put_low(f, x):
            el[f, rr, :] = x

        store_fields(raw[:3], raw[3:], put_high, put_low)


def last_kernel(far_ref, near_ref, sums_in, part_inner, part_ends, mask_ref, total_ref, hh, hl, halo_inner, ends_ref, out_ref, eh, el, stack):
    rows = out_ref.shape[2]
    width = 2 * LANES
    gy_odd = lax.axis_index("gy") % 2 == 1
    both_rows = 2 * HMAX

    def halo(at):
        near, far = near_ref[:, at], far_ref[:, at]
        return jnp.concatenate([jnp.where(gy_odd, near, far), jnp.where(gy_odd, far, near)], axis=0)

    zl = halo(slice(0, LANES))
    zr = halo(slice(LANES, 2 * LANES))
    below = rot(zl[:HMAX], -9 * NX)[0:1]
    above = rot(zl[HMAX:], -9 * NX)[0:1]
    height = jnp.concatenate([to_column(below, HMAX), to_column(above, HMAX)], axis=0)
    lane = lane_iota((both_rows, LANES))
    heights = jnp.where(lane[0:1] < HMAX, below, rot(above, HMAX))
    outside = jnp.where(lane < both_rows, mask_ref[...] * heights, 0.0)
    inv = 1.0 / (total_ref[...] + jnp.sum(outside, axis=1, keepdims=True))
    scale = [inv[:HMAX], inv[HMAX:]]
    mask = mask_ref[:, : 2 * both_rows].astype(BF16)

    edge_fields(zl, zr, eh, el)
    zero = jnp.zeros((HMAX, LANES), F32)
    sums = [[zero, zero], [zero, zero]]
    blocks = halo_inner.shape[0]
    g_ends = smooth_ends(hh, hl, eh, el, ends_ref)
    for n in range(blocks + 1):
        if n < blocks:
            g = [halo_inner[n, f] for f in range(FIELDS)]
            part = part_inner.at[n]
        else:
            part = part_ends
            g = g_ends
        for f in range(FIELDS):
            hi, lo = split2(g[f] * height)
            stack[n, 0:both_rows, f * width : (f + 1) * width] = hi
            stack[n, both_rows:, f * width : (f + 1) * width] = lo
        merged = jnp.dot(mask, stack[n], preferred_element_type=F32)
        for i in range(2):
            rr = slice(i * HMAX, (i + 1) * HMAX)
            for c in range(2):
                at = slice(c * LANES, (c + 1) * LANES)
                values = [
                    part[f, rr, at] + merged[rr, f * width + c * LANES : f * width + (c + 1) * LANES]
                    for f in range(FIELDS)
                ]
                sums[i] = list(contract(values, scale[i], *sums[i]))
    row = lax.broadcasted_iota(jnp.int32, (both_rows, LANES), 0)
    row = jnp.where(row < HMAX, row, row + rows - both_rows)
    for k in range(2):
        values = jnp.concatenate([sums[0][k], sums[1][k]], axis=0) * (inv * inv)
        total = sums_in[k : k + 1, :] + to_row(jnp.sum(values, axis=1, keepdims=True), row)
        out_ref[:, k : k + 1, :] = jnp.broadcast_to(total[None, :, :rows], (out_ref.shape[0], 1, rows))


def call(kernel, out_shape, scratch, limit, *operands, aliases=None):
    vmem = pl.BlockSpec(memory_space=pltpu.VMEM)
    return pl.pallas_call(
        kernel,
        in_specs=[vmem] * len(operands),
        out_specs=jax.tree.map(lambda _: vmem, out_shape),
        out_shape=out_shape,
        scratch_shapes=scratch,
        input_output_aliases=aliases or {},
        compiler_params=pltpu.CompilerParams(vmem_limit_bytes=limit),
        cost_estimate=pl.CostEstimate(flops=4 * 10**9, bytes_accessed=2**20, transcendentals=0),
    )(*operands)


def local(velocity, strain, cell_height, stencil_reach):
    rows, cells = velocity.shape[1:]
    width = 2 * LANES
    blocks = cells // width - 1
    ends = 2 * HMAX
    shape = jax.ShapeDtypeStruct
    heights = cell_height.reshape(1, rows)
    near, far, wall_near, wall_far, velocity, strain, pair, both_ends = first_call(velocity, strain)
    own_work = [
        shape((FIELDS, rows, cells), BF16),
        shape((WIDE, rows, cells), BF16),
        shape((blocks, FIELDS, rows, width), F32),
    ]
    messages = (near, far, wall_near, wall_far)
    fh, fl, inner, near, far, wall_near, wall_far = call(
        early_kernel,
        own_work + [shape(x.shape, x.dtype) for x in messages],
        [],
        LARGE_VMEM,
        velocity,
        strain,
        pair,
        *messages,
        aliases={3 + i: 3 + i for i in range(4)},
    )
    znear = lax.ppermute(near, "gz", near_pairs("gz"))
    zfar = lax.ppermute(far, "gz", far_pairs("gz", True))
    yfar = lax.ppermute(wall_far, "gy", far_pairs("gy", False))
    ynear = lax.ppermute(wall_near, "gy", near_pairs("gy"))
    fh, fl, inner = call(
        late_kernel,
        own_work,
        [],
        LARGE_VMEM,
        velocity,
        strain,
        pair,
        fh,
        fl,
        inner,
        aliases={3 + i: i for i in range(3)},
    )
    acc, part_inner, own, height, inv, mask, totals = call(
        wall_kernel,
        [
            shape((2, rows, LANES), F32),
            shape((blocks, FIELDS, ends, width), F32),
            shape((rows, width), BF16),
            shape((rows, LANES), F32),
            shape((rows, LANES), F32),
            shape((ends, LANES), F32),
            shape((ends, LANES), F32),
        ],
        [pltpu.VMEM((blocks, 2 * rows, FIELDS * width), BF16)],
        LARGE_VMEM,
        heights,
        stencil_reach,
        inner,
    )
    near, far = corner_call(heights, znear, zfar)
    corner_far = lax.ppermute(far, "gy", far_pairs("gy", False))
    corner_near = lax.ppermute(near, "gy", near_pairs("gy"))
    sums, part_ends, hh, hl, halo_inner = call(
        outer_kernel,
        [
            shape((2, LANES), F32),
            shape((FIELDS, ends, width), F32),
            shape((FIELDS, ends, cells), BF16),
            shape((WIDE, ends, cells), BF16),
            shape((blocks, FIELDS, ends, width), F32),
        ],
        [
            pltpu.VMEM((FIELDS, rows, LANES), BF16),
            pltpu.VMEM((WIDE, rows, LANES), BF16),
            pltpu.VMEM((2 * rows, FIELDS * width), BF16),
            pltpu.VMEM((2, rows, LANES), F32),
        ],
        LARGE_VMEM,
        fh,
        fl,
        znear,
        zfar,
        ynear,
        yfar,
        pair,
        both_ends,
        acc,
        own,
        height,
        inv,
    )
    sums = call(
        last_kernel,
        shape((lax.axis_size("gz"), 2, rows), F32),
        [
            pltpu.VMEM((FIELDS, ends, LANES), BF16),
            pltpu.VMEM((WIDE, ends, LANES), BF16),
            pltpu.VMEM((blocks + 1, 2 * ends, FIELDS * width), BF16),
        ],
        LARGE_VMEM,
        corner_far,
        corner_near,
        sums,
        part_inner,
        part_ends,
        mask,
        totals,
        hh,
        hl,
        halo_inner,
        both_ends,
    )
    sums = jnp.sum(lax.all_to_all(sums, "gz", 0, 0), axis=0)
    total = lax.axis_size("gz") * cells
    return sums[0] / total / (sums[1] / total + 1e-06)


def near_pairs(axis):
    return [(i, i ^ 1) for i in range(lax.axis_size(axis))]


def far_pairs(axis, closed):
    n = lax.axis_size(axis)
    pairs = []
    for i in range(1, n if closed else n - 1, 2):
        pairs += [(i, (i + 1) % n), ((i + 1) % n, i)]
    return pairs


def solution(mesh):
    in_specs = (P(None, "gy", "gz"), P(None, "gy", "gz"), P("gy"), P(None, "gy"))
    return jax.shard_map(local, mesh=mesh, in_specs=in_specs, out_specs=P("gy"), check_vma=False)
```
